32 devices in a mesh: shard: 8 (over y, x, core), rep: 4 (over z).
Axes of the slice: x: 2, y: 2, z: 4, core: 2. Of those that a mesh axis runs over, the one named last changes fastest.
Arguments:
- big_images: bfloat16 [32, 32, 32, 384], P(('shard', 'rep')), may hold values from -6 to 6
- small_images: bfloat16 [32, 16, 16, 384], P(('shard', 'rep')), may hold values from -6 to 6
- big_labels: int32 [32], P(('shard', 'rep')), may hold values from 0 to 999
- small_labels: int32 [32], P(('shard', 'rep')), may hold values from 0 to 999
- big_sigmas: int32 [32], P(('shard', 'rep')), may hold values from 0 to 255
- small_sigmas: int32 [32], P(('shard', 'rep')), may hold values from 0 to 255
- loads: int32 [32, 2], P(('shard', 'rep')), may hold values from 0 to 1, as said below
- class_table: bfloat16 [1000, 768], replicated, may hold values from -6 to 6
- sigma_table: bfloat16 [256, 768], replicated, may hold values from -6 to 6
- norm_gains: bfloat16 [3, 384], P(None, 'shard'), may hold values from 0.099609375 to 1.8984375
- biases: bfloat16 [10, 384], P(None, 'shard'), may hold values from -1.796875 to 1.796875
- w_conv0: bfloat16 [3456, 384], P('shard'), may hold values from -0.109375 to 0.109375
- w_conv1: bfloat16 [3456, 384], P('shard'), may hold values from -0.109375 to 0.109375
- w_affine: bfloat16 [768, 768], P('shard'), may hold values from -0.21875 to 0.21875
- w_qkv: bfloat16 [384, 1152], P('shard'), may hold values from -0.3125 to 0.3125
- w_proj: bfloat16 [384, 384], P('shard'), may hold values from -1.25 to 1.25
- big_cotangent: bfloat16 [32, 32, 32, 384], P(('shard', 'rep')), may hold values from -6 to 6
- small_cotangent: bfloat16 [32, 16, 16, 384], P(('shard', 'rep')), may hold values from -6 to 6
Outputs:
- big_output: bfloat16 [32, 32, 32, 384], P(('shard', 'rep'))
- small_output: bfloat16 [32, 16, 16, 384], P(('shard', 'rep'))
- big_grad: bfloat16 [32, 32, 32, 384], P(('shard', 'rep'))
- small_grad: bfloat16 [32, 16, 16, 384], P(('shard', 'rep'))
- grad_norm_gains: float32 [3, 384], P(None, 'shard')
- grad_biases: float32 [10, 384], P(None, 'shard')
- grad_conv0: float32 [3456, 384], P('shard')
- grad_conv1: float32 [3456, 384], P('shard')
- grad_affine: float32 [768, 768], P('shard')
- grad_qkv: float32 [384, 1152], P('shard')
- grad_proj: float32 [384, 384], P('shard')
The draws below stay inside these ranges and needn't reach their ends.
Inputs may be any that keep to these rules, and one draw needn't show every extreme that they name: Row d of loads belongs to the device holding slots d * 1 onward of the large and d * 1 onward of the small images; column 0 counts its live large images (0 to 1), column 1 its live small images (1 to 1); the live images are the first slots of the device; in every draw some device has all its slots live.
All inputs are finite; a program needn't handle non-finite values.
Results may differ from the reference program's by a relative error of at most 0.017.
Values may be sent and summed in bfloat16 or wider, within the bound.
A program may use at most 192 MiB of HBM per device.

```python
import math
import jax
import jax.numpy as jnp
from jax import lax

C = 384
E = 768
HEADS = 6
GROUPS = 32
CLASSES = 1000
LEVELS = 256
BIG_SIDE = 32
SMALL_SIDE = 16
BIG_CAP = 1
SMALL_CAP = 1
NBIG = 32
NSMALL = 32
N_SHARD = 8
N_REP = 4


def draw_loads(key, part):
    key = jax.random.fold_in(key, 11)
    devices_total = N_SHARD * N_REP
    key_list = jax.random.split(key, 3)
    big_live = jax.random.randint(key_list[0], (devices_total,), 0, BIG_CAP + 1)
    small_live = jax.random.randint(key_list[1], (devices_total,), 1, SMALL_CAP + 1)
    fullest_device = jax.random.randint(key_list[2], (), 0, devices_total)
    is_fullest = jnp.arange(devices_total) == fullest_device
    big_live = jnp.where(is_fullest, BIG_CAP, big_live)
    small_live = jnp.where(is_fullest, SMALL_CAP, small_live)
    return jnp.stack([big_live, small_live], axis=1).astype(jnp.int32)


def with_ends(drawn, key, least, largest):
    spot = [jax.random.randint(jax.random.fold_in(key, axis), (), 0, length) for axis, length in enumerate(drawn.shape)]
    widest = drawn.shape.index(max(drawn.shape))
    neighbour = spot[:widest] + [(spot[widest] + 1) % drawn.shape[widest]] + spot[widest + 1:]
    return drawn.at[tuple(spot)].set(least).at[tuple(neighbour)].set(largest)


def steps_of(own_key, dims, shards, smallest, largest):
    loudness = 1.0
    for dim, blocks in shards:
        steps = jax.random.uniform(jax.random.fold_in(jax.random.fold_in(own_key, 6), dim), (blocks,), jnp.float32, smallest / len(shards), largest / len(shards))
        loudness = loudness * jnp.repeat(jnp.exp(steps), dims[dim] // blocks).reshape((-1,) + (1,) * (len(dims) - 1 - dim))
    return loudness


def scatter_about(stream_key, shape, scale, limit, shards=(), dtype=jnp.bfloat16):
    drawn = jax.random.normal(stream_key, shape, jnp.float32) * scale
    if len(shards) > 0:
        drawn = steps_of(stream_key, shape, shards, -0.22, 0.18) * drawn
    return jnp.clip(drawn, min=-limit, max=limit).astype(dtype)


def setup_inputs(seed: int = 0) -> dict:
    arg_keys = jax.random.split(jax.random.key(seed), 19)
    return {
        "big_images": scatter_about(arg_keys[0], (NBIG, BIG_SIDE, BIG_SIDE, C), 1.0, 6.0, ((0, 32),)),
        "small_images": scatter_about(arg_keys[1], (NSMALL, SMALL_SIDE, SMALL_SIDE, C), 1.0, 6.0, ((0, 32),)),
        "big_labels": with_ends(jax.random.randint(arg_keys[2], (NBIG,), 0, CLASSES), jax.random.fold_in(arg_keys[2], 1), 0, CLASSES - 1).astype(jnp.int32),
        "small_labels": with_ends(jax.random.randint(arg_keys[3], (NSMALL,), 0, CLASSES), jax.random.fold_in(arg_keys[3], 1), 0, CLASSES - 1).astype(jnp.int32),
        "big_sigmas": with_ends(jax.random.randint(arg_keys[4], (NBIG,), 0, LEVELS), jax.random.fold_in(arg_keys[4], 1), 0, LEVELS - 1).astype(jnp.int32),
        "small_sigmas": with_ends(jax.random.randint(arg_keys[5], (NSMALL,), 0, LEVELS), jax.random.fold_in(arg_keys[5], 1), 0, LEVELS - 1).astype(jnp.int32),
        "loads": draw_loads(jax.random.fold_in(arg_keys[18], 71), 0),
        "class_table": scatter_about(arg_keys[7], (CLASSES, E), 1.0, 6.0),
        "sigma_table": scatter_about(arg_keys[8], (LEVELS, E), 1.0, 6.0),
        "norm_gains": jnp.clip(1.0 + 0.18 * jax.random.normal(arg_keys[9], (3, C), jnp.float32), 0.099609375, 1.8984375).astype(jnp.bfloat16),
        "biases": scatter_about(arg_keys[10], (10, C), 0.3, 1.796875, ((1, 8),)),
        "w_conv0": scatter_about(arg_keys[11], (9 * C, C), (9 * C) ** -0.5, 0.109375, ((0, 8),)),
        "w_conv1": scatter_about(arg_keys[12], (9 * C, C), (9 * C) ** -0.5, 0.109375, ((0, 8),)),
        "w_affine": scatter_about(arg_keys[13], (E, 2 * C), E ** -0.5, 0.21875, ((0, 8),)),
        "w_qkv": scatter_about(arg_keys[14], (C, 3 * C), C ** -0.5, 0.3125, ((0, 8),)),
        "w_proj": scatter_about(arg_keys[15], (C, C), (C // 16) ** -0.5, 1.25, ((0, 8),)),
        "big_cotangent": scatter_about(arg_keys[16], (NBIG, BIG_SIDE, BIG_SIDE, C), 1.0, 6.0, ((0, 32),)),
        "small_cotangent": scatter_about(arg_keys[17], (NSMALL, SMALL_SIDE, SMALL_SIDE, C), 1.0, 6.0, ((0, 32),)),
    }


HIGHEST = lax.Precision.HIGHEST
EPSILON = 1e-05

@jax.custom_vjp
def low(v):
    return lax.optimization_barrier(v.astype(jnp.bfloat16)).astype(jnp.float32)

@jax.custom_vjp
def low_back(v):
    return v

def low_keep(v):
    return (low(v), None)

def low_pass(kept, grad):
    return (grad,)

def back_keep(v):
    return (v, None)

def back_low(kept, grad):
    return (low(grad),)
low.defvjp(low_keep, low_pass)
low_back.defvjp(back_keep, back_low)

def group_norm(values, gain_row, shift_row):
    batch_size, pixels, channels = values.shape
    grouped = values.reshape(batch_size, pixels, GROUPS, channels // GROUPS)
    centre = lax.optimization_barrier(jnp.mean(grouped, axis=(1, 3), keepdims=True))
    spread = lax.optimization_barrier(jnp.mean(jnp.square(grouped - centre), axis=(1, 3), keepdims=True))
    normal = (grouped - centre) * lax.rsqrt(spread + EPSILON)
    return normal.reshape(batch_size, pixels, channels) * gain_row + shift_row

def convolve(images, weight, side_len):
    batch_size, pixels, channels = images.shape
    kernel = weight.reshape(3, 3, channels, weight.shape[1])
    result = lax.conv_general_dilated(images.reshape(batch_size, side_len, side_len, channels), kernel, (1, 1), 'SAME', dimension_numbers=('NHWC', 'HWIO', 'NHWC'), precision=HIGHEST)
    return result.reshape(batch_size, pixels, weight.shape[1])

def block_forward(images, embeds, params, side_len):
    gain_all, shifts, w_conv0, w_conv1, w_affine, w_qkv, w_proj = params
    batch_size, pixels, channels = images.shape
    head_width = channels // HEADS
    score_scale = 1.0 / math.sqrt(head_width)
    entry_act = low(jax.nn.silu(group_norm(images, gain_all[0], shifts[0])))
    first_out = low_back(convolve(entry_act, w_conv0, side_len) + shifts[1])
    modulate = low_back(jnp.dot(embeds, w_affine, precision=HIGHEST) + jnp.concatenate([shifts[2], shifts[3]]))
    stretch = modulate[:, None, :channels]
    offset = modulate[:, None, channels:]
    middle_act = low(jax.nn.silu(offset + group_norm(first_out, gain_all[1], shifts[4]) * (stretch + 1.0)))
    second = low_back(convolve(middle_act, w_conv1, side_len) + shifts[5])
    residual = second + images
    normed = low(group_norm(residual, gain_all[2], shifts[6]))
    qkv_shift = jnp.concatenate([shifts[7], jnp.zeros_like(shifts[7]), shifts[8]])
    projected = low_back(jnp.einsum('bpc,cd->bpd', normed, w_qkv, precision=HIGHEST) + qkv_shift)
    queries = low(projected[:, :, :channels]).reshape(batch_size, pixels, HEADS, head_width)
    key_rows = low(projected[:, :, channels:2 * channels]).reshape(batch_size, pixels, HEADS, head_width)
    value_rows = low(projected[:, :, 2 * channels:]).reshape(batch_size, pixels, HEADS, head_width)
    scores = low_back(jnp.einsum('bqhd,bkhd->bhqk', queries, key_rows, precision=HIGHEST) * score_scale)
    attn_probs = low(jax.nn.softmax(scores, axis=-1))
    attended = jnp.einsum('bhqk,bkhd->bqhd', attn_probs, value_rows, precision=HIGHEST).reshape(batch_size, pixels, channels)
    attended = low(low_back(attended))
    branch = low_back(jnp.einsum('bpc,cd->bpd', attended, w_proj, precision=HIGHEST) + shifts[9])
    return branch + residual

def reference(big_images, small_images, big_labels, small_labels, big_sigmas, small_sigmas, loads, class_table, sigma_table, norm_gains, biases, w_conv0, w_conv1, w_affine, w_qkv, w_proj, big_cotangent, small_cotangent):
    devices_total = N_SHARD * N_REP
    big_pixels = BIG_SIDE * BIG_SIDE
    small_pixels = SMALL_SIDE * SMALL_SIDE

    def embed_of(labels, sigmas):
        table_rows = class_table.astype(jnp.float32)[labels] + sigma_table.astype(jnp.float32)[sigmas]
        return low(jax.nn.silu(table_rows))
    big_embed = embed_of(big_labels, big_sigmas).reshape(devices_total, BIG_CAP, E)
    small_embed = embed_of(small_labels, small_sigmas).reshape(devices_total, SMALL_CAP, E)
    big_live = (jnp.arange(BIG_CAP)[None, :] < loads[:, 0:1]).astype(jnp.float32)
    small_live = (jnp.arange(SMALL_CAP)[None, :] < loads[:, 1:2]).astype(jnp.float32)
    params = tuple((weight_array.astype(jnp.float32) for weight_array in (norm_gains, biases, w_conv0, w_conv1, w_affine, w_qkv, w_proj)))
    big_in = big_images.astype(jnp.float32).reshape(devices_total, BIG_CAP, big_pixels, C)
    small_in = small_images.astype(jnp.float32).reshape(devices_total, SMALL_CAP, small_pixels, C)

    def device_step(params_now, inputs):
        big_part, small_part, big_emb, small_emb = inputs
        return (block_forward(big_part, big_emb, params_now, BIG_SIDE), block_forward(small_part, small_emb, params_now, SMALL_SIDE))
    saved_step = jax.checkpoint(device_step)

    def forward(params_now, big_now, small_now):

        def scan_step(carry_in, inputs):
            return (carry_in, saved_step(params_now, inputs))
        unused, outputs = lax.scan(scan_step, jnp.zeros((), jnp.float32), (big_now, small_now, big_embed, small_embed))
        return outputs
    (big_out, small_out), pullback = jax.vjp(forward, params, big_in, small_in)
    big_mask = big_live[:, :, None, None]
    small_mask = small_live[:, :, None, None]
    big_cot = big_cotangent.astype(jnp.float32).reshape(devices_total, BIG_CAP, big_pixels, C) * big_mask
    small_cot = small_cotangent.astype(jnp.float32).reshape(devices_total, SMALL_CAP, small_pixels, C) * small_mask
    param_grads, big_input_grad, small_input_grad = pullback((big_cot, small_cot))
    big_output = (big_out * big_mask).reshape(big_images.shape).astype(jnp.bfloat16)
    small_output = (small_out * small_mask).reshape(small_images.shape).astype(jnp.bfloat16)
    big_grad = (big_input_grad * big_mask).reshape(big_images.shape).astype(jnp.bfloat16)
    small_grad = (small_input_grad * small_mask).reshape(small_images.shape).astype(jnp.bfloat16)
    return (big_output, small_output, big_grad, small_grad, param_grads[0], param_grads[1], param_grads[2], param_grads[3], param_grads[4], param_grads[5], param_grads[6])
```

```python
import math
import types

import jax
import jax.numpy as jnp
from jax import lax
from jax.experimental import pallas as pl
from jax.experimental.pallas import tpu as pltpu
from jax.sharding import PartitionSpec as P

HEADS = 6
GROUPS = 32
EPSILON = 1e-05
BF = jnp.bfloat16
F32 = jnp.float32
BLK = 256


def mm(left, right, lc=1, rc=0):
    return lax.dot_general(left, right, (((lc,), (rc,)), ((), ())), preferred_element_type=F32)


def fold(values):
    rows, cols = values.shape
    return jnp.sum(values.reshape(rows // 8, 8, cols), axis=0)


def total(folded):
    return jnp.sum(folded, axis=0, keepdims=True)


def sigmoid(z):
    return 0.5 * jnp.tanh(0.5 * z) + 0.5


class Seg:
    def __init__(self, index, row, pad, side):
        self.index, self.row, self.pad, self.side = index, row, pad, side
        self.pixels = side * side


def make_segs(sides):
    segs, row, pad = [], 0, 0
    for index, side in enumerate(sides):
        segs.append(Seg(index, row, pad + side, side))
        row += side * side
        pad += side * side + 2 * side
    return segs, row, pad


def each_block(seg, body, carry, ticks=None):
    count = seg.pixels // BLK
    due = {n: act for (image, n), act in (ticks or {}).items() if image == seg.index}
    if count == 1:
        for act in due.values():
            act()
        return body(0, carry)

    def step(i, c):
        for n, act in due.items():
            pl.when(i == n)(act)
        return body(pl.multiple_of(i * BLK, BLK), c)

    return lax.fori_loop(0, count, step, carry)


def rows_at(start, size=BLK):
    return pl.ds(pl.multiple_of(start, 16) if not isinstance(start, int) else start, size)


def three_parts(value):
    high = value.astype(BF).astype(F32)
    mid = (value - high).astype(BF).astype(F32)
    return [high, mid, (value - high - mid).astype(BF).astype(F32)]


def group_mean(rows, group_ref):
    count, channels = len(rows), rows[0].shape[1]
    parts = []
    for row in rows:
        parts += three_parts(row)
    padded = -(-3 * count // 16) * 16
    parts.append(jnp.zeros((padded - 3 * count, channels), F32))
    stacked = jnp.concatenate(parts, axis=0).astype(BF)
    sums = mm(stacked, group_ref[...]) * (GROUPS / channels)
    return [total(sums[3 * i : 3 * i + 3]) for i in range(count)]


def shift_pair(values, side):
    rows = values.shape[0]
    place = lax.broadcasted_iota(jnp.int32, (rows, 1), 0) % side
    before = jnp.where(place == 0, 0.0, pltpu.roll(values, 1, 0))
    after = jnp.where(place == side - 1, 0.0, pltpu.roll(values, rows - 1, 0))
    return before, after


class Moments:
    @staticmethod
    def start(channels):
        return (jnp.zeros((1, channels), F32), jnp.zeros((8, channels), F32), jnp.zeros((8, channels), F32))

    @staticmethod
    def add(carry, values, first):
        about, once, twice = carry
        about = jnp.where(first, values[0:1], about)
        off = values - about
        return (about, once + fold(off), twice + fold(off * off))


def norm_stats(segs, sums, group_ref):
    means, variances = [], []
    for seg, (about, once, twice) in zip(segs, sums):
        off = total(once) * (1.0 / seg.pixels)
        means.append(about + off)
        variances.append(jnp.maximum(total(twice) * (1.0 / seg.pixels) - off * off, 0.0))
    centres = group_mean(means, group_ref)
    spreads = group_mean(
        [v + (m - c) * (m - c) for v, m, c in zip(variances, means, centres)], group_ref
    )
    return [(c, lax.rsqrt(s + EPSILON)) for c, s in zip(centres, spreads)]


def norm_back_terms(segs, sums, stats, scales, group_ref):
    rows = []
    for seg, (s0, s1), scale in zip(segs, sums, scales):
        rows += [scale * s0 * (1.0 / seg.pixels), scale * s1 * (1.0 / seg.pixels)]
    means = group_mean(rows, group_ref)
    result = []
    for i, ((centre, inverse), scale) in enumerate(zip(stats, scales)):
        result.append((inverse * scale, inverse * means[2 * i], inverse * inverse * means[2 * i + 1]))
    return result


def store_triple(ref, seg, start, values, backward):
    channels = values.shape[1]
    before, after = shift_pair(values, seg.side)
    low, high = (after, before) if backward else (before, after)
    at = rows_at(seg.pad + start)
    ref[at, 0:channels] = low.astype(BF)
    ref[at, channels : 2 * channels] = values.astype(BF)
    ref[at, 2 * channels : 3 * channels] = high.astype(BF)


def zero_pads(ref, segs):
    columns = ref.shape[1]
    for seg in segs:
        ref[seg.pad - seg.side : seg.pad, :] = jnp.zeros((seg.side, columns), ref.dtype)
        ref[seg.pad + seg.pixels : seg.pad + seg.pixels + seg.side, :] = jnp.zeros((seg.side, columns), ref.dtype)


def conv_block(triple, weight, seg, start):
    width = triple.shape[1]
    out = None
    for a in range(3):
        term = mm(triple[rows_at(seg.pad + start + (a - 1) * seg.side), :], weight[a * width : (a + 1) * width, :])
        out = term if out is None else out + term
    return out


def conv_back_block(triple, crossed, seg, start):
    width = triple.shape[1]
    third = width // 3
    out = None
    for a in range(3):
        term = mm(
            triple[rows_at(seg.pad + start - (a - 1) * seg.side), :], crossed[a * third : (a + 1) * third, :], 1, 1
        )
        out = term if out is None else out + term
    return out


def cross_weight(source, target):
    channels = source.shape[1]

    def step(a, carry):
        for b in range(3):
            target[pl.ds(pl.multiple_of(a * channels, channels), channels), b * channels : (b + 1) * channels] = source[
                pl.ds(pl.multiple_of((3 * a + b) * channels, channels), channels), :
            ]
        return carry

    lax.fori_loop(0, 3, step, 0)


def conv_weight_grad(kept, triple, segs, store, columns):
    channels = kept.shape[1]
    first_col, last_col = columns
    width = last_col - first_col
    for a in range(3):
        out = None
        for seg in segs:
            first = seg.pad + (a - 1) * seg.side
            span = slice(seg.pad, seg.pad + seg.pixels)
            if width == channels:
                right = triple[span, :]
            else:
                right = jnp.concatenate(
                    [triple[span, b * channels + first_col : b * channels + last_col] for b in range(3)], axis=1
                )
            term = mm(kept[first : first + seg.pixels, :], right, 0, 0)
            out = term if out is None else out + term
        for b in range(3):
            store((3 * a + b) * channels, first_col, out[:, b * width : (b + 1) * width])


def attention(seg, block, keyvalue, qkv_t, datt_t, dkv):
    channels = datt_t.shape[0]
    head = channels // HEADS
    pair = 2 * head
    pixels = seg.pixels
    span = pl.ds(seg.row, pixels)
    place = lax.broadcasted_iota(jnp.int32, (pair, 1), 0)

    def heads(index, carry):
        ro = pl.multiple_of(index * pair, pair)
        keys = keyvalue[span, pl.ds(channels + ro, pair)]
        values = keyvalue[span, pl.ds(2 * channels + ro, pair)]

        def queries(step, inner):
            r = seg.row + step * block
            at = pl.ds(pl.multiple_of(r, block) if not isinstance(r, int) else r, block)
            q_pair = qkv_t[pl.ds(ro, pair), at]
            d_pair = datt_t[pl.ds(ro, pair), at]
            dk, dv = 0, 0
            for h in range(2):
                mine = (place < head) if h == 0 else (place >= head)
                q = jnp.where(mine, q_pair, 0).astype(BF)
                scores = mm(keys, q)
                peak = jnp.max(scores, axis=0, keepdims=True)
                probs = jnp.exp(scores - peak)
                inverse = 1.0 / jnp.sum(probs, axis=0, keepdims=True)
                probs_b = probs.astype(BF)
                k_t = qkv_t[pl.ds(channels + ro + h * head, head), span]
                v_t = qkv_t[pl.ds(2 * channels + ro + h * head, head), span]
                out_t = mm(v_t, probs_b) * inverse
                d_att = (jnp.where(mine, d_pair, 0).astype(F32) * inverse).astype(BF)
                dots = jnp.sum(d_att[h * head : (h + 1) * head].astype(F32) * out_t, axis=0, keepdims=True)
                d_probs = mm(values, d_att)
                d_scores = (probs * (d_probs - dots)).astype(BF)
                qkv_t[pl.ds(ro + h * head, head), at] = out_t.astype(BF)
                datt_t[pl.ds(ro + h * head, head), at] = (mm(k_t, d_scores) * (1.0 / math.sqrt(head))).astype(BF)
                dk = dk + mm(d_scores, q, 1, 1)
                dv = dv + mm(probs_b, d_att, 1, 1)
            if isinstance(step, int):
                dkv[span, pl.ds(ro, pair)] = dk
                dkv[span, pl.ds(channels + ro, pair)] = dv
            else:
                first = step == 0
                dkv[span, pl.ds(ro, pair)] = dk + jnp.where(first, 0.0, dkv[span, pl.ds(ro, pair)])
                dkv[span, pl.ds(channels + ro, pair)] = dv + jnp.where(first, 0.0, dkv[span, pl.ds(channels + ro, pair)])
            return inner

        if pixels == block:
            return queries(0, carry)
        return lax.fori_loop(0, pixels // block, queries, carry)

    lax.fori_loop(0, HEADS // 2, heads, 0)


def block_body(sides, r, hook=lambda name: None, ticks=lambda name: None):
    segs, rows_all, pad_all = make_segs(sides)
    ch = r.x.shape[1]
    x, g, out, grad = r.x, r.g, r.out, r.grad
    triple, kept0, kept1 = r.triple, r.kept0, r.kept1
    y0, res, wide = r.y0, r.res, r.wide
    gain = lambda i: r.params[i : i + 1, :]
    shift_row = lambda i: r.params[3 + i : 4 + i, :]
    groups = r.groups
    for ref in (triple, kept0, kept1):
        zero_pads(ref, segs)
    lane = lax.broadcasted_iota(jnp.int32, (ch, ch), 1)
    sub = lax.broadcasted_iota(jnp.int32, (ch, ch), 0)
    width = ch // GROUPS
    diff = sub // width - lane // width
    groups[...] = jnp.where(diff == 0, 1.0, 0.0).astype(BF)

    sums = []
    for seg in segs:
        def go(start, carry, seg=seg):
            return Moments.add(carry, x[rows_at(seg.row + start), :].astype(F32), start == 0)
        sums.append(each_block(seg, go, Moments.start(ch)))
    hook("shifts")
    stats0 = norm_stats(segs, sums, groups)
    for seg, (centre, inverse) in zip(segs, stats0):
        scale, shift = inverse * gain(0), shift_row(0)
        def go(start, carry, seg=seg, centre=centre, scale=scale, shift=shift):
            z = (x[rows_at(seg.row + start), :].astype(F32) - centre) * scale + shift
            a0 = z * sigmoid(z)
            store_triple(triple, seg, start, a0, False)
            kept0[rows_at(seg.pad + start), :] = a0.astype(BF)
            return carry
        each_block(seg, go, 0)

    hook("w0")
    sums = []
    for seg in segs:
        def go(start, carry, seg=seg):
            value = conv_block(triple, r.w0, seg, start) + shift_row(1)
            y0[rows_at(seg.row + start), :] = value
            return Moments.add(carry, value, start == 0)
        sums.append(each_block(seg, go, Moments.start(ch), ticks("conv0")))
    hook("conv0")
    stats1 = norm_stats(segs, sums, groups)
    hook("affine")
    mod = r.mod
    scales1, consts1 = [], []
    for seg, (centre, inverse) in zip(segs, stats1):
        stretch = mod[seg.index : seg.index + 1, :ch] + shift_row(2) + 1.0
        offset = mod[seg.index : seg.index + 1, ch:] + shift_row(3)
        scales1.append(gain(1) * stretch)
        shift = shift_row(4) * stretch + offset
        consts1.append((stretch, centre, inverse, inverse * scales1[-1], shift))
        _, _, _, scale, _ = consts1[-1]
        def go(start, carry, seg=seg, centre=centre, scale=scale, shift=shift):
            z = (y0[rows_at(seg.row + start), :] - centre) * scale + shift
            a1 = z * sigmoid(z)
            store_triple(triple, seg, start, a1, False)
            kept1[rows_at(seg.pad + start), :] = a1.astype(BF)
            return carry
        each_block(seg, go, 0)

    hook("w1")
    sums = []
    for seg in segs:
        def go(start, carry, seg=seg):
            at = rows_at(seg.row + start)
            value = conv_block(triple, r.w1, seg, start) + shift_row(5) + x[at, :].astype(F32)
            res[at, :] = value
            return Moments.add(carry, value, start == 0)
        sums.append(each_block(seg, go, Moments.start(ch), ticks("conv1")))
    stats2 = norm_stats(segs, sums, groups)

    hook("wqkv")
    hook("wproj")
    a2, kv, qkv_t, datt_t = r.a2, r.dqkv, r.qkv_t, r.datt_t
    w_qkv, w_proj = r.wqkv, r.wproj
    for seg, (centre, inverse) in zip(segs, stats2):
        scale, shift = inverse * gain(2), shift_row(6)
        def go(start, carry, seg=seg, centre=centre, scale=scale, shift=shift):
            at = rows_at(seg.row + start)
            normed = ((res[at, :] - centre) * scale + shift).astype(BF)
            a2[at, :] = normed
            lanes = pl.ds(pl.multiple_of(seg.row + start, BLK) if not isinstance(start, int) else seg.row + start, BLK)
            for part in range(3):
                value = mm(normed, w_qkv[:, part * ch : (part + 1) * ch])
                if part != 1:
                    value = value + shift_row(7 if part == 0 else 8)
                low = value.astype(BF)
                if part:
                    kv[at, part * ch : (part + 1) * ch] = low
                else:
                    low = low * (1.0 / math.sqrt(ch // HEADS))
                qkv_t[part * ch : (part + 1) * ch, lanes] = low.T
            datt_t[:, lanes] = mm(w_proj[...], g[at, :], 1, 1).astype(BF)
            return carry
        each_block(seg, go, 0)

    dkv = r.dkv
    for seg in segs:
        attention(seg, min(512, seg.pixels), kv, qkv_t, datt_t, dkv)

    dqkv = r.dqkv
    r.grad_proj(mm(qkv_t[0:ch, :], g[...]))
    hook("grad_proj")
    zero = jnp.zeros((8, ch), F32)
    sums2 = []
    q_sum, v_sum, g_sum = zero, zero, zero
    for seg, (centre, inverse) in zip(segs, stats2):
        live = r.live(seg.index)
        def go(start, carry, seg=seg, centre=centre, inverse=inverse, live=live):
            s0, s1, q_sum, v_sum, g_sum = carry
            at = rows_at(seg.row + start)
            lanes = pl.ds(pl.multiple_of(seg.row + start, BLK) if not isinstance(start, int) else seg.row + start, BLK)
            value = res[at, :]
            made = mm(qkv_t[0:ch, lanes], w_proj[...], 0, 0) + shift_row(9) + value
            out[at, :] = jnp.where(live, made, 0.0).astype(BF)
            g_sum = g_sum + fold(g[at, :].astype(F32))
            dq = datt_t[:, lanes].T
            dqkv[at, 0:ch] = dq
            dqkv[at, ch : 3 * ch] = dkv[at, :].astype(BF)
            q_sum = q_sum + fold(dq.astype(F32))
            v_sum = v_sum + fold(dkv[at, ch : 2 * ch])
            da2 = mm(dqkv[at, :], w_qkv[...], 1, 1)
            wide[at, :] = da2
            normal = (value - centre) * inverse
            return (s0 + fold(da2), s1 + fold(da2 * normal), q_sum, v_sum, g_sum)
        s0, s1, q_sum, v_sum, g_sum = each_block(seg, go, (zero, zero, q_sum, v_sum, g_sum))
        sums2.append((total(s0), total(s1)))
    hook("out")
    r.grad_qkv(mm(a2[...], dqkv[...], 0, 0))
    hook("grad_qkv")
    terms2 = norm_back_terms(segs, sums2, stats2, [gain(2)] * len(segs), groups)
    y1_sum = zero
    for seg, (centre, inverse), (factor, const, slope) in zip(segs, stats2, terms2):
        def go(start, carry, seg=seg, centre=centre, factor=factor, const=const, slope=slope):
            at = rows_at(seg.row + start)
            d_res = g[at, :].astype(F32) + wide[at, :] * factor - const - (res[at, :] - centre) * slope
            res[at, :] = d_res
            store_triple(triple, seg, start, d_res, True)
            return carry + fold(d_res)
        y1_sum = each_block(seg, go, y1_sum)
    gain2 = sums2[0][1] + sums2[1][1]
    shift6 = sums2[0][0] + sums2[1][0]

    hook("dr")

    for n, columns in enumerate(r.columns):
        conv_weight_grad(kept1, triple, segs, r.grad1, columns)
        hook(("grad1", n))
    cross_weight(r.w1, r.crossed)
    sums1 = []
    for seg, (stretch, centre, inverse, scale, shift) in zip(segs, consts1):
        def go(start, carry, seg=seg, centre=centre, inverse=inverse, scale=scale, shift=shift):
            s0, s1 = carry
            at = rows_at(seg.row + start)
            da1 = conv_back_block(triple, r.crossed, seg, start)
            off = y0[at, :] - centre
            z = off * scale + shift
            sig = sigmoid(z)
            dz = da1 * (sig * (1.0 + z * (1.0 - sig)))
            wide[at, :] = dz
            return (s0 + fold(dz), s1 + fold(dz * (off * inverse)))
        s0, s1 = each_block(seg, go, (zero, zero), ticks("back1"))
        sums1.append((total(s0), total(s1)))
    hook("back1")
    stats = [(centre, inverse) for _, centre, inverse, _, _ in consts1]
    terms1 = norm_back_terms(segs, sums1, stats, scales1, groups)
    y0_sum = zero
    for seg, (centre, inverse), (factor, const, slope) in zip(segs, stats, terms1):
        def go(start, carry, seg=seg, centre=centre, factor=factor, const=const, slope=slope):
            at = rows_at(seg.row + start)
            dy0 = wide[at, :] * factor - const - (y0[at, :] - centre) * slope
            store_triple(triple, seg, start, dy0, True)
            return carry + fold(dy0)
        y0_sum = each_block(seg, go, y0_sum)
    dmod, gain1, shift4 = [], 0.0, 0.0
    for (s0, s1), (stretch, *_) in zip(sums1, consts1):
        dmod.append(jnp.concatenate([gain(1) * s1 + shift_row(4) * s0, s0], axis=1))
        gain1 = gain1 + stretch * s1
        shift4 = shift4 + stretch * s0
    dmod = [d.astype(BF).astype(F32) for d in dmod]
    dmod_sum = dmod[0] + dmod[1]
    r.grad_affine(dmod)

    hook("dy0")

    for n, columns in enumerate(r.columns):
        conv_weight_grad(kept0, triple, segs, r.grad0, columns)
        hook(("grad0", n))
    cross_weight(r.w0, r.crossed)
    sums0 = []
    for seg, (centre, inverse) in zip(segs, stats0):
        scale, shift = inverse * gain(0), shift_row(0)
        def go(start, carry, seg=seg, centre=centre, inverse=inverse, scale=scale, shift=shift):
            s0, s1 = carry
            at = rows_at(seg.row + start)
            da0 = conv_back_block(triple, r.crossed, seg, start)
            off = x[at, :].astype(F32) - centre
            z = off * scale + shift
            sig = sigmoid(z)
            dz = da0 * (sig * (1.0 + z * (1.0 - sig)))
            wide[at, :] = dz
            return (s0 + fold(dz), s1 + fold(dz * (off * inverse)))
        s0, s1 = each_block(seg, go, (zero, zero), ticks("back0"))
        sums0.append((total(s0), total(s1)))
    hook("back0")
    terms0 = norm_back_terms(segs, sums0, stats0, [gain(0)] * len(segs), groups)
    r.rows[...] = jnp.concatenate(
        [
            sums0[0][1] + sums0[1][1],
            gain1,
            gain2,
            sums0[0][0] + sums0[1][0],
            total(y0_sum),
            dmod_sum[:, :ch],
            dmod_sum[:, ch:],
            shift4,
            total(y1_sum),
            shift6,
            total(q_sum),
            total(v_sum),
            total(g_sum),
            jnp.zeros((3, ch), F32),
        ],
        axis=0,
    )
    hook("rows")
    hook("grad")
    for seg, (centre, inverse), (factor, const, slope) in zip(segs, stats0, terms0):
        def go(start, carry, seg=seg, centre=centre, factor=factor, const=const, slope=slope):
            at = rows_at(seg.row + start)
            off = x[at, :].astype(F32) - centre
            grad[at, :] = (res[at, :] + wide[at, :] * factor - const - off * slope).astype(BF)
            return carry
        each_block(seg, go, 0)


def block_scratch(sides, ch):
    _, rows, pads = make_segs(sides)
    return dict(
        triple=pltpu.VMEM((pads, 3 * ch), BF),
        kept0=pltpu.VMEM((pads, ch), BF),
        kept1=pltpu.VMEM((pads, ch), BF),
        y0=pltpu.VMEM((rows, ch), F32),
        res=pltpu.VMEM((rows, ch), F32),
        wide=pltpu.VMEM((rows, ch), F32),
        groups=pltpu.VMEM((ch, ch), BF),
        a2=pltpu.VMEM((rows, ch), BF),
        qkv_t=pltpu.VMEM((3 * ch, rows), BF),
        datt_t=pltpu.VMEM((ch, rows), BF),
        dkv=pltpu.VMEM((rows, 2 * ch), F32),
        dqkv=pltpu.VMEM((rows, 3 * ch), BF),
        crossed=pltpu.VMEM((3 * ch, 3 * ch), BF),
    )


MESH = pl.DeviceIdType.MESH
VMEM_LIMIT = 63 * 2**20
FLIPS = ("s", "x", "y", "d", "xs", "ys", "ds")
OTHER = {"x": "y", "y": "x"}
SMALL = ("p", "m", "n", "q")
WEIGHTS = ("w0", "w1", "wqkv", "wproj")


class Net:
    def __init__(self, names, send, recv):
        self.at = {name: i for i, name in enumerate(names)}
        self.send, self.recv, self.sent = send, recv, []

    def copy(self, name, src, dst, peer):
        i = self.at[name]
        return pltpu.make_async_remote_copy(
            src_ref=src,
            dst_ref=dst,
            send_sem=self.send.at[i],
            recv_sem=self.recv.at[i],
            device_id=peer,
            device_id_type=MESH,
        )

    def push(self, name, make):
        self.copy(name, *make()).start()
        self.sent.append((name, make))

    def take(self, name, dst, peer):
        self.copy(name, dst, dst, peer).wait_recv()

    def drain(self):
        for name, make in self.sent:
            self.copy(name, *make()).wait_send()
        self.sent = []


def spans(rows, pieces):
    tiles = rows // 16
    cuts = [16 * (tiles * i // pieces) for i in range(pieces)] + [rows]
    return [(a, b - a) for a, b in zip(cuts, cuts[1:])]


def gather_units(block):
    units = []
    for name in ("w0", "w1"):
        units += [(name, first, count, axis) for (first, count), axis in zip(spans(block[name], 2), "xy")]
    third = block["wqkv"] // 3
    return units + [
        ("wqkv", 0, 2 * third, "x"),
        ("wqkv", 2 * third, third, "y"),
        ("wproj", 0, block["wproj"], "y"),
    ]


def column_spans(ch):
    return [(0, 2 * ch // 3), (2 * ch // 3, ch)]


def reduce_units(block, ch):
    third = block["wqkv"] // 3
    units = [
        ("wqkv", 0, 2 * third, 0, 3 * ch, "x"),
        ("wqkv", 2 * third, third, 0, 3 * ch, "y"),
        ("wproj", 0, block["wproj"], 0, ch, "y"),
    ]
    for name in ("w1", "w0"):
        for (low, high), pieces in zip(column_spans(ch), (4, 2)):
            for (first, count), axis in zip(spans(block[name], pieces), "xyxy"):
                units.append((name, first, count, low, high - low, axis))
    return units


def transfer_names(out_units, in_units):
    names = [(i, t) for i in range(len(out_units)) for t in ("x", "y", "s", "d", "sx", "sy", "sd")]
    names += [(i, t) for i in range(len(in_units)) for t in "abc"]
    names += [(i, t) for i in list(range(len(in_units))) + ["za", "zr"] for t in ("z0", "z1", "z2")]
    return names + [(what, flip) for what in SMALL for flip in FLIPS]


def packed(rows, height):
    count, columns = rows.shape
    pieces = [rows[i : i + 1, j : j + 128] for i in range(count) for j in range(0, columns, 128)]
    return jnp.concatenate(pieces + [jnp.zeros((height - len(pieces), 128), rows.dtype)], axis=0)


def unpacked(values, count, columns):
    per = columns // 128
    return jnp.concatenate(
        [jnp.concatenate([values[i * per + j : i * per + j + 1, :] for j in range(per)], axis=1) for i in range(count)],
        axis=0,
    )


def fused_kernel(sides, block, r):
    segs, _, _ = make_segs(sides)
    ch = r.triple.shape[1] // 3
    wide_rows = 2 * ch
    out_units, in_units = gather_units(block), reduce_units(block, ch)
    me, z = lax.axis_index("shard"), lax.axis_index("rep")
    core, px, py = me % 2, (me // 2) % 2, me // 4
    outer = (z == 0) | (z == 3)
    inner = jnp.logical_not(outer)

    def index(flip):
        fx = 1 - px if ("x" in flip or "d" in flip) else px
        fy = 1 - py if ("y" in flip or "d" in flip) else py
        fc = 1 - core if "s" in flip else core
        return (fy * 2 + fx) * 2 + fc

    at = {flip: index(flip) for flip in FLIPS + ("",)}
    peer = {flip: (at[flip], z) for flip in FLIPS}
    z_in, z_out, z_cross = (me, jnp.where(z < 2, 1, 2)), (me, jnp.where(z < 2, 0, 3)), (me, 3 - z)
    net = Net(transfer_names(out_units, in_units), r.send, r.recv)

    local = []

    def fetch(src, dst):
        copy = pltpu.make_async_copy(src, dst, r.local.at[len(local)])
        copy.start()
        local.append(copy)
        return copy

    got_x = [fetch(src, r.x.at[s.row : s.row + s.pixels, :]) for src, s in zip((r.big_x, r.small_x), segs)]

    barrier = pltpu.get_barrier_semaphore()
    for flip in FLIPS:
        pl.semaphore_signal(barrier, inc=1, device_id=peer[flip], device_id_type=MESH)

    @pl.when(outer)
    def _():
        pl.semaphore_signal(barrier, inc=1, device_id=z_in, device_id_type=MESH)

    @pl.when(inner)
    def _():
        pl.semaphore_signal(barrier, inc=1, device_id=z_out, device_id_type=MESH)
        pl.semaphore_signal(barrier, inc=1, device_id=z_cross, device_id_type=MESH)

    pl.semaphore_wait(barrier, jnp.where(outer, 8, 9))

    gathered = {name: getattr(r, name) for name in WEIGHTS}
    own = dict(w0=r.own_w0, w1=r.own_w1, wqkv=r.own_wqkv, wproj=r.own_wproj)
    mine = {}

    def part(i, flip):
        name, first, count, _ = out_units[i]
        start = pl.multiple_of(at[flip] * block[name] + first, 16)
        return gathered[name].at[pl.ds(start, count), :]

    def out_start(chosen):
        for flip in ("x", "y", "s"):
            for i in chosen:
                name, first, count, _ = out_units[i]
                net.push(
                    (i, flip),
                    lambda i=i, flip=flip, src=own[name].at[first : first + count, :]: (src, part(i, ""), peer[flip]),
                )
        for i in chosen:
            name, first, count, _ = out_units[i]
            mine[i] = fetch(own[name].at[first : first + count, :], part(i, ""))

    def out_pass(chosen):
        for direct in (True, False):
            for i in chosen:
                axis = out_units[i][3]
                if not direct:
                    axis = OTHER[axis]
                net.take((i, axis), part(i, axis), peer[axis])
                if direct:
                    net.push((i, "d"), lambda i=i, axis=axis: (part(i, axis), part(i, axis), peer[OTHER[axis]]))
                net.push((i, "s" + axis), lambda i=i, axis=axis: (part(i, axis), part(i, axis), peer["s"]))

    def out_late(chosen):
        for i in chosen:
            net.take((i, "d"), part(i, "d"), peer[OTHER[out_units[i][3]]])
            net.push((i, "sd"), lambda i=i: (part(i, "d"), part(i, "d"), peer["s"]))

    def out_end(chosen):
        for i in chosen:
            mine[i].wait()
            for name, flip in (("s", "s"), ("sx", "xs"), ("sy", "ys"), ("sd", "ds")):
                net.take((i, name), part(i, flip), peer["s"])

    grads = dict(w0=r.grad_w0, w1=r.grad_w1, wqkv=r.grad_wqkv, wproj=r.grad_wproj)
    results = dict(w0=r.out_w0, w1=r.out_w1, wqkv=r.out_wqkv, wproj=r.out_wproj)
    done = []

    def unit_ref(i):
        name, first, count, low, width, _ = in_units[i]
        return grads[name], (slice(first, first + count), slice(low, low + width))

    def in_core(chosen):
        for i in chosen:
            ref, span = unit_ref(i)
            net.push((i, "a"), lambda i=i, ref=ref, span=span: (ref.at[(1 - core, slice(None), slice(None)) + span], r.ra[i], peer["s"]))

    def away(i):
        axis = in_units[i][5]
        return (slice(None), 1 - px) if axis == "x" else (1 - py, slice(None))

    def near(i):
        axis = in_units[i][5]
        return (slice(None), px) if axis == "x" else (py, slice(None))

    def cross(i):
        return (1 - py, px) if in_units[i][5] == "x" else (py, 1 - px)

    def add_to(ref, where, value):
        ref[where] = ref[where] + value

    def in_first(chosen):
        for i in chosen:
            ref, span = unit_ref(i)
            axis = in_units[i][5]
            net.take((i, "a"), r.ra[i], peer["s"])
            add_to(ref, (core, slice(None), slice(None)) + span, r.ra[i][...])
            net.push((i, "b"), lambda i=i, ref=ref, span=span, axis=axis: (ref.at[(core,) + away(i) + span], r.rb[i], peer[axis]))

    def in_second(chosen):
        for i in chosen:
            ref, span = unit_ref(i)
            axis = in_units[i][5]
            net.take((i, "b"), r.rb[i], peer[axis])
            add_to(ref, (core,) + near(i) + span, r.rb[i][...])
            net.push((i, "c"), lambda i=i, ref=ref, span=span, axis=axis: (ref.at[(core,) + cross(i) + span], r.rc[i], peer[OTHER[axis]]))

    def z_out_of(i):
        if i == "za":
            return r.own_affine, r.rza
        if i == "zr":
            return r.own_rows, r.rzr
        ref, span = unit_ref(i)
        return ref.at[(core, py, px) + span], r.rz[i]

    def in_third(chosen):
        for i in chosen:
            ref, span = unit_ref(i)
            net.take((i, "c"), r.rc[i], peer[OTHER[in_units[i][5]]])
            add_to(ref, (core, py, px) + span, r.rc[i][...])
            z_first([i])

    def z_first(chosen):
        for i in chosen:
            src, slots = z_out_of(i)

            @pl.when(outer)
            def _():
                net.copy((i, "z0"), src, slots.at[0], z_in).start()

    def z_second(chosen):
        for i in chosen:
            src, slots = z_out_of(i)

            @pl.when(inner)
            def _():
                net.take((i, "z0"), slots.at[0], z_out)
                src[...] = src[...] + slots[0]
                net.copy((i, "z1"), src, slots.at[1], z_cross).start()

    def z_third(chosen):
        for i in chosen:
            src, slots = z_out_of(i)

            @pl.when(inner)
            def _():
                net.take((i, "z1"), slots.at[1], z_cross)
                slots[0] = src[...] + slots[1]
                net.copy((i, "z2"), slots.at[0], slots.at[0], z_out).start()

    def z_end(chosen):
        for i in chosen:
            src, slots = z_out_of(i)

            @pl.when(outer)
            def _():
                net.take((i, "z2"), slots.at[0], z_in)

            if i == "za":
                target = r.out_affine
            elif i == "zr":
                target = r.out_rows
            else:
                name, first, count, low, width, _ = in_units[i]
                target = results[name].at[first : first + count, low : low + width]
            done.append(fetch(slots.at[0], target))

    def z_drain(chosen):
        for i in chosen:
            src, slots = z_out_of(i)

            @pl.when(outer)
            def _():
                net.copy((i, "z0"), src, slots.at[0], z_in).wait_send()

            @pl.when(inner)
            def _():
                net.copy((i, "z1"), src, slots.at[1], z_cross).wait_send()
                net.copy((i, "z2"), slots.at[0], slots.at[0], z_out).wait_send()

    def keep(ref, rows_per):
        def store(row, col, value):
            height, width = value.shape
            start = row
            while start < row + height:
                owner = start // rows_per
                stop = min(row + height, (owner + 1) * rows_per)
                ref[owner % 2, owner // 4, (owner // 2) % 2, start - owner * rows_per : stop - owner * rows_per, col : col + width] = value[
                    start - row : stop - row, :
                ].astype(BF)
                start = stop

        return store

    P0, P1 = [0, 1, 2], [3, 4, 5, 6]
    P2, Q1, Q2 = [7, 8], [9, 10, 11, 12], [13, 14]
    W0, W1, REST = [0, 1], [2, 3], [4, 5, 6]
    copied_out = []
    r.grad = r.out
    r.columns = column_spans(ch)
    r.live = lambda i: r.loads[0, i] > 0
    r.grad0, r.grad1 = keep(r.grad_w0, block["w0"]), keep(r.grad_w1, block["w1"])
    keep_qkv, keep_proj = keep(r.grad_wqkv, block["wqkv"]), keep(r.grad_wproj, block["wproj"])
    r.grad_qkv = lambda value: keep_qkv(0, 0, value)
    r.grad_proj = lambda value: keep_proj(0, 0, value)

    def exchange(what, src, slots):
        each = len(src.shape) == len(slots.shape)
        for flip in FLIPS:
            net.push(
                (what, flip),
                lambda flip=flip: (src.at[at[flip]] if each else src, slots.at[me], peer[flip]),
            )

    def exchanged(what, slots):
        for flip in FLIPS:
            net.take((what, flip), slots.at[at[flip]], peer[flip])

    def hook(name):
        if name == "shifts":
            copied_message.wait()
            exchanged("p", r.messages)
            own_width = 128
            per = ch // 8
            lane = lax.broadcasted_iota(jnp.int32, (8 * own_width, ch), 1)
            sub = lax.broadcasted_iota(jnp.int32, (8 * own_width, ch), 0)
            place = jnp.where(sub % own_width < per, (sub // own_width) * per + sub % own_width, -1)
            spread = jnp.where(lane == place, 1.0, 0.0).astype(BF)
            side_by_side = jnp.concatenate([r.messages[o, 0:16, :] for o in range(8)], axis=1)
            r.params[...] = mm(side_by_side, spread)
            everyone = r.messages[:, 16:32, :].astype(F32).reshape(16, 8, 128)
            chosen = lax.broadcasted_iota(jnp.int32, (16, 8, 128), 1) == me
            r.embeds[...] = jnp.sum(jnp.where(chosen, everyone, 0.0), axis=1).astype(BF)
            copied_affine.wait()
            partial = mm(r.embeds[...], r.waff[...])
            for o in range(8):
                r.mod_out[o] = packed(partial[2 * o : 2 * o + 2, :], 16)
            exchange("m", r.mod_out, r.mod_in)
            r.mod_in[pl.ds(me, 1)] = r.mod_out[pl.ds(me, 1)]
        if name == "w0":
            out_pass(W0)
            out_late(W0)
            out_start(W1)
            out_end(W0)
        if name == "conv0":
            out_pass(W1)
            out_start(REST)
        if name == "affine":
            exchanged("m", r.mod_in)
            r.mod[...] = unpacked(jnp.sum(r.mod_in[...], axis=0), 2, wide_rows)
        if name == "w1":
            out_late(W1)
            out_end(W1)
        if name == "wqkv":
            out_pass(REST)
            out_late(REST)
            out_end(REST)
            for copy in got_g:
                copy.wait()
            for seg in segs:
                rows = slice(seg.row, seg.row + seg.pixels)
                r.g[rows, :] = jnp.where(r.live(seg.index), r.g[rows, :], 0).astype(BF)
        if name == "out":
            for seg, out in zip(segs, (r.big_out, r.small_out)):
                copied_out.append(fetch(r.out.at[seg.row : seg.row + seg.pixels, :], out))
        if name == "grad_qkv":
            in_core(P0)
        if name == "dr":
            in_first(P0)
        if name == ("grad1", 0):
            in_core(P1)
        if name == ("grad1", 1):
            in_core(P2)
            in_second(P0)
            in_first(P1)
        if name == "back1":
            in_second(P1[:2])
            z_second(P0)
        if name == "dy0":
            in_second(P1[2:])
            exchanged("n", r.dmod_in)
            terms = unpacked_rows(r.dmod_in)
            grad = mm(r.embeds[...], terms, 0, 0)
            r.own_affine[...] = grad[0 : block["waff"], :].astype(BF)
            z_first(["za"])
            z_third(P0)
        if name == ("grad0", 0):
            in_core(Q1)
            in_second(P2)
            in_third(P1)
        if name == ("grad0", 1):
            in_core(Q2)
            in_third(P2)
            in_first(Q1)
            z_end(P0)
        if name == "back0":
            in_second(Q1[2:])
            in_second(Q2)
            z_third(P2 + ["za"])
        if name == "rows":
            exchange("q", r.rows, r.rows_in)
            r.rows_in[pl.ds(me, 1)] = r.rows[...][None]
        if name == "grad":
            for copy in copied_out:
                copy.wait()

    def unpacked_rows(ref):
        values = ref[...].astype(F32)
        return jnp.concatenate([unpacked(values[o], 2, wide_rows) for o in range(8)], axis=0).astype(BF)

    def ticks(name):
        if name == "back1":
            return {
                (0, 1): lambda: in_first(P2),
                (0, 2): lambda: in_third(P0),
            }
        if name == "back0":
            return {
                (0, 1): lambda: in_first(Q2),
                (0, 2): lambda: z_second(P1),
                (0, 3): lambda: in_second(Q1[:2]),
                (1, 0): lambda: (z_second(P2 + ["za"]), z_third(P1)),
            }
        return {}

    def grad_affine(rows):
        r.dmod[...] = packed(jnp.concatenate(rows, axis=0), 16).astype(BF)
        exchange("n", r.dmod, r.dmod_in)
        r.dmod_in[pl.ds(me, 1)] = r.dmod[...][None]

    r.grad_affine = grad_affine
    exchange("p", r.message, r.messages)
    copied_message = fetch(r.message, r.messages.at[me])
    out_start(W0)
    r.waff[...] = jnp.zeros_like(r.waff)
    copied_affine = fetch(r.own_waff, r.waff.at[0 : block["waff"], :])
    got_g = [fetch(src, r.g.at[s.row : s.row + s.pixels, :]) for src, s in zip((r.big_g, r.small_g), segs)]
    for copy in got_x:
        copy.wait()
    block_body(sides, r, hook, ticks)

    for seg, out in zip(segs, (r.big_grad, r.small_grad)):
        done.append(fetch(r.grad.at[seg.row : seg.row + seg.pixels, :], out))
    exchanged("q", r.rows_in)
    sums = jnp.concatenate(three_parts(jnp.sum(r.rows_in[...], axis=0)), axis=0).astype(BF)
    lane = lax.broadcasted_iota(jnp.int32, (ch, 128), 1)
    sub = lax.broadcasted_iota(jnp.int32, (ch, 128), 0)
    per = ch // 8
    cut = mm(sums, jnp.where((sub - per * me == lane) & (lane < per), 1.0, 0.0).astype(BF))
    r.own_rows[...] = cut[0:16] + cut[16:32] + cut[32:48]
    z_first(["zr"])
    in_third(Q1[:2])
    z_end(P1 + P2 + ["za"])
    in_third(Q1[2:])
    z_second(["zr"] + Q1[:2])
    in_third(Q2)
    z_second(Q1[2:])
    z_third(["zr"] + Q1[:2])
    z_second(Q2)
    z_third(Q1[2:] + Q2)
    z_end(["zr"] + Q1 + Q2)
    z_drain(P0 + P1 + P2 + Q1 + Q2 + ["za", "zr"])
    net.drain()
    for copy in done:
        copy.wait()


def embed_rows(class_table, sigma_table, labels, sigmas):
    summed = class_table[labels].astype(F32) + sigma_table[sigmas].astype(F32)
    return jax.nn.silu(summed).astype(BF)


def named(names, refs):
    return dict(zip(names, refs))


def fused_call(sides, ch, arrays):
    block = dict(
        w0=arrays["own_w0"].shape[0],
        w1=arrays["own_w1"].shape[0],
        waff=arrays["own_waff"].shape[0],
        wqkv=arrays["own_wqkv"].shape[0],
        wproj=arrays["own_wproj"].shape[0],
    )
    segs, rows, _ = make_segs(sides)
    out_units, in_units = gather_units(block), reduce_units(block, ch)
    width = dict(w0=ch, w1=ch, wqkv=3 * ch, wproj=ch)
    buffer = lambda *shape: pltpu.VMEM(shape, BF)
    wide_buffer = lambda *shape: pltpu.VMEM(shape, F32)
    whole = {name: buffer(8 * block[name], width[name]) for name in WEIGHTS}
    grads = {name: buffer(2, 2, 2, block[name], width[name]) for name in WEIGHTS}
    copies = len(transfer_names(out_units, in_units))
    scratch = dict(
        block_scratch(sides, ch),
        **whole,
        grad_w0=grads["w0"],
        grad_w1=grads["w1"],
        grad_wqkv=grads["wqkv"],
        grad_wproj=grads["wproj"],
        x=buffer(rows, ch),
        g=buffer(rows, ch),
        out=buffer(rows, ch),
        params=wide_buffer(16, ch),
        messages=buffer(8, 32, 128),
        embeds=buffer(16, 128),
        waff=buffer(128, 2 * ch),
        mod_out=wide_buffer(8, 16, 128),
        mod_in=wide_buffer(8, 16, 128),
        mod=wide_buffer(2, 2 * ch),
        dmod=buffer(16, 128),
        dmod_in=buffer(8, 16, 128),
        own_affine=buffer(block["waff"], 2 * ch),
        rza=buffer(2, block["waff"], 2 * ch),
        rows=wide_buffer(16, ch),
        rows_in=wide_buffer(8, 16, ch),
        own_rows=wide_buffer(16, 128),
        rzr=wide_buffer(2, 16, 128),
        send=pltpu.SemaphoreType.DMA((copies,)),
        recv=pltpu.SemaphoreType.DMA((copies,)),
        local=pltpu.SemaphoreType.DMA((48,)),
    )
    slots = [
        [buffer(2, 2, n, w) for _, _, n, _, w, _ in in_units],
        [buffer(2, n, w) for _, _, n, _, w, _ in in_units],
        [buffer(n, w) for _, _, n, _, w, _ in in_units],
        [buffer(2, n, w) for _, _, n, _, w, _ in in_units],
    ]
    big, small = segs[0].pixels, segs[1].pixels
    outs = dict(
        big_out=((big, ch), BF),
        small_out=((small, ch), BF),
        big_grad=((big, ch), BF),
        small_grad=((small, ch), BF),
        out_rows=((16, 128), F32),
        out_affine=((block["waff"], 2 * ch), BF),
        out_w0=((block["w0"], ch), BF),
        out_w1=((block["w1"], ch), BF),
        out_wqkv=((block["wqkv"], 3 * ch), BF),
        out_wproj=((block["wproj"], ch), BF),
    )
    names = list(arrays) + list(outs) + list(scratch)

    def kernel(*refs):
        r = types.SimpleNamespace(**dict(zip(names, refs)))
        rest = list(refs[len(names) :])
        n = len(in_units)
        r.ra, r.rb, r.rc, r.rz = rest[:n], rest[n : 2 * n], rest[2 * n : 3 * n], rest[3 * n :]
        fused_kernel(sides, block, r)

    results = pl.pallas_call(
        kernel,
        out_shape=[jax.ShapeDtypeStruct(*shape) for shape in outs.values()],
        in_specs=[pl.BlockSpec(memory_space=pltpu.SMEM)] + [pl.BlockSpec(memory_space=pl.ANY)] * (len(arrays) - 1),
        out_specs=[pl.BlockSpec(memory_space=pl.ANY)] * len(outs),
        scratch_shapes=list(scratch.values()) + sum(slots, []),
        compiler_params=pltpu.CompilerParams(
            collective_id=0, has_side_effects=True, vmem_limit_bytes=VMEM_LIMIT
        ),
    )(*arrays.values())
    return results


def finish_call(results, per):
    images, rows, weights = results[:4], results[4], results[5:]
    outs = [jax.ShapeDtypeStruct(image.shape, image.dtype) for image in images]
    outs += [jax.ShapeDtypeStruct((3, per), F32), jax.ShapeDtypeStruct((10, per), F32)]
    outs += [jax.ShapeDtypeStruct(weight.shape, F32) for weight in weights]
    total_in, total_out = len(results), len(outs)

    def kernel(*refs):
        sources, targets = refs[:total_in], refs[total_in : total_in + total_out]
        rest = refs[total_in + total_out :]
        held, made, sems = rest[:total_in], rest[total_in:-1], rest[-1]
        inward = [pltpu.make_async_copy(s, h, sems.at[i]) for i, (s, h) in enumerate(zip(sources, held))]
        for copy in inward:
            copy.start()
        outward = []

        def send(source, target):
            copy = pltpu.make_async_copy(source, target, sems.at[total_in + len(outward)])
            copy.start()
            outward.append(copy)

        for i in range(5, total_in):
            inward[i].wait()
            made[i - 3][...] = held[i][...].astype(F32)
            send(made[i - 3], targets[i + 1])
        for i in range(4):
            inward[i].wait()
            send(held[i], targets[i])
        inward[4].wait()
        made[0][...] = held[4][0:3, 0:per]
        made[1][...] = held[4][3:13, 0:per]
        send(made[0], targets[4])
        send(made[1], targets[5])
        for copy in outward:
            copy.wait()

    any_spec = pl.BlockSpec(memory_space=pl.ANY)
    return pl.pallas_call(
        kernel,
        out_shape=outs,
        in_specs=[any_spec] * total_in,
        out_specs=[any_spec] * total_out,
        scratch_shapes=[pltpu.VMEM(array.shape, array.dtype) for array in results]
        + [pltpu.VMEM(out.shape, out.dtype) for out in outs[4:]]
        + [pltpu.SemaphoreType.DMA((total_in + total_out,))],
        compiler_params=pltpu.CompilerParams(vmem_limit_bytes=VMEM_LIMIT),
    )(*results)


def plain_call(sides, ch, arrays):
    _, rows, _ = make_segs(sides)
    scratch = dict(
        block_scratch(sides, ch), mod=pltpu.VMEM((16, 2 * ch), F32), masked=pltpu.VMEM((rows, ch), BF)
    )
    outs = dict(
        out=((rows, ch), BF),
        grad=((rows, ch), BF),
        terms0=((9 * ch, ch), BF),
        terms1=((9 * ch, ch), BF),
        affine=((2 * ch, 2 * ch), BF),
        terms_qkv=((ch, 3 * ch), BF),
        terms_proj=((ch, ch), BF),
        rows=((16, ch), F32),
    )
    names = list(arrays) + list(outs) + list(scratch)

    def kernel(*refs):
        r = types.SimpleNamespace(**dict(zip(names, refs)))
        segs, _, _ = make_segs(sides)
        given = r.g
        r.live = lambda i: r.loads[0, i] > 0
        r.g = r.masked
        r.columns = [(0, ch)]
        for seg in segs:
            span = slice(seg.row, seg.row + seg.pixels)
            r.masked[span, :] = jnp.where(r.live(seg.index), given[span, :], 0).astype(BF)

        def hook(name):
            if name == "affine":
                r.mod[...] = mm(r.emb[...], r.waff[...])

        def keep(ref):
            def store(row, col, value):
                ref[row : row + value.shape[0], col : col + value.shape[1]] = value.astype(BF)

            return store

        def grad_affine(terms):
            zeros = jnp.zeros((14, 2 * ch), F32)
            r.affine[...] = mm(r.emb[...], jnp.concatenate(terms + [zeros], axis=0).astype(BF), 0, 0).astype(BF)

        r.grad0, r.grad1 = keep(r.terms0), keep(r.terms1)
        r.grad_qkv = lambda value: keep(r.terms_qkv)(0, 0, value)
        r.grad_proj = lambda value: keep(r.terms_proj)(0, 0, value)
        r.grad_affine = grad_affine
        block_body(sides, r, hook)

    return pl.pallas_call(
        kernel,
        out_shape=[jax.ShapeDtypeStruct(*shape) for shape in outs.values()],
        in_specs=[pl.BlockSpec(memory_space=pltpu.SMEM)]
        + [pl.BlockSpec(memory_space=pltpu.VMEM)] * (len(arrays) - 1),
        out_specs=[pl.BlockSpec(memory_space=pltpu.VMEM)] * len(outs),
        scratch_shapes=list(scratch.values()),
        compiler_params=pltpu.CompilerParams(vmem_limit_bytes=VMEM_LIMIT),
    )(*arrays.values())


def on_device(
    fused,
    big_images,
    small_images,
    big_labels,
    small_labels,
    big_sigmas,
    small_sigmas,
    loads,
    class_table,
    sigma_table,
    norm_gains,
    biases,
    w_conv0,
    w_conv1,
    w_affine,
    w_qkv,
    w_proj,
    big_cotangent,
    small_cotangent,
):
    sides = (big_images.shape[1], small_images.shape[1])
    ch = big_images.shape[-1]
    flat = lambda array: array.reshape(-1, ch)
    big_embed = embed_rows(class_table, sigma_table, big_labels, big_sigmas)
    small_embed = embed_rows(class_table, sigma_table, small_labels, small_sigmas)
    emb = jnp.concatenate([big_embed, small_embed], axis=0)
    own_rows = jnp.concatenate([norm_gains, biases], axis=0)
    shapes = [big_images.shape, small_images.shape] * 2
    if fused:
        per = own_rows.shape[1]
        slices = emb.reshape(16, -1)
        message = jnp.concatenate(
            [
                jnp.pad(own_rows, ((0, 3), (0, 128 - per))),
                jnp.pad(slices, ((0, 0), (0, 128 - slices.shape[1]))),
            ],
            axis=0,
        )
        made = fused_call(
            sides,
            ch,
            dict(
                loads=loads,
                big_x=flat(big_images),
                small_x=flat(small_images),
                big_g=flat(big_cotangent),
                small_g=flat(small_cotangent),
                message=message,
                own_w0=w_conv0,
                own_w1=w_conv1,
                own_waff=w_affine,
                own_wqkv=w_qkv,
                own_wproj=w_proj,
            ),
        )
        made = finish_call(made, per)
        images, gains, shifts = made[:4], made[4], made[5]
        affine, first, second, qkv, proj = made[6:]
        weights = [first, second, affine, qkv, proj]
    else:
        gather = lambda array, axis=0: lax.all_gather(array, "shard", axis=axis, tiled=True)
        out, grad, terms0, terms1, affine, terms_qkv, terms_proj, rows = plain_call(
            sides,
            ch,
            dict(
                loads=loads,
                x=jnp.concatenate([flat(big_images), flat(small_images)], axis=0),
                g=jnp.concatenate([flat(big_cotangent), flat(small_cotangent)], axis=0),
                emb=jnp.pad(emb, ((0, 14), (0, 0))),
                params=jnp.pad(gather(own_rows, 1).astype(F32), ((0, 3), (0, 0))),
                w0=gather(w_conv0),
                w1=gather(w_conv1),
                waff=gather(w_affine),
                wqkv=gather(w_qkv),
                wproj=gather(w_proj),
            ),
        )

        def owned(terms, axis=0):
            mine = lax.psum_scatter(terms, "shard", scatter_dimension=axis, tiled=True)
            return lax.psum(mine, "rep").astype(F32)

        big = sides[0] * sides[0]
        images = [out[:big], out[big:], grad[:big], grad[big:]]
        sums = owned(rows, 1)
        gains, shifts = sums[:3], sums[3:13]
        weights = [owned(terms) for terms in (terms0, terms1, affine, terms_qkv, terms_proj)]
    return tuple(image.reshape(shape) for image, shape in zip(images, shapes)) + (gains, shifts, *weights)


def solution(mesh):
    fused = mesh.shape["shard"] == 8 and mesh.shape["rep"] == 4
    split = P(("shard", "rep"))
    image = P(("shard", "rep"), None, None, None)
    rows, columns = P("shard", None), P(None, "shard")
    return jax.shard_map(
        lambda *arrays: on_device(fused, *arrays),
        mesh=mesh,
        in_specs=(image, image, split, split, split, split, P(("shard", "rep"), None), P(), P(), columns, columns)
        + (rows,) * 5
        + (image, image),
        out_specs=(image,) * 4 + (columns,) * 2 + (rows,) * 5,
        check_vma=False,
    )
```

```python
import math
import types

import jax
import jax.numpy as jnp
from jax import lax
from jax.experimental import pallas as pl
from jax.experimental.pallas import tpu as pltpu
from jax.sharding import PartitionSpec as P

HEADS = 6
GROUPS = 32
EPSILON = 1e-05
BF = jnp.bfloat16
F32 = jnp.float32
BLK = 256


def mm(left, right, lc=1, rc=0):
    return lax.dot_general(left, right, (((lc,), (rc,)), ((), ())), preferred_element_type=F32)


def fold(values):
    rows, cols = values.shape
    return jnp.sum(values.reshape(rows // 8, 8, cols), axis=0)


def total(folded):
    return jnp.sum(folded, axis=0, keepdims=True)


def sigmoid(z):
    return 0.5 * jnp.tanh(0.5 * z) + 0.5


class Seg:
    def __init__(self, index, row, pad, side):
        self.index, self.row, self.pad, self.side = index, row, pad, side
        self.pixels = side * side


def make_segs(sides):
    segs, row, pad = [], 0, 0
    for index, side in enumerate(sides):
        segs.append(Seg(index, row, pad + side, side))
        row += side * side
        pad += side * side + 2 * side
    return segs, row, pad


def each_block(seg, body, carry, ticks=None):
    count = seg.pixels // BLK
    due = {n: act for (image, n), act in (ticks or {}).items() if image == seg.index}
    if count == 1:
        for act in due.values():
            act()
        return body(0, carry)

    def step(i, c):
        for n, act in due.items():

            @pl.when(i == n)
            def _(act=act):
                act()

        return body(pl.multiple_of(i * BLK, BLK), c)

    return lax.fori_loop(0, count, step, carry)


def rows_at(start, size=BLK):
    return pl.ds(pl.multiple_of(start, 16) if not isinstance(start, int) else start, size)


def three_parts(value):
    high = value.astype(BF).astype(F32)
    mid = (value - high).astype(BF).astype(F32)
    return [high, mid, (value - high - mid).astype(BF).astype(F32)]


def group_mean(rows, group_ref):
    count, channels = len(rows), rows[0].shape[1]
    parts = []
    for row in rows:
        parts += three_parts(row)
    padded = -(-3 * count // 16) * 16
    parts.append(jnp.zeros((padded - 3 * count, channels), F32))
    stacked = jnp.concatenate(parts, axis=0).astype(BF)
    sums = mm(stacked, group_ref[...]) * (GROUPS / channels)
    return [total(sums[3 * i : 3 * i + 3]) for i in range(count)]


def shift_pair(values, side):
    rows = values.shape[0]
    place = lax.broadcasted_iota(jnp.int32, (rows, 1), 0) % side
    before = jnp.where(place == 0, 0.0, pltpu.roll(values, 1, 0))
    after = jnp.where(place == side - 1, 0.0, pltpu.roll(values, rows - 1, 0))
    return before, after


class Moments:
    @staticmethod
    def start(channels):
        return (jnp.zeros((1, channels), F32), jnp.zeros((8, channels), F32), jnp.zeros((8, channels), F32))

    @staticmethod
    def add(carry, values, first):
        about, once, twice = carry
        about = jnp.where(first, values[0:1], about)
        off = values - about
        return (about, once + fold(off), twice + fold(off * off))


def norm_stats(segs, sums, group_ref):
    means, variances = [], []
    for seg, (about, once, twice) in zip(segs, sums):
        off = total(once) * (1.0 / seg.pixels)
        means.append(about + off)
        variances.append(jnp.maximum(total(twice) * (1.0 / seg.pixels) - off * off, 0.0))
    centres = group_mean(means, group_ref)
    spreads = group_mean(
        [v + (m - c) * (m - c) for v, m, c in zip(variances, means, centres)], group_ref
    )
    return [(c, lax.rsqrt(s + EPSILON)) for c, s in zip(centres, spreads)]


def norm_back_terms(segs, sums, stats, scales, group_ref):
    rows = []
    for seg, (s0, s1), scale in zip(segs, sums, scales):
        rows += [scale * s0 * (1.0 / seg.pixels), scale * s1 * (1.0 / seg.pixels)]
    means = group_mean(rows, group_ref)
    result = []
    for i, ((centre, inverse), scale) in enumerate(zip(stats, scales)):
        result.append((inverse * scale, inverse * means[2 * i], inverse * inverse * means[2 * i + 1]))
    return result


def store_triple(ref, seg, start, values, backward):
    channels = values.shape[1]
    before, after = shift_pair(values, seg.side)
    low, high = (after, before) if backward else (before, after)
    at = rows_at(seg.pad + start)
    ref[at, 0:channels] = low.astype(BF)
    ref[at, channels : 2 * channels] = values.astype(BF)
    ref[at, 2 * channels : 3 * channels] = high.astype(BF)


def zero_pads(ref, segs):
    columns = ref.shape[1]
    for seg in segs:
        ref[seg.pad - seg.side : seg.pad, :] = jnp.zeros((seg.side, columns), ref.dtype)
        ref[seg.pad + seg.pixels : seg.pad + seg.pixels + seg.side, :] = jnp.zeros((seg.side, columns), ref.dtype)


def conv_block(triple, weight, seg, start):
    width = triple.shape[1]
    out = None
    for a in range(3):
        term = mm(triple[rows_at(seg.pad + start + (a - 1) * seg.side), :], weight[a * width : (a + 1) * width, :])
        out = term if out is None else out + term
    return out


def conv_back_block(triple, crossed, seg, start):
    width = triple.shape[1]
    third = width // 3
    out = None
    for a in range(3):
        term = mm(
            triple[rows_at(seg.pad + start - (a - 1) * seg.side), :], crossed[a * third : (a + 1) * third, :], 1, 1
        )
        out = term if out is None else out + term
    return out


def cross_weight(source, target):
    channels = source.shape[1]

    def step(a, carry):
        for b in range(3):
            target[pl.ds(pl.multiple_of(a * channels, channels), channels), b * channels : (b + 1) * channels] = source[
                pl.ds(pl.multiple_of((3 * a + b) * channels, channels), channels), :
            ]
        return carry

    lax.fori_loop(0, 3, step, 0)


def conv_weight_grad(kept, triple, segs, store, columns, ticks):
    channels = kept.shape[1]
    first_col, last_col = columns
    width = last_col - first_col
    for a in range(3):
        ticks.get(a, lambda: None)()
        out = None
        for seg in segs:
            first = seg.pad + (a - 1) * seg.side
            span = slice(seg.pad, seg.pad + seg.pixels)
            if width == channels:
                right = triple[span, :]
            else:
                right = jnp.concatenate(
                    [triple[span, b * channels + first_col : b * channels + last_col] for b in range(3)], axis=1
                )
            term = mm(kept[first : first + seg.pixels, :], right, 0, 0)
            out = term if out is None else out + term
        for b in range(3):
            store((3 * a + b) * channels, first_col, out[:, b * width : (b + 1) * width])


class HeadPart:
    def __init__(self, refs, span, chunk, pair_row, half, at):
        self.qkv_t, self.datt_t, self.keyvalue, self.dkv = refs
        self.first, self.pixels, self.chunk = span.start, span.stop - span.start, chunk
        self.channels = self.datt_t.shape[0]
        self.head = self.channels // HEADS
        self.pair, self.half, self.at = pair_row, half, at
        self.row = pair_row + half * self.head
        self.scores, self.probs, self.d_scores = {}, {}, {}
        self.peak, self.sums, self.out, self.dq = None, 0.0, 0.0, 0.0

    def keys(self, n):
        return slice(self.first + n * self.chunk, self.first + (n + 1) * self.chunk)

    def last(self, n):
        return n == self.pixels // self.chunk - 1

    def score(self, n):
        width = 2 * self.head
        rows = pl.ds(self.pair, width)
        if n == 0:
            place = lax.broadcasted_iota(jnp.int32, (width, 1), 0)
            mine = (place < self.head) if self.half == 0 else (place >= self.head)
            self.q = jnp.where(mine, self.qkv_t[rows, self.at], 0).astype(BF)
            self.d_att = jnp.where(mine, self.datt_t[rows, self.at], 0).astype(F32)
        self.scores[n] = mm(self.keyvalue[self.keys(n), pl.ds(self.channels + self.pair, width)], self.q)
        peak = jnp.max(self.scores[n], axis=0, keepdims=True)
        self.peak = peak if self.peak is None else jnp.maximum(self.peak, peak)

    def attend(self, n):
        probs = jnp.exp(self.scores.pop(n) - self.peak)
        self.sums = self.sums + jnp.sum(probs, axis=0, keepdims=True)
        self.probs[n] = probs.astype(BF)
        values_t = self.qkv_t[pl.ds(2 * self.channels + self.row, self.head), self.keys(n)]
        self.out = self.out + mm(values_t, self.probs[n])
        if self.last(n):
            inverse = 1.0 / self.sums
            out = self.out * inverse
            self.d_att = (self.d_att * inverse).astype(BF)
            mine = self.d_att[self.half * self.head : (self.half + 1) * self.head].astype(F32)
            self.dots = jnp.sum(mine * out, axis=0, keepdims=True)
            self.qkv_t[pl.ds(self.row, self.head), self.at] = out.astype(BF)

    def back(self, n):
        width = 2 * self.head
        lanes = pl.ds(self.channels + self.pair, width)
        d_probs = mm(self.keyvalue[self.keys(n), pl.ds(2 * self.channels + self.pair, width)], self.d_att)
        self.d_scores[n] = (self.probs[n].astype(F32) * (d_probs - self.dots)).astype(BF)
        self.dkv[self.keys(n), lanes] += mm(self.probs.pop(n), self.d_att, 1, 1)

    def last_products(self, n):
        d_scores = self.d_scores.pop(n)
        self.dkv[self.keys(n), pl.ds(self.pair, 2 * self.head)] += mm(d_scores, self.q, 1, 1)
        keys_t = self.qkv_t[pl.ds(self.channels + self.row, self.head), self.keys(n)]
        self.dq = self.dq + mm(keys_t, d_scores)
        if self.last(n):
            self.datt_t[pl.ds(self.row, self.head), self.at] = (self.dq * (1.0 / math.sqrt(self.head))).astype(BF)


def attention(seg, block, chunk, keyvalue, qkv_t, datt_t, dkv):
    pair = 2 * datt_t.shape[0] // HEADS
    span = slice(seg.row, seg.row + seg.pixels)
    dkv[span, :] = jnp.zeros((seg.pixels, dkv.shape[1]), F32)

    def heads(index, carry):
        row = pl.multiple_of(index * pair, pair)
        parts = [
            HeadPart((qkv_t, datt_t, keyvalue, dkv), span, chunk, row, half, slice(first, first + block))
            for first in range(span.start, span.stop, block)
            for half in range(2)
        ]
        for k in range(-1, len(parts) + 2):
            for n in range(seg.pixels // chunk):
                if 0 <= k - 2 < len(parts):
                    parts[k - 2].last_products(n)
                if 0 <= k - 1 < len(parts):
                    parts[k - 1].back(n)
                if 0 <= k < len(parts):
                    parts[k].attend(n)
                if 0 <= k + 1 < len(parts):
                    parts[k + 1].score(n)
        return carry

    lax.fori_loop(0, HEADS // 2, heads, 0)


def block_body(sides, r, hook=lambda name: None, ticks=lambda name: {}):
    segs, rows_all, pad_all = make_segs(sides)
    ch = r.x.shape[1]
    x, g, out, grad = r.x, r.g, r.out, r.grad
    triple, kept0, kept1 = r.triple, r.kept0, r.kept1
    y0, res, wide = r.y0, r.res, r.wide
    gain = lambda i: r.params[i : i + 1, :]
    shift_row = lambda i: r.params[3 + i : 4 + i, :]
    groups = r.groups
    for ref in (triple, kept0, kept1):
        zero_pads(ref, segs)
    lane = lax.broadcasted_iota(jnp.int32, (ch, ch), 1)
    sub = lax.broadcasted_iota(jnp.int32, (ch, ch), 0)
    width = ch // GROUPS
    diff = sub // width - lane // width
    groups[...] = jnp.where(diff == 0, 1.0, 0.0).astype(BF)

    sums = []
    for seg in segs:
        def go(start, carry, seg=seg):
            return Moments.add(carry, x[rows_at(seg.row + start), :].astype(F32), start == 0)
        sums.append(each_block(seg, go, Moments.start(ch)))
    hook("shifts")
    stats0 = norm_stats(segs, sums, groups)
    for seg, (centre, inverse) in zip(segs, stats0):
        scale, shift = inverse * gain(0), shift_row(0)
        def go(start, carry, seg=seg, centre=centre, scale=scale, shift=shift):
            z = (x[rows_at(seg.row + start), :].astype(F32) - centre) * scale + shift
            a0 = z * sigmoid(z)
            store_triple(triple, seg, start, a0, False)
            kept0[rows_at(seg.pad + start), :] = a0.astype(BF)
            return carry
        each_block(seg, go, 0)

    hook("w0")
    sums = []
    for seg in segs:
        def go(start, carry, seg=seg):
            value = conv_block(triple, r.w0, seg, start) + shift_row(1)
            y0[rows_at(seg.row + start), :] = value
            return Moments.add(carry, value, start == 0)
        sums.append(each_block(seg, go, Moments.start(ch), ticks("conv0")))
    hook("conv0")
    stats1 = norm_stats(segs, sums, groups)
    hook("affine")
    mod = r.mod
    scales1, consts1 = [], []
    for seg, (centre, inverse) in zip(segs, stats1):
        stretch = mod[seg.index : seg.index + 1, :ch] + shift_row(2) + 1.0
        offset = mod[seg.index : seg.index + 1, ch:] + shift_row(3)
        scales1.append(gain(1) * stretch)
        shift = shift_row(4) * stretch + offset
        consts1.append((stretch, centre, inverse, inverse * scales1[-1], shift))
        _, _, _, scale, _ = consts1[-1]
        def go(start, carry, seg=seg, centre=centre, scale=scale, shift=shift):
            z = (y0[rows_at(seg.row + start), :] - centre) * scale + shift
            a1 = z * sigmoid(z)
            store_triple(triple, seg, start, a1, False)
            kept1[rows_at(seg.pad + start), :] = a1.astype(BF)
            return carry
        each_block(seg, go, 0)

    hook("w1")
    sums = []
    for seg in segs:
        def go(start, carry, seg=seg):
            at = rows_at(seg.row + start)
            value = conv_block(triple, r.w1, seg, start) + shift_row(5) + x[at, :].astype(F32)
            res[at, :] = value
            return Moments.add(carry, value, start == 0)
        sums.append(each_block(seg, go, Moments.start(ch), ticks("conv1")))
    stats2 = norm_stats(segs, sums, groups)

    hook("wqkv")
    hook("wproj")
    a2, kv, qkv_t, datt_t = r.a2, r.dqkv, r.qkv_t, r.datt_t
    w_qkv, w_proj = r.wqkv, r.wproj
    for seg, (centre, inverse) in zip(segs, stats2):
        scale, shift = inverse * gain(2), shift_row(6)
        def go(start, carry, seg=seg, centre=centre, scale=scale, shift=shift):
            at = rows_at(seg.row + start)
            normed = ((res[at, :] - centre) * scale + shift).astype(BF)
            a2[at, :] = normed
            lanes = pl.ds(pl.multiple_of(seg.row + start, BLK) if not isinstance(start, int) else seg.row + start, BLK)
            for part in range(3):
                value = mm(normed, w_qkv[:, part * ch : (part + 1) * ch])
                if part != 1:
                    value = value + shift_row(7 if part == 0 else 8)
                low = value.astype(BF)
                if part:
                    kv[at, part * ch : (part + 1) * ch] = low
                else:
                    low = low * (1.0 / math.sqrt(ch // HEADS))
                qkv_t[part * ch : (part + 1) * ch, lanes] = low.T
            datt_t[:, lanes] = mm(w_proj[...], g[at, :], 1, 1).astype(BF)
            return carry
        each_block(seg, go, 0)

    dkv = r.dkv
    for seg in segs:
        attention(seg, min(512, seg.pixels), min(256, seg.pixels), kv, qkv_t, datt_t, dkv)

    hook("att")
    dqkv = r.dqkv
    r.grad_proj(mm(qkv_t[0:ch, :], g[...]))
    hook("grad_proj")
    zero = jnp.zeros((8, ch), F32)
    sums2 = []
    q_sum, v_sum, g_sum = zero, zero, zero
    for seg, (centre, inverse) in zip(segs, stats2):
        def go(start, carry, seg=seg, centre=centre, inverse=inverse):
            s0, s1, q_sum, v_sum, g_sum = carry
            at = rows_at(seg.row + start)
            lanes = pl.ds(pl.multiple_of(seg.row + start, BLK) if not isinstance(start, int) else seg.row + start, BLK)
            g_sum = g_sum + fold(g[at, :].astype(F32))
            dq = datt_t[:, lanes].T
            dqkv[at, 0:ch] = dq
            dqkv[at, ch : 3 * ch] = dkv[at, :].astype(BF)
            q_sum = q_sum + fold(dq.astype(F32))
            v_sum = v_sum + fold(dkv[at, ch : 2 * ch])
            da2 = mm(dqkv[at, :], w_qkv[...], 1, 1)
            wide[at, :] = da2
            normal = (res[at, :] - centre) * inverse
            return (s0 + fold(da2), s1 + fold(da2 * normal), q_sum, v_sum, g_sum)
        s0, s1, q_sum, v_sum, g_sum = each_block(seg, go, (zero, zero, q_sum, v_sum, g_sum), ticks("out"))
        sums2.append((total(s0), total(s1)))
    r.grad_qkv(mm(a2[...], dqkv[...], 0, 0))
    hook("grad_qkv")
    terms2 = norm_back_terms(segs, sums2, stats2, [gain(2)] * len(segs), groups)
    y1_sum = zero
    for seg, (centre, inverse), (factor, const, slope) in zip(segs, stats2, terms2):
        def go(start, carry, seg=seg, centre=centre, factor=factor, const=const, slope=slope):
            at = rows_at(seg.row + start)
            d_res = g[at, :].astype(F32) + wide[at, :] * factor - const - (res[at, :] - centre) * slope
            dkv[at, 0:ch] = d_res
            store_triple(triple, seg, start, d_res, True)
            return carry + fold(d_res)
        y1_sum = each_block(seg, go, y1_sum, ticks("dr"))
    gain2 = sums2[0][1] + sums2[1][1]
    shift6 = sums2[0][0] + sums2[1][0]

    hook("dr")

    conv_weight_grad(kept1, triple, segs, r.grad1, (0, ch), ticks(("grad1", 0)))
    hook("grad1")
    cross_weight(r.w1, r.crossed)
    sums1 = []
    for seg, (stretch, centre, inverse, scale, shift) in zip(segs, consts1):
        def go(start, carry, seg=seg, centre=centre, inverse=inverse, scale=scale, shift=shift):
            s0, s1 = carry
            at = rows_at(seg.row + start)
            da1 = conv_back_block(triple, r.crossed, seg, start)
            off = y0[at, :] - centre
            z = off * scale + shift
            sig = sigmoid(z)
            dz = da1 * (sig * (1.0 + z * (1.0 - sig)))
            wide[at, :] = dz
            return (s0 + fold(dz), s1 + fold(dz * (off * inverse)))
        s0, s1 = each_block(seg, go, (zero, zero), ticks("back1"))
        sums1.append((total(s0), total(s1)))
    hook("back1")
    stats = [(centre, inverse) for _, centre, inverse, _, _ in consts1]
    terms1 = norm_back_terms(segs, sums1, stats, scales1, groups)
    y0_sum = zero
    for seg, (centre, inverse), (factor, const, slope) in zip(segs, stats, terms1):
        def go(start, carry, seg=seg, centre=centre, factor=factor, const=const, slope=slope):
            at = rows_at(seg.row + start)
            dy0 = wide[at, :] * factor - const - (y0[at, :] - centre) * slope
            store_triple(triple, seg, start, dy0, True)
            return carry + fold(dy0)
        y0_sum = each_block(seg, go, y0_sum, ticks("dy0"))
    dmod, gain1, shift4 = [], 0.0, 0.0
    for (s0, s1), (stretch, *_) in zip(sums1, consts1):
        dmod.append(jnp.concatenate([gain(1) * s1 + shift_row(4) * s0, s0], axis=1))
        gain1 = gain1 + stretch * s1
        shift4 = shift4 + stretch * s0
    dmod = [d.astype(BF).astype(F32) for d in dmod]
    dmod_sum = dmod[0] + dmod[1]
    r.grad_affine(dmod)

    hook("dy0")

    for n, columns in enumerate(r.columns):
        conv_weight_grad(kept0, triple, segs, r.grad0, columns, ticks(("grad0", n)))
        hook(("grad0", n))
    cross_weight(r.w0, r.crossed)
    sums0 = []
    for seg, (centre, inverse) in zip(segs, stats0):
        scale, shift = inverse * gain(0), shift_row(0)
        def go(start, carry, seg=seg, centre=centre, inverse=inverse, scale=scale, shift=shift):
            s0, s1 = carry
            at = rows_at(seg.row + start)
            da0 = conv_back_block(triple, r.crossed, seg, start)
            off = x[at, :].astype(F32) - centre
            z = off * scale + shift
            sig = sigmoid(z)
            dz = da0 * (sig * (1.0 + z * (1.0 - sig)))
            wide[at, :] = dz
            return (s0 + fold(dz), s1 + fold(dz * (off * inverse)))
        s0, s1 = each_block(seg, go, (zero, zero), ticks("back0"))
        sums0.append((total(s0), total(s1)))
    hook("back0")
    terms0 = norm_back_terms(segs, sums0, stats0, [gain(0)] * len(segs), groups)
    r.rows[...] = jnp.concatenate(
        [
            sums0[0][1] + sums0[1][1],
            gain1,
            gain2,
            sums0[0][0] + sums0[1][0],
            total(y0_sum),
            dmod_sum[:, :ch],
            dmod_sum[:, ch:],
            shift4,
            total(y1_sum),
            shift6,
            total(q_sum),
            total(v_sum),
            total(g_sum),
            jnp.zeros((3, ch), F32),
        ],
        axis=0,
    )
    hook("rows")
    for seg in segs:
        live = r.live(seg.index)
        def go(start, carry, seg=seg, live=live):
            at = rows_at(seg.row + start)
            lanes = pl.ds(pl.multiple_of(seg.row + start, BLK) if not isinstance(start, int) else seg.row + start, BLK)
            made = mm(qkv_t[0:ch, lanes], w_proj[...], 0, 0) + shift_row(9) + res[at, :]
            out[at, :] = jnp.where(live, made, 0.0).astype(BF)
            return carry
        each_block(seg, go, 0, ticks("late"))
    hook("late")
    for seg, (centre, inverse), (factor, const, slope) in zip(segs, stats0, terms0):
        def go(start, carry, seg=seg, centre=centre, factor=factor, const=const, slope=slope):
            at = rows_at(seg.row + start)
            off = x[at, :].astype(F32) - centre
            grad[at, :] = (dkv[at, 0:ch] + wide[at, :] * factor - const - off * slope).astype(BF)
            return carry
        each_block(seg, go, 0, ticks("grad"))


def block_scratch(sides, ch):
    _, rows, pads = make_segs(sides)
    return dict(
        triple=pltpu.VMEM((pads, 3 * ch), BF),
        kept0=pltpu.VMEM((pads, ch), BF),
        kept1=pltpu.VMEM((pads, ch), BF),
        y0=pltpu.VMEM((rows, ch), F32),
        res=pltpu.VMEM((rows, ch), F32),
        wide=pltpu.VMEM((rows, ch), F32),
        groups=pltpu.VMEM((ch, ch), BF),
        a2=pltpu.VMEM((rows, ch), BF),
        qkv_t=pltpu.VMEM((3 * ch, rows), BF),
        datt_t=pltpu.VMEM((ch, rows), BF),
        dkv=pltpu.VMEM((rows, 2 * ch), F32),
        dqkv=pltpu.VMEM((rows, 3 * ch), BF),
        crossed=pltpu.VMEM((3 * ch, 3 * ch), BF),
    )


MESH = pl.DeviceIdType.MESH
VMEM_LIMIT = 63 * 2**20
FLIPS = ("s", "x", "y", "d", "xs", "ys", "ds")
OTHER = {"x": "y", "y": "x"}
SMALL = ("p", "m", "n", "q")
WEIGHTS = ("w0", "w1", "wqkv", "wproj")


SCHEDULE = {
    "grad_qkv": ((0, 0), (1, 0)),
    ("dr", 0, 2): ((0, 1),),
    ("dr", 0, 3): ((1, 1),),
    "grad1": ((0, 2), (1, 2), (2, 0), (3, 0), (4, 0), (5, 0)),
    ("back1", 0, 1): ((2, 1), (3, 1), (0, 3), (1, 3)),
    ("back1", 0, 3): ((4, 1), (0, 4), (5, 1)),
    "back1": ((1, 4), (0, 5), (2, 2), (3, 2)),
    ("dy0", 1, 0): ((1, 5), (4, 2), (5, 2)),
    ("grad0", 0, 1): ((2, 3), (3, 3)),
    ("grad0", 0): ((4, 3), (5, 3), (12, 3), (6, 0), (7, 0), (2, 4), (8, 0), (9, 0)),
    ("grad0", 1, 1): ((6, 1), (7, 1)),
    ("grad0", 1, 2): ((3, 4),),
    ("grad0", 1): ((10, 0), (11, 0), (8, 1), (2, 5), (9, 1)),
    ("back0", 0, 1): ((4, 4), (3, 5), (6, 2), (7, 2)),
    ("back0", 0, 2): ((5, 4), (10, 1), (11, 1)),
    ("back0", 0, 3): ((4, 5), (8, 2), (7, 3), (6, 3), (9, 2), (12, 4)),
    ("back0", 1, 0): ((5, 5),),
    "back0": ((7, 4), (10, 2), (11, 2), (6, 4), (9, 3), (8, 3)),
    ("late", 0, 1): ((12, 5),),
    ("late", 0, 2): ((10, 3), (7, 5), (9, 4), (11, 3)),
    ("late", 1, 0): ((6, 5), (8, 4)),
    ("grad", 0, 0): ((9, 5), (10, 4), (13, 3)),
    ("grad", 0, 2): ((11, 4), (13, 4), (8, 5)),
}
TAIL = ((0, 6), (1, 6), (10, 5), (7, 6), (2, 6), (3, 6), (4, 6), (6, 6), (5, 6), (12, 6), (11, 5), (13, 5), (9, 6), (8, 6), (10, 6), (11, 6), (13, 6))


class Net:
    def __init__(self, names, send, recv):
        self.at = {name: i for i, name in enumerate(names)}
        self.send, self.recv, self.sent = send, recv, []

    def copy(self, name, src, dst, peer):
        i = self.at[name]
        return pltpu.make_async_remote_copy(
            src_ref=src,
            dst_ref=dst,
            send_sem=self.send.at[i],
            recv_sem=self.recv.at[i],
            device_id=peer,
            device_id_type=MESH,
        )

    def push(self, name, make):
        self.copy(name, *make()).start()
        self.sent.append((name, make))

    def take(self, name, dst, peer):
        self.copy(name, dst, dst, peer).wait_recv()

    def drain(self):
        for name, make in self.sent:
            self.copy(name, *make()).wait_send()
        self.sent = []


def spans(rows, pieces):
    tiles = rows // 16
    cuts = [16 * (tiles * i // pieces) for i in range(pieces)] + [rows]
    return [(a, b - a) for a, b in zip(cuts, cuts[1:])]


def column_spans(ch):
    return [(0, 2 * ch // 3), (2 * ch // 3, ch)]


def reduce_units(block, ch):
    units = [("both", 0, block["wqkv"], 0, 2 * ch, "x"), ("both", 0, block["wqkv"], 2 * ch, 2 * ch, "y")]
    for (first, count), axis in zip(spans(block["w1"], 4), "xyxy"):
        units.append(("w1", first, count, 0, ch, axis))
    for (low, high), pieces in zip(column_spans(ch), (4, 2)):
        for (first, count), axis in zip(spans(block["w0"], pieces), "xyxy"):
            units.append(("w0", first, count, low, high - low, axis))
    return units


OUT_STEPS = ("x0", "x1", "y0", "y1", "s", "d0", "d1", "zx", "zy", "zd", "sx", "sy", "sd", "ox", "oy", "od")


def transfer_names(in_units):
    names = [(-1 - i, t) for i in range(len(WEIGHTS)) for t in OUT_STEPS]
    names += [(i, t) for i in range(len(in_units)) for t in "abc"]
    names += [(i, t) for i in range(len(in_units) + 2) for t in ("z0", "z1", "z2")]
    return names + [(what, flip) for what in SMALL for flip in FLIPS]


def packed(rows, height):
    count, columns = rows.shape
    pieces = [rows[i : i + 1, j : j + 128] for i in range(count) for j in range(0, columns, 128)]
    return jnp.concatenate(pieces + [jnp.zeros((height - len(pieces), 128), rows.dtype)], axis=0)


def unpacked(values, count, columns):
    per = columns // 128
    return jnp.concatenate(
        [jnp.concatenate([values[i * per + j : i * per + j + 1, :] for j in range(per)], axis=1) for i in range(count)],
        axis=0,
    )


def fused_kernel(sides, block, r):
    segs, _, _ = make_segs(sides)
    ch = r.triple.shape[1] // 3
    wide_rows = 2 * ch
    in_units = reduce_units(block, ch)
    me, z = lax.axis_index("shard"), lax.axis_index("rep")
    core, px, py = me % 2, (me // 2) % 2, me // 4
    outer = (z == 0) | (z == 3)
    inner = jnp.logical_not(outer)

    def index(flip):
        fx = 1 - px if ("x" in flip or "d" in flip) else px
        fy = 1 - py if ("y" in flip or "d" in flip) else py
        fc = 1 - core if "s" in flip else core
        return (fy * 2 + fx) * 2 + fc

    at = {flip: index(flip) for flip in FLIPS + ("",)}
    peer = {flip: (at[flip], z) for flip in FLIPS}
    z_in, z_out, z_cross = (me, jnp.where(z < 2, 1, 2)), (me, jnp.where(z < 2, 0, 3)), (me, 3 - z)
    net = Net(transfer_names(in_units), r.send, r.recv)

    local = []

    def fetch(src, dst):
        copy = pltpu.make_async_copy(src, dst, r.local.at[len(local)])
        copy.start()
        local.append(copy)
        return copy

    got_x = [fetch(src, r.x.at[s.row : s.row + s.pixels, :]) for src, s in zip((r.big_x, r.small_x), segs)]

    barrier = pltpu.get_barrier_semaphore()
    for flip in FLIPS:
        pl.semaphore_signal(barrier, inc=1, device_id=peer[flip], device_id_type=MESH)

    @pl.when(outer)
    def _():
        pl.semaphore_signal(barrier, inc=1, device_id=z_in, device_id_type=MESH)

    @pl.when(inner)
    def _():
        pl.semaphore_signal(barrier, inc=1, device_id=z_out, device_id_type=MESH)
        pl.semaphore_signal(barrier, inc=1, device_id=z_cross, device_id_type=MESH)

    pl.semaphore_wait(barrier, jnp.where(outer, 8, 9))

    gathered = [getattr(r, name) for name in WEIGHTS]
    own = (r.own_w0, r.own_w1, r.own_wqkv, r.own_wproj)
    mine = {}
    side = z % 2
    z_peer = (me, z + 1 - 2 * side)

    def part(i, flip, first, count):
        third = own[i].shape[0] // 3
        at_third = {-1: side, 0: 2 * side, 1: 1, 2: 2 - 2 * side, 3: 0}[first]
        start = pl.multiple_of((at[flip] * 3 + at_third) * third, 16)
        return gathered[i].at[pl.ds(start, count * third), :]

    def own_part(i, first):
        third = own[i].shape[0] // 3
        return own[i].at[pl.ds(pl.multiple_of((2 * side if first == 0 else 1) * third, 16), third), :]

    def pass_on(i, step, flip, first, count, target):
        place = lambda: part(i, flip, first, count)
        net.push((-1 - i, step), lambda: (place(), place(), target))

    def out_start(i):
        for first in (0, 1):
            for axis in "xy":
                net.push(
                    (-1 - i, axis + str(first)),
                    lambda first=first, axis=axis: (own_part(i, first), part(i, "", first, 1), peer[axis]),
                )
        net.push((-1 - i, "s"), lambda: (own[i], part(i, "", 3, 3), peer["s"]))
        mine[i] = fetch(own[i], part(i, "", 3, 3))

    def took(i, step, flip, first, count, source):
        net.take((-1 - i, step), part(i, flip, first, count), source)

    def out_first(i):
        took(i, "x0", "x", 0, 1, peer["x"])
        pass_on(i, "d0", "x", 0, 1, peer["y"])
        pass_on(i, "zx", "x", 0, 1, z_peer)
        took(i, "y0", "y", 0, 1, peer["y"])
        pass_on(i, "zy", "y", 0, 1, z_peer)

    def out_second(i):
        took(i, "y1", "y", 1, 1, peer["y"])
        pass_on(i, "d1", "y", 1, 1, peer["x"])
        pass_on(i, "sy", "y", -1, 2, peer["s"])
        took(i, "x1", "x", 1, 1, peer["x"])
        pass_on(i, "sx", "x", -1, 2, peer["s"])

    def out_third(i):
        took(i, "d0", "d", 0, 1, peer["y"])
        pass_on(i, "zd", "d", 0, 1, z_peer)

    def out_fourth(i):
        took(i, "d1", "d", 1, 1, peer["x"])
        pass_on(i, "sd", "d", -1, 2, peer["s"])
        took(i, "zx", "x", 2, 1, z_peer)
        pass_on(i, "ox", "x", 2, 1, peer["s"])
        took(i, "zy", "y", 2, 1, z_peer)
        pass_on(i, "oy", "y", 2, 1, peer["s"])

    def out_fifth(i):
        took(i, "zd", "d", 2, 1, z_peer)
        pass_on(i, "od", "d", 2, 1, peer["s"])

    def out_end(i):
        mine[i].wait()
        took(i, "s", "s", 3, 3, peer["s"])
        for flip in "xyd":
            took(i, "s" + flip, flip + "s", -1, 2, peer["s"])
            took(i, "o" + flip, flip + "s", 2, 1, peer["s"])

    grads = dict(w0=r.grad_w0, w1=r.grad_w1, both=r.grad_both)
    results = dict(w0=r.out_w0, w1=r.out_w1, both=r.out_both)
    done = []

    def unit_ref(i):
        name, first, count, low, width, _ = in_units[i]
        return grads[name], (slice(first, first + count), slice(low, low + width))

    def in_core(i):
        ref, span = unit_ref(i)
        net.push((i, "a"), lambda i=i, ref=ref, span=span: (ref.at[(1 - core, slice(None), slice(None)) + span], r.ra[i], peer["s"]))

    def away(i):
        axis = in_units[i][5]
        return (slice(None), 1 - px) if axis == "x" else (1 - py, slice(None))

    def near(i):
        axis = in_units[i][5]
        return (slice(None), px) if axis == "x" else (py, slice(None))

    def cross(i):
        return (1 - py, px) if in_units[i][5] == "x" else (py, 1 - px)

    def add_to(ref, where, value):
        ref[where] = ref[where] + value

    def in_first(i):
        ref, span = unit_ref(i)
        axis = in_units[i][5]
        net.take((i, "a"), r.ra[i], peer["s"])
        add_to(ref, (core, slice(None), slice(None)) + span, r.ra[i][...])
        net.push((i, "b"), lambda i=i, ref=ref, span=span, axis=axis: (ref.at[(core,) + away(i) + span], r.rb[i], peer[axis]))

    def in_second(i):
        ref, span = unit_ref(i)
        axis = in_units[i][5]
        net.take((i, "b"), r.rb[i], peer[axis])
        add_to(ref, (core,) + near(i) + span, r.rb[i][...])
        net.push((i, "c"), lambda i=i, ref=ref, span=span, axis=axis: (ref.at[(core,) + cross(i) + span], r.rc[i], peer[OTHER[axis]]))

    def z_out_of(i):
        if i >= len(in_units):
            return ((r.own_affine, r.rza), (r.own_rows, r.rzr))[i - len(in_units)]
        ref, span = unit_ref(i)
        return ref.at[(core, py, px) + span], r.rz[i]

    def in_third(i):
        if i >= len(in_units):
            z_first(i)
            return
        ref, span = unit_ref(i)
        net.take((i, "c"), r.rc[i], peer[OTHER[in_units[i][5]]])
        add_to(ref, (core, py, px) + span, r.rc[i][...])
        z_first(i)

    def z_first(i):
        src, slots = z_out_of(i)

        @pl.when(outer)
        def _():
            net.copy((i, "z0"), src, slots.at[0], z_in).start()

    def z_second(i):
        src, slots = z_out_of(i)

        @pl.when(inner)
        def _():
            net.take((i, "z0"), slots.at[0], z_out)
            src[...] = src[...] + slots[0]
            net.copy((i, "z1"), src, slots.at[1], z_cross).start()

    def z_third(i):
        src, slots = z_out_of(i)

        @pl.when(inner)
        def _():
            net.take((i, "z1"), slots.at[1], z_cross)
            slots[0] = src[...] + slots[1]
            net.copy((i, "z2"), slots.at[0], slots.at[0], z_out).start()

    def z_end(i):
        src, slots = z_out_of(i)

        @pl.when(outer)
        def _():
            net.take((i, "z2"), slots.at[0], z_in)

        if i >= len(in_units):
            target = (r.out_affine, r.out_rows)[i - len(in_units)]
        else:
            name, first, count, low, width, _ = in_units[i]
            target = results[name].at[first : first + count, low : low + width]
        done.append(fetch(slots.at[0], target))

    def z_drain(chosen):
        for i in chosen:
            src, slots = z_out_of(i)

            @pl.when(outer)
            def _():
                net.copy((i, "z0"), src, slots.at[0], z_in).wait_send()

            @pl.when(inner)
            def _():
                net.copy((i, "z1"), src, slots.at[1], z_cross).wait_send()
                net.copy((i, "z2"), slots.at[0], slots.at[0], z_out).wait_send()

    STEPS = (in_core, in_first, in_second, in_third, z_second, z_third, z_end)

    def run(chosen):
        for i, step in chosen:
            STEPS[step](i)

    def keep(ref, rows_per):
        def store(row, col, value):
            height, width = value.shape
            start = row
            while start < row + height:
                owner = start // rows_per
                stop = min(row + height, (owner + 1) * rows_per)
                ref[owner % 2, owner // 4, (owner // 2) % 2, start - owner * rows_per : stop - owner * rows_per, col : col + width] = value[
                    start - row : stop - row, :
                ].astype(BF)
                start = stop

        return store

    r.grad = r.a2
    r.columns = column_spans(ch)
    r.live = lambda i: r.loads[0, i] > 0
    r.grad0, r.grad1 = keep(r.grad_w0, block["w0"]), keep(r.grad_w1, block["w1"])
    keep_both = keep(r.grad_both, block["wqkv"])
    r.grad_qkv = lambda value: keep_both(0, 0, value)
    r.grad_proj = lambda value: keep_both(0, 3 * ch, value)

    def exchange(what, src, slots):
        each = len(src.shape) == len(slots.shape)
        for flip in FLIPS:
            net.push(
                (what, flip),
                lambda flip=flip: (src.at[at[flip]] if each else src, slots.at[me], peer[flip]),
            )

    def exchanged(what, slots):
        for flip in FLIPS:
            net.take((what, flip), slots.at[at[flip]], peer[flip])

    def hook(name):
        if name == "shifts":
            copied_message.wait()
            exchanged("p", r.messages)
            own_width = 128
            per = ch // 8
            lane = lax.broadcasted_iota(jnp.int32, (8 * own_width, ch), 1)
            sub = lax.broadcasted_iota(jnp.int32, (8 * own_width, ch), 0)
            place = jnp.where(sub % own_width < per, (sub // own_width) * per + sub % own_width, -1)
            spread = jnp.where(lane == place, 1.0, 0.0).astype(BF)
            side_by_side = jnp.concatenate([r.messages[o, 0:16, :] for o in range(8)], axis=1)
            r.params[...] = mm(side_by_side, spread)
            everyone = r.messages[:, 16:32, :].astype(F32).reshape(16, 8, 128)
            chosen = lax.broadcasted_iota(jnp.int32, (16, 8, 128), 1) == me
            r.embeds[...] = jnp.sum(jnp.where(chosen, everyone, 0.0), axis=1).astype(BF)
            copied_affine.wait()
            partial = mm(r.embeds[...], r.waff[...])
            for o in range(8):
                r.mod_out[o] = packed(partial[2 * o : 2 * o + 2, :], 16)
            exchange("m", r.mod_out, r.mod_in)
            r.mod_in[pl.ds(me, 1)] = r.mod_out[pl.ds(me, 1)]
        if name == "w0":
            out_first(0)
            out_second(0)
            out_third(0)
            out_start(1)
            out_fourth(0)
            out_fifth(0)
            out_end(0)
            out_first(1)
        if name == "affine":
            exchanged("m", r.mod_in)
            r.mod[...] = unpacked(jnp.sum(r.mod_in[...], axis=0), 2, wide_rows)
            out_fourth(1)
        if name == "w1":
            for i in (2, 3):
                out_first(i)
                out_second(i)
            out_fifth(1)
            out_end(1)
        if name == "wqkv":
            for i in (2, 3):
                out_end(i)
            for copy in got_g:
                copy.wait()
            for seg in segs:
                rows = slice(seg.row, seg.row + seg.pixels)
                r.g[rows, :] = jnp.where(r.live(seg.index), r.g[rows, :], 0).astype(BF)
        if name == ("grad0", 0):
            exchanged("n", r.dmod_in)
            terms = unpacked_rows(r.dmod_in)
            grad = mm(r.embeds[...], terms, 0, 0)
            r.own_affine[...] = grad[0 : block["waff"], :].astype(BF)
        if name == "rows":
            exchange("q", r.rows, r.rows_in)
            r.rows_in[pl.ds(me, 1)] = r.rows[...][None]
        if name == "late":
            for seg, out in zip(segs, (r.big_out, r.small_out)):
                done.append(fetch(r.out.at[seg.row : seg.row + seg.pixels, :], out))
            exchanged("q", r.rows_in)
            sums = jnp.concatenate(three_parts(jnp.sum(r.rows_in[...], axis=0)), axis=0).astype(BF)
            lane = lax.broadcasted_iota(jnp.int32, (ch, 128), 1)
            sub = lax.broadcasted_iota(jnp.int32, (ch, 128), 0)
            per = ch // 8
            cut = mm(sums, jnp.where((sub - per * me == lane) & (lane < per), 1.0, 0.0).astype(BF))
            r.own_rows[...] = cut[0:16] + cut[16:32] + cut[32:48]
        run(SCHEDULE.get(name, ()))

    def unpacked_rows(ref):
        values = ref[...].astype(F32)
        return jnp.concatenate([unpacked(values[o], 2, wide_rows) for o in range(8)], axis=0).astype(BF)

    def ticks(name):
        if name == "conv0":
            return {
                (0, 1): lambda: out_second(1),
                (1, 0): lambda: (out_third(1), out_start(2), out_start(3)),
            }
        if name == "conv1":
            return {
                (0, 1): lambda: (out_third(2), out_third(3)),
                (0, 2): lambda: (out_fourth(2), out_fourth(3)),
                (1, 0): lambda: (out_fifth(2), out_fifth(3)),
            }
        at_rows = type(name) is str
        due = {
            (key[1:] if at_rows else key[2]): chosen
            for key, chosen in SCHEDULE.items()
            if type(key) is tuple and len(key) == 3 and (key[0] == name if at_rows else key[:2] == name)
        }
        return {where: lambda chosen=chosen: run(chosen) for where, chosen in due.items()}

    def grad_affine(rows):
        r.dmod[...] = packed(jnp.concatenate(rows, axis=0), 16).astype(BF)
        exchange("n", r.dmod, r.dmod_in)
        r.dmod_in[pl.ds(me, 1)] = r.dmod[...][None]

    r.grad_affine = grad_affine
    exchange("p", r.message, r.messages)
    copied_message = fetch(r.message, r.messages.at[me])
    out_start(0)
    r.waff[...] = jnp.zeros_like(r.waff)
    copied_affine = fetch(r.own_waff, r.waff.at[0 : block["waff"], :])
    got_g = [fetch(src, r.g.at[s.row : s.row + s.pixels, :]) for src, s in zip((r.big_g, r.small_g), segs)]
    for copy in got_x:
        copy.wait()
    block_body(sides, r, hook, ticks)

    for seg, out in zip(segs, (r.big_grad, r.small_grad)):
        done.append(fetch(r.grad.at[seg.row : seg.row + seg.pixels, :], out))
    run(TAIL)
    z_drain(range(len(in_units) + 2))
    net.drain()
    for copy in done:
        copy.wait()


def embed_rows(class_table, sigma_table, labels, sigmas):
    summed = class_table[labels].astype(F32) + sigma_table[sigmas].astype(F32)
    return jax.nn.silu(summed).astype(BF)


def named(names, refs):
    return dict(zip(names, refs))


def fused_call(sides, ch, arrays):
    block = dict(
        w0=arrays["own_w0"].shape[0],
        w1=arrays["own_w1"].shape[0],
        waff=arrays["own_waff"].shape[0],
        wqkv=arrays["own_wqkv"].shape[0],
        wproj=arrays["own_wproj"].shape[0],
    )
    segs, rows, _ = make_segs(sides)
    in_units = reduce_units(block, ch)
    width = dict(w0=ch, w1=ch, wqkv=3 * ch, wproj=ch)
    buffer = lambda *shape: pltpu.VMEM(shape, BF)
    wide_buffer = lambda *shape: pltpu.VMEM(shape, F32)
    whole = {name: buffer(8 * block[name], width[name]) for name in WEIGHTS}
    copies = len(transfer_names(in_units))
    scratch = dict(
        block_scratch(sides, ch),
        **whole,
        grad_w0=buffer(2, 2, 2, block["w0"], ch),
        grad_w1=buffer(2, 2, 2, block["w1"], ch),
        grad_both=buffer(2, 2, 2, block["wqkv"], 4 * ch),
        x=buffer(rows, ch),
        g=buffer(rows, ch),
        out=buffer(rows, ch),
        params=wide_buffer(16, ch),
        messages=buffer(8, 32, 128),
        embeds=buffer(16, 128),
        waff=buffer(128, 2 * ch),
        mod_out=wide_buffer(8, 16, 128),
        mod_in=wide_buffer(8, 16, 128),
        mod=wide_buffer(2, 2 * ch),
        dmod=buffer(16, 128),
        dmod_in=buffer(8, 16, 128),
        own_affine=buffer(block["waff"], 2 * ch),
        rza=buffer(2, block["waff"], 2 * ch),
        rows=wide_buffer(16, ch),
        rows_in=wide_buffer(8, 16, ch),
        own_rows=wide_buffer(16, 128),
        rzr=wide_buffer(2, 16, 128),
        send=pltpu.SemaphoreType.DMA((copies,)),
        recv=pltpu.SemaphoreType.DMA((copies,)),
        local=pltpu.SemaphoreType.DMA((48,)),
    )
    slots = [
        [buffer(2, 2, n, w) for _, _, n, _, w, _ in in_units],
        [buffer(2, n, w) for _, _, n, _, w, _ in in_units],
        [buffer(n, w) for _, _, n, _, w, _ in in_units],
        [buffer(2, n, w) for _, _, n, _, w, _ in in_units],
    ]
    big, small = segs[0].pixels, segs[1].pixels
    outs = dict(
        big_out=((big, ch), BF),
        small_out=((small, ch), BF),
        big_grad=((big, ch), BF),
        small_grad=((small, ch), BF),
        out_rows=((16, 128), F32),
        out_affine=((block["waff"], 2 * ch), BF),
        out_w0=((block["w0"], ch), BF),
        out_w1=((block["w1"], ch), BF),
        out_both=((block["wqkv"], 4 * ch), BF),
    )
    names = list(arrays) + list(outs) + list(scratch)

    def kernel(*refs):
        r = types.SimpleNamespace(**dict(zip(names, refs)))
        rest = list(refs[len(names) :])
        n = len(in_units)
        r.ra, r.rb, r.rc, r.rz = rest[:n], rest[n : 2 * n], rest[2 * n : 3 * n], rest[3 * n :]
        fused_kernel(sides, block, r)

    results = pl.pallas_call(
        kernel,
        out_shape=[jax.ShapeDtypeStruct(*shape) for shape in outs.values()],
        in_specs=[pl.BlockSpec(memory_space=pltpu.SMEM)] + [pl.BlockSpec(memory_space=pl.ANY)] * (len(arrays) - 1),
        out_specs=[pl.BlockSpec(memory_space=pl.ANY)] * len(outs),
        scratch_shapes=list(scratch.values()) + sum(slots, []),
        compiler_params=pltpu.CompilerParams(
            collective_id=0, has_side_effects=True, vmem_limit_bytes=VMEM_LIMIT
        ),
    )(*arrays.values())
    return results


def finish_call(results, per):
    images, both = results[:4], results[8]
    ch = both.shape[1] // 4
    outs = [jax.ShapeDtypeStruct(image.shape, image.dtype) for image in images]
    shapes = [(3, per), (10, per)] + [weight.shape for weight in results[5:8]]
    shapes += [(both.shape[0], 3 * ch), (both.shape[0], ch)]
    outs += [jax.ShapeDtypeStruct(shape, F32) for shape in shapes]
    total_in, total_out = len(results), len(outs)

    def kernel(*refs):
        sources, targets = refs[:total_in], refs[total_in : total_in + total_out]
        rest = refs[total_in + total_out :]
        held, made, sems = rest[:total_in], rest[total_in:-1], rest[-1]
        inward = [pltpu.make_async_copy(s, h, sems.at[i]) for i, (s, h) in enumerate(zip(sources, held))]
        for copy in inward:
            copy.start()
        outward = []

        def send(source, target):
            copy = pltpu.make_async_copy(source, target, sems.at[total_in + len(outward)])
            copy.start()
            outward.append(copy)

        for i in (8, 5, 6, 7):
            inward[i].wait()
            if i < 8:
                made[i - 3][...] = held[i][...].astype(F32)
                send(made[i - 3], targets[i + 1])
            else:
                made[5][...] = held[i][:, 0 : 3 * ch].astype(F32)
                made[6][...] = held[i][:, 3 * ch :].astype(F32)
                send(made[5], targets[9])
                send(made[6], targets[10])
        for i in range(4):
            inward[i].wait()
            send(held[i], targets[i])
        inward[4].wait()
        made[0][...] = held[4][0:3, 0:per]
        made[1][...] = held[4][3:13, 0:per]
        send(made[0], targets[4])
        send(made[1], targets[5])
        for copy in outward:
            copy.wait()

    any_spec = pl.BlockSpec(memory_space=pl.ANY)
    return pl.pallas_call(
        kernel,
        out_shape=outs,
        in_specs=[any_spec] * total_in,
        out_specs=[any_spec] * total_out,
        scratch_shapes=[pltpu.VMEM(array.shape, array.dtype) for array in results]
        + [pltpu.VMEM(out.shape, out.dtype) for out in outs[4:]]
        + [pltpu.SemaphoreType.DMA((total_in + total_out,))],
        compiler_params=pltpu.CompilerParams(vmem_limit_bytes=VMEM_LIMIT),
    )(*results)


def plain_call(sides, ch, arrays):
    _, rows, _ = make_segs(sides)
    scratch = dict(
        block_scratch(sides, ch), mod=pltpu.VMEM((16, 2 * ch), F32), masked=pltpu.VMEM((rows, ch), BF)
    )
    outs = dict(
        out=((rows, ch), BF),
        grad=((rows, ch), BF),
        terms0=((9 * ch, ch), BF),
        terms1=((9 * ch, ch), BF),
        affine=((2 * ch, 2 * ch), BF),
        terms_qkv=((ch, 3 * ch), BF),
        terms_proj=((ch, ch), BF),
        rows=((16, ch), F32),
    )
    names = list(arrays) + list(outs) + list(scratch)

    def kernel(*refs):
        r = types.SimpleNamespace(**dict(zip(names, refs)))
        segs, _, _ = make_segs(sides)
        given = r.g
        r.live = lambda i: r.loads[0, i] > 0
        r.g = r.masked
        r.columns = [(0, ch)]
        for seg in segs:
            span = slice(seg.row, seg.row + seg.pixels)
            r.masked[span, :] = jnp.where(r.live(seg.index), given[span, :], 0).astype(BF)

        def hook(name):
            if name == "affine":
                r.mod[...] = mm(r.emb[...], r.waff[...])

        def keep(ref):
            def store(row, col, value):
                ref[row : row + value.shape[0], col : col + value.shape[1]] = value.astype(BF)

            return store

        def grad_affine(terms):
            zeros = jnp.zeros((14, 2 * ch), F32)
            r.affine[...] = mm(r.emb[...], jnp.concatenate(terms + [zeros], axis=0).astype(BF), 0, 0).astype(BF)

        r.grad0, r.grad1 = keep(r.terms0), keep(r.terms1)
        r.grad_qkv = lambda value: keep(r.terms_qkv)(0, 0, value)
        r.grad_proj = lambda value: keep(r.terms_proj)(0, 0, value)
        r.grad_affine = grad_affine
        block_body(sides, r, hook)

    return pl.pallas_call(
        kernel,
        out_shape=[jax.ShapeDtypeStruct(*shape) for shape in outs.values()],
        in_specs=[pl.BlockSpec(memory_space=pltpu.SMEM)]
        + [pl.BlockSpec(memory_space=pltpu.VMEM)] * (len(arrays) - 1),
        out_specs=[pl.BlockSpec(memory_space=pltpu.VMEM)] * len(outs),
        scratch_shapes=list(scratch.values()),
        compiler_params=pltpu.CompilerParams(vmem_limit_bytes=VMEM_LIMIT),
    )(*arrays.values())


def on_device(
    fused,
    big_images,
    small_images,
    big_labels,
    small_labels,
    big_sigmas,
    small_sigmas,
    loads,
    class_table,
    sigma_table,
    norm_gains,
    biases,
    w_conv0,
    w_conv1,
    w_affine,
    w_qkv,
    w_proj,
    big_cotangent,
    small_cotangent,
):
    sides = (big_images.shape[1], small_images.shape[1])
    ch = big_images.shape[-1]
    flat = lambda array: array.reshape(-1, ch)
    big_embed = embed_rows(class_table, sigma_table, big_labels, big_sigmas)
    small_embed = embed_rows(class_table, sigma_table, small_labels, small_sigmas)
    emb = jnp.concatenate([big_embed, small_embed], axis=0)
    own_rows = jnp.concatenate([norm_gains, biases], axis=0)
    shapes = [big_images.shape, small_images.shape] * 2
    if fused:
        per = own_rows.shape[1]
        slices = emb.reshape(16, -1)
        message = jnp.concatenate(
            [
                jnp.pad(own_rows, ((0, 3), (0, 128 - per))),
                jnp.pad(slices, ((0, 0), (0, 128 - slices.shape[1]))),
            ],
            axis=0,
        )
        made = fused_call(
            sides,
            ch,
            dict(
                loads=loads,
                big_x=flat(big_images),
                small_x=flat(small_images),
                big_g=flat(big_cotangent),
                small_g=flat(small_cotangent),
                message=message,
                own_w0=w_conv0,
                own_w1=w_conv1,
                own_waff=w_affine,
                own_wqkv=w_qkv,
                own_wproj=w_proj,
            ),
        )
        made = finish_call(made, per)
        images, gains, shifts = made[:4], made[4], made[5]
        affine, first, second, qkv, proj = made[6:]
        weights = [first, second, affine, qkv, proj]
    else:
        gather = lambda array, axis=0: lax.all_gather(array, "shard", axis=axis, tiled=True)
        out, grad, terms0, terms1, affine, terms_qkv, terms_proj, rows = plain_call(
            sides,
            ch,
            dict(
                loads=loads,
                x=jnp.concatenate([flat(big_images), flat(small_images)], axis=0),
                g=jnp.concatenate([flat(big_cotangent), flat(small_cotangent)], axis=0),
                emb=jnp.pad(emb, ((0, 14), (0, 0))),
                params=jnp.pad(gather(own_rows, 1).astype(F32), ((0, 3), (0, 0))),
                w0=gather(w_conv0),
                w1=gather(w_conv1),
                waff=gather(w_affine),
                wqkv=gather(w_qkv),
                wproj=gather(w_proj),
            ),
        )

        def owned(terms, axis=0):
            mine = lax.psum_scatter(terms, "shard", scatter_dimension=axis, tiled=True)
            return lax.psum(mine, "rep").astype(F32)

        big = sides[0] * sides[0]
        images = [out[:big], out[big:], grad[:big], grad[big:]]
        sums = owned(rows, 1)
        gains, shifts = sums[:3], sums[3:13]
        weights = [owned(terms) for terms in (terms0, terms1, affine, terms_qkv, terms_proj)]
    return tuple(image.reshape(shape) for image, shape in zip(images, shapes)) + (gains, shifts, *weights)


def solution(mesh):
    fused = mesh.shape["shard"] == 8 and mesh.shape["rep"] == 4
    split = P(("shard", "rep"))
    image = P(("shard", "rep"), None, None, None)
    rows, columns = P("shard", None), P(None, "shard")
    return jax.shard_map(
        lambda *arrays: on_device(fused, *arrays),
        mesh=mesh,
        in_specs=(image, image, split, split, split, split, P(("shard", "rep"), None), P(), P(), columns, columns)
        + (rows,) * 5
        + (image, image),
        out_specs=(image,) * 4 + (columns,) * 2 + (rows,) * 5,
        check_vma=False,
    )
```

```python
import math
import types

import jax
import jax.numpy as jnp
from jax import lax
from jax.experimental import pallas as pl
from jax.experimental.pallas import tpu as pltpu
from jax.sharding import PartitionSpec as P

HEADS = 6
GROUPS = 32
EPSILON = 1e-05
BF = jnp.bfloat16
F32 = jnp.float32
BLK = 256


def mm(left, right, lc=1, rc=0):
    return lax.dot_general(left, right, (((lc,), (rc,)), ((), ())), preferred_element_type=F32)


def fold(values):
    rows, cols = values.shape
    return jnp.sum(values.reshape(rows // 8, 8, cols), axis=0)


def total(folded):
    return jnp.sum(folded, axis=0, keepdims=True)


def sigmoid(z):
    return 0.5 * jnp.tanh(0.5 * z) + 0.5


class Seg:
    def __init__(self, index, row, pad, side):
        self.index, self.row, self.pad, self.side = index, row, pad, side
        self.pixels = side * side


def make_segs(sides):
    segs, row, pad = [], 0, 0
    for index, side in enumerate(sides):
        segs.append(Seg(index, row, pad + side, side))
        row += side * side
        pad += side * side + 2 * side
    return segs, row, pad


def each_block(seg, body, carry, ticks=None):
    count = seg.pixels // BLK
    due = {n: act for (image, n), act in (ticks or {}).items() if image == seg.index}
    if count == 1:
        for act in due.values():
            act()
        return body(0, carry)

    def step(i, c):
        for n, act in due.items():

            @pl.when(i == n)
            def _(act=act):
                act()

        return body(pl.multiple_of(i * BLK, BLK), c)

    return lax.fori_loop(0, count, step, carry)


def rows_at(start, size=BLK):
    return pl.ds(pl.multiple_of(start, 16) if not isinstance(start, int) else start, size)


def three_parts(value):
    high = value.astype(BF).astype(F32)
    mid = (value - high).astype(BF).astype(F32)
    return [high, mid, (value - high - mid).astype(BF).astype(F32)]


def group_mean(rows, group_ref):
    count, channels = len(rows), rows[0].shape[1]
    parts = []
    for row in rows:
        parts += three_parts(row)
    padded = -(-3 * count // 16) * 16
    parts.append(jnp.zeros((padded - 3 * count, channels), F32))
    stacked = jnp.concatenate(parts, axis=0).astype(BF)
    sums = mm(stacked, group_ref[...]) * (GROUPS / channels)
    return [total(sums[3 * i : 3 * i + 3]) for i in range(count)]


def shift_pair(values, side):
    rows = values.shape[0]
    place = lax.broadcasted_iota(jnp.int32, (rows, 1), 0) % side
    before = jnp.where(place == 0, 0.0, pltpu.roll(values, 1, 0))
    after = jnp.where(place == side - 1, 0.0, pltpu.roll(values, rows - 1, 0))
    return before, after


class Moments:
    @staticmethod
    def start(channels):
        return (jnp.zeros((1, channels), F32), jnp.zeros((8, channels), F32), jnp.zeros((8, channels), F32))

    @staticmethod
    def add(carry, values, first):
        about, once, twice = carry
        about = jnp.where(first, values[0:1], about)
        off = values - about
        return (about, once + fold(off), twice + fold(off * off))


def norm_stats(segs, sums, group_ref):
    means, variances = [], []
    for seg, (about, once, twice) in zip(segs, sums):
        off = total(once) * (1.0 / seg.pixels)
        means.append(about + off)
        variances.append(jnp.maximum(total(twice) * (1.0 / seg.pixels) - off * off, 0.0))
    centres = group_mean(means, group_ref)
    spreads = group_mean(
        [v + (m - c) * (m - c) for v, m, c in zip(variances, means, centres)], group_ref
    )
    return [(c, lax.rsqrt(s + EPSILON)) for c, s in zip(centres, spreads)]


def norm_back_terms(segs, sums, stats, scales, group_ref):
    rows = []
    for seg, (s0, s1), scale in zip(segs, sums, scales):
        rows += [scale * s0 * (1.0 / seg.pixels), scale * s1 * (1.0 / seg.pixels)]
    means = group_mean(rows, group_ref)
    result = []
    for i, ((centre, inverse), scale) in enumerate(zip(stats, scales)):
        result.append((inverse * scale, inverse * means[2 * i], inverse * inverse * means[2 * i + 1]))
    return result


def store_triple(ref, seg, start, values, backward):
    channels = values.shape[1]
    before, after = shift_pair(values, seg.side)
    low, high = (after, before) if backward else (before, after)
    at = rows_at(seg.pad + start)
    ref[at, 0:channels] = low.astype(BF)
    ref[at, channels : 2 * channels] = values.astype(BF)
    ref[at, 2 * channels : 3 * channels] = high.astype(BF)


def zero_pads(ref, segs):
    columns = ref.shape[1]
    for seg in segs:
        ref[seg.pad - seg.side : seg.pad, :] = jnp.zeros((seg.side, columns), ref.dtype)
        ref[seg.pad + seg.pixels : seg.pad + seg.pixels + seg.side, :] = jnp.zeros((seg.side, columns), ref.dtype)


def conv_block(triple, weight, seg, start):
    width = triple.shape[1]
    out = None
    for a in range(3):
        term = mm(triple[rows_at(seg.pad + start + (a - 1) * seg.side), :], weight[a * width : (a + 1) * width, :])
        out = term if out is None else out + term
    return out


def conv_back_block(triple, crossed, seg, start):
    width = triple.shape[1]
    third = width // 3
    out = None
    for a in range(3):
        term = mm(
            triple[rows_at(seg.pad + start - (a - 1) * seg.side), :], crossed[a * third : (a + 1) * third, :], 1, 1
        )
        out = term if out is None else out + term
    return out


def cross_weight(source, target):
    channels = source.shape[1]

    def step(a, carry):
        for b in range(3):
            target[pl.ds(pl.multiple_of(a * channels, channels), channels), b * channels : (b + 1) * channels] = source[
                pl.ds(pl.multiple_of((3 * a + b) * channels, channels), channels), :
            ]
        return carry

    lax.fori_loop(0, 3, step, 0)


def conv_weight_grad(kept, triple, segs, store, columns, ticks):
    channels = kept.shape[1]
    first_col, last_col = columns
    width = last_col - first_col
    for a in range(3):
        ticks.get(a, lambda: None)()
        out = None
        for seg in segs:
            first = seg.pad + (a - 1) * seg.side
            span = slice(seg.pad, seg.pad + seg.pixels)
            if width == channels:
                right = triple[span, :]
            else:
                right = jnp.concatenate(
                    [triple[span, b * channels + first_col : b * channels + last_col] for b in range(3)], axis=1
                )
            term = mm(kept[first : first + seg.pixels, :], right, 0, 0)
            out = term if out is None else out + term
        for b in range(3):
            store((3 * a + b) * channels, first_col, out[:, b * width : (b + 1) * width])


class HeadPart:
    def __init__(self, refs, span, chunk, pair_row, half, at):
        self.qkv_t, self.datt_t, self.keyvalue, self.dkv = refs
        self.first, self.pixels, self.chunk = span.start, span.stop - span.start, chunk
        self.channels = self.datt_t.shape[0]
        self.head = self.channels // HEADS
        self.pair, self.half, self.at = pair_row, half, at
        self.row = pair_row + half * self.head
        self.scores, self.probs, self.d_scores = {}, {}, {}
        self.peak, self.sums, self.out, self.dq = None, 0.0, 0.0, 0.0

    def keys(self, n):
        return slice(self.first + n * self.chunk, self.first + (n + 1) * self.chunk)

    def last(self, n):
        return n == self.pixels // self.chunk - 1

    def score(self, n):
        width = 2 * self.head
        rows = pl.ds(self.pair, width)
        if n == 0:
            place = lax.broadcasted_iota(jnp.int32, (width, 1), 0)
            mine = (place < self.head) if self.half == 0 else (place >= self.head)
            self.q = jnp.where(mine, self.qkv_t[rows, self.at], 0).astype(BF)
            self.d_att = jnp.where(mine, self.datt_t[rows, self.at], 0).astype(F32)
        self.scores[n] = mm(self.keyvalue[self.keys(n), pl.ds(self.channels + self.pair, width)], self.q)
        peak = jnp.max(self.scores[n], axis=0, keepdims=True)
        self.peak = peak if self.peak is None else jnp.maximum(self.peak, peak)

    def attend(self, n):
        probs = jnp.exp(self.scores.pop(n) - self.peak)
        self.sums = self.sums + jnp.sum(probs, axis=0, keepdims=True)
        self.probs[n] = probs.astype(BF)
        values_t = self.qkv_t[pl.ds(2 * self.channels + self.row, self.head), self.keys(n)]
        self.out = self.out + mm(values_t, self.probs[n])
        if self.last(n):
            inverse = 1.0 / self.sums
            out = self.out * inverse
            self.d_att = (self.d_att * inverse).astype(BF)
            mine = self.d_att[self.half * self.head : (self.half + 1) * self.head].astype(F32)
            self.dots = jnp.sum(mine * out, axis=0, keepdims=True)
            self.qkv_t[pl.ds(self.row, self.head), self.at] = out.astype(BF)

    def back(self, n):
        width = 2 * self.head
        lanes = pl.ds(self.channels + self.pair, width)
        d_probs = mm(self.keyvalue[self.keys(n), pl.ds(2 * self.channels + self.pair, width)], self.d_att)
        self.d_scores[n] = (self.probs[n].astype(F32) * (d_probs - self.dots)).astype(BF)
        self.dkv[self.keys(n), lanes] += mm(self.probs.pop(n), self.d_att, 1, 1)

    def last_products(self, n):
        d_scores = self.d_scores.pop(n)
        self.dkv[self.keys(n), pl.ds(self.pair, 2 * self.head)] += mm(d_scores, self.q, 1, 1)
        keys_t = self.qkv_t[pl.ds(self.channels + self.row, self.head), self.keys(n)]
        self.dq = self.dq + mm(keys_t, d_scores)
        if self.last(n):
            self.datt_t[pl.ds(self.row, self.head), self.at] = (self.dq * (1.0 / math.sqrt(self.head))).astype(BF)


def attention(segs, keyvalue, qkv_t, datt_t, dkv):
    pair = 2 * datt_t.shape[0] // HEADS
    dkv[...] = jnp.zeros(dkv.shape, F32)

    def heads(index, carry):
        row = pl.multiple_of(index * pair, pair)
        parts = []
        for seg in segs:
            span = slice(seg.row, seg.row + seg.pixels)
            block, chunk = min(512, seg.pixels), min(256, seg.pixels)
            for first in range(span.start, span.stop, block):
                for half in range(2):
                    at = slice(first, first + block)
                    parts.append(HeadPart((qkv_t, datt_t, keyvalue, dkv), span, chunk, row, half, at))

        def step(k, what, n):
            if 0 <= k < len(parts) and n < parts[k].pixels // parts[k].chunk:
                getattr(parts[k], what)(n)

        chunks = max(part.pixels // part.chunk for part in parts)
        for k in range(-1, len(parts) + 2):
            for n in range(chunks):
                step(k - 2, "last_products", n)
                step(k - 1, "back", n)
                step(k, "attend", n)
                step(k + 1, "score", n)
        return carry

    lax.fori_loop(0, HEADS // 2, heads, 0)


def block_body(sides, r, hook=lambda name: None, ticks=lambda name: {}):
    segs, rows_all, pad_all = make_segs(sides)
    ch = r.x.shape[1]
    x, g, out, grad = r.x, r.g, r.out, r.grad
    triple, kept0, kept1 = r.triple, r.kept0, r.kept1
    y0, res, wide = r.y0, r.res, r.wide
    gain = lambda i: r.params[i : i + 1, :]
    shift_row = lambda i: r.params[3 + i : 4 + i, :]
    groups = r.groups
    for ref in (triple, kept0, kept1):
        zero_pads(ref, segs)
    lane = lax.broadcasted_iota(jnp.int32, (ch, ch), 1)
    sub = lax.broadcasted_iota(jnp.int32, (ch, ch), 0)
    width = ch // GROUPS
    diff = sub // width - lane // width
    groups[...] = jnp.where(diff == 0, 1.0, 0.0).astype(BF)

    sums = []
    for seg in segs:
        def go(start, carry, seg=seg):
            return Moments.add(carry, x[rows_at(seg.row + start), :].astype(F32), start == 0)
        sums.append(each_block(seg, go, Moments.start(ch)))
    hook("shifts")
    stats0 = norm_stats(segs, sums, groups)
    for seg, (centre, inverse) in zip(segs, stats0):
        scale, shift = inverse * gain(0), shift_row(0)
        def go(start, carry, seg=seg, centre=centre, scale=scale, shift=shift):
            z = (x[rows_at(seg.row + start), :].astype(F32) - centre) * scale + shift
            a0 = z * sigmoid(z)
            store_triple(triple, seg, start, a0, False)
            kept0[rows_at(seg.pad + start), :] = a0.astype(BF)
            return carry
        each_block(seg, go, 0)

    hook("w0")
    sums = []
    for seg in segs:
        def go(start, carry, seg=seg):
            value = conv_block(triple, r.w0, seg, start) + shift_row(1)
            y0[rows_at(seg.row + start), :] = value
            return Moments.add(carry, value, start == 0)
        sums.append(each_block(seg, go, Moments.start(ch), ticks("conv0")))
    hook("conv0")
    stats1 = norm_stats(segs, sums, groups)
    hook("affine")
    mod = r.mod
    scales1, consts1 = [], []
    for seg, (centre, inverse) in zip(segs, stats1):
        stretch = mod[seg.index : seg.index + 1, :ch] + shift_row(2) + 1.0
        offset = mod[seg.index : seg.index + 1, ch:] + shift_row(3)
        scales1.append(gain(1) * stretch)
        shift = shift_row(4) * stretch + offset
        consts1.append((stretch, centre, inverse, inverse * scales1[-1], shift))
        _, _, _, scale, _ = consts1[-1]
        def go(start, carry, seg=seg, centre=centre, scale=scale, shift=shift):
            z = (y0[rows_at(seg.row + start), :] - centre) * scale + shift
            a1 = z * sigmoid(z)
            store_triple(triple, seg, start, a1, False)
            kept1[rows_at(seg.pad + start), :] = a1.astype(BF)
            return carry
        each_block(seg, go, 0, ticks("a1"))

    hook("w1")
    sums = []
    for seg in segs:
        def go(start, carry, seg=seg):
            at = rows_at(seg.row + start)
            value = conv_block(triple, r.w1, seg, start) + shift_row(5) + x[at, :].astype(F32)
            res[at, :] = value
            return Moments.add(carry, value, start == 0)
        sums.append(each_block(seg, go, Moments.start(ch), ticks("conv1")))
    stats2 = norm_stats(segs, sums, groups)

    hook("wqkv")
    hook("wproj")
    a2, kv, qkv_t, datt_t = r.a2, r.dqkv, r.qkv_t, r.datt_t
    w_qkv, w_proj = r.wqkv, r.wproj
    for seg, (centre, inverse) in zip(segs, stats2):
        scale, shift = inverse * gain(2), shift_row(6)
        def go(start, carry, seg=seg, centre=centre, scale=scale, shift=shift):
            at = rows_at(seg.row + start)
            normed = ((res[at, :] - centre) * scale + shift).astype(BF)
            a2[at, :] = normed
            lanes = pl.ds(pl.multiple_of(seg.row + start, BLK) if not isinstance(start, int) else seg.row + start, BLK)
            for part in range(3):
                value = mm(normed, w_qkv[:, part * ch : (part + 1) * ch])
                if part != 1:
                    value = value + shift_row(7 if part == 0 else 8)
                low = value.astype(BF)
                if part:
                    kv[at, part * ch : (part + 1) * ch] = low
                else:
                    low = low * (1.0 / math.sqrt(ch // HEADS))
                qkv_t[part * ch : (part + 1) * ch, lanes] = low.T
            datt_t[:, lanes] = mm(w_proj[...], g[at, :], 1, 1).astype(BF)
            return carry
        each_block(seg, go, 0)

    dkv = r.dkv
    attention(segs, kv, qkv_t, datt_t, dkv)

    hook("att")
    dqkv = r.dqkv
    r.grad_proj(mm(qkv_t[0:ch, :], g[...]))
    hook("grad_proj")
    zero = jnp.zeros((8, ch), F32)
    sums2 = []
    q_sum, v_sum, g_sum = zero, zero, zero
    for seg, (centre, inverse) in zip(segs, stats2):
        def go(start, carry, seg=seg, centre=centre, inverse=inverse):
            s0, s1, q_sum, v_sum, g_sum = carry
            at = rows_at(seg.row + start)
            lanes = pl.ds(pl.multiple_of(seg.row + start, BLK) if not isinstance(start, int) else seg.row + start, BLK)
            g_sum = g_sum + fold(g[at, :].astype(F32))
            dq = datt_t[:, lanes].T
            dqkv[at, 0:ch] = dq
            dqkv[at, ch : 3 * ch] = dkv[at, :].astype(BF)
            q_sum = q_sum + fold(dq.astype(F32))
            v_sum = v_sum + fold(dkv[at, ch : 2 * ch])
            da2 = mm(dqkv[at, :], w_qkv[...], 1, 1)
            wide[at, :] = da2
            normal = (res[at, :] - centre) * inverse
            return (s0 + fold(da2), s1 + fold(da2 * normal), q_sum, v_sum, g_sum)
        s0, s1, q_sum, v_sum, g_sum = each_block(seg, go, (zero, zero, q_sum, v_sum, g_sum), ticks("out"))
        sums2.append((total(s0), total(s1)))
    r.grad_qkv(mm(a2[...], dqkv[...], 0, 0))
    hook("grad_qkv")
    terms2 = norm_back_terms(segs, sums2, stats2, [gain(2)] * len(segs), groups)
    y1_sum = zero
    for seg, (centre, inverse), (factor, const, slope) in zip(segs, stats2, terms2):
        def go(start, carry, seg=seg, centre=centre, factor=factor, const=const, slope=slope):
            at = rows_at(seg.row + start)
            d_res = g[at, :].astype(F32) + wide[at, :] * factor - const - (res[at, :] - centre) * slope
            dkv[at, 0:ch] = d_res
            store_triple(triple, seg, start, d_res, True)
            return carry + fold(d_res)
        y1_sum = each_block(seg, go, y1_sum, ticks("dr"))
    gain2 = sums2[0][1] + sums2[1][1]
    shift6 = sums2[0][0] + sums2[1][0]

    hook("dr")

    conv_weight_grad(kept1, triple, segs, r.grad1, (0, ch), ticks(("grad1", 0)))
    hook("grad1")
    cross_weight(r.w1, r.crossed)
    sums1 = []
    for seg, (stretch, centre, inverse, scale, shift) in zip(segs, consts1):
        def go(start, carry, seg=seg, centre=centre, inverse=inverse, scale=scale, shift=shift):
            s0, s1 = carry
            at = rows_at(seg.row + start)
            da1 = conv_back_block(triple, r.crossed, seg, start)
            off = y0[at, :] - centre
            z = off * scale + shift
            sig = sigmoid(z)
            dz = da1 * (sig * (1.0 + z * (1.0 - sig)))
            wide[at, :] = dz
            return (s0 + fold(dz), s1 + fold(dz * (off * inverse)))
        s0, s1 = each_block(seg, go, (zero, zero), ticks("back1"))
        sums1.append((total(s0), total(s1)))
    hook("back1")
    stats = [(centre, inverse) for _, centre, inverse, _, _ in consts1]
    terms1 = norm_back_terms(segs, sums1, stats, scales1, groups)
    y0_sum = zero
    for seg, (centre, inverse), (factor, const, slope) in zip(segs, stats, terms1):
        def go(start, carry, seg=seg, centre=centre, factor=factor, const=const, slope=slope):
            at = rows_at(seg.row + start)
            dy0 = wide[at, :] * factor - const - (y0[at, :] - centre) * slope
            store_triple(triple, seg, start, dy0, True)
            return carry + fold(dy0)
        y0_sum = each_block(seg, go, y0_sum, ticks("dy0"))
    dmod, gain1, shift4 = [], 0.0, 0.0
    for (s0, s1), (stretch, *_) in zip(sums1, consts1):
        dmod.append(jnp.concatenate([gain(1) * s1 + shift_row(4) * s0, s0], axis=1))
        gain1 = gain1 + stretch * s1
        shift4 = shift4 + stretch * s0
    dmod = [d.astype(BF).astype(F32) for d in dmod]
    dmod_sum = dmod[0] + dmod[1]
    r.grad_affine(dmod)

    hook("dy0")

    for n, columns in enumerate(r.columns):
        conv_weight_grad(kept0, triple, segs, r.grad0, columns, ticks(("grad0", n)))
        hook(("grad0", n))
    cross_weight(r.w0, r.crossed)
    sums0 = []
    for seg, (centre, inverse) in zip(segs, stats0):
        scale, shift = inverse * gain(0), shift_row(0)
        def go(start, carry, seg=seg, centre=centre, inverse=inverse, scale=scale, shift=shift):
            s0, s1 = carry
            at = rows_at(seg.row + start)
            da0 = conv_back_block(triple, r.crossed, seg, start)
            off = x[at, :].astype(F32) - centre
            z = off * scale + shift
            sig = sigmoid(z)
            dz = da0 * (sig * (1.0 + z * (1.0 - sig)))
            wide[at, :] = dz
            return (s0 + fold(dz), s1 + fold(dz * (off * inverse)))
        s0, s1 = each_block(seg, go, (zero, zero), ticks("back0"))
        sums0.append((total(s0), total(s1)))
    hook("back0")
    terms0 = norm_back_terms(segs, sums0, stats0, [gain(0)] * len(segs), groups)
    r.rows[...] = jnp.concatenate(
        [
            sums0[0][1] + sums0[1][1],
            gain1,
            gain2,
            sums0[0][0] + sums0[1][0],
            total(y0_sum),
            dmod_sum[:, :ch],
            dmod_sum[:, ch:],
            shift4,
            total(y1_sum),
            shift6,
            total(q_sum),
            total(v_sum),
            total(g_sum),
            jnp.zeros((3, ch), F32),
        ],
        axis=0,
    )
    hook("rows")
    for seg in segs:
        live = r.live(seg.index)
        def go(start, carry, seg=seg, live=live):
            at = rows_at(seg.row + start)
            lanes = pl.ds(pl.multiple_of(seg.row + start, BLK) if not isinstance(start, int) else seg.row + start, BLK)
            made = mm(qkv_t[0:ch, lanes], w_proj[...], 0, 0) + shift_row(9) + res[at, :]
            out[at, :] = jnp.where(live, made, 0.0).astype(BF)
            return carry
        each_block(seg, go, 0, ticks("late"))
    hook("late")
    for seg, (centre, inverse), (factor, const, slope) in zip(segs, stats0, terms0):
        def go(start, carry, seg=seg, centre=centre, factor=factor, const=const, slope=slope):
            at = rows_at(seg.row + start)
            off = x[at, :].astype(F32) - centre
            grad[at, :] = (dkv[at, 0:ch] + wide[at, :] * factor - const - off * slope).astype(BF)
            return carry
        each_block(seg, go, 0, ticks("grad"))


def block_scratch(sides, ch):
    _, rows, pads = make_segs(sides)
    return dict(
        triple=pltpu.VMEM((pads, 3 * ch), BF),
        kept0=pltpu.VMEM((pads, ch), BF),
        kept1=pltpu.VMEM((pads, ch), BF),
        y0=pltpu.VMEM((rows, ch), F32),
        res=pltpu.VMEM((rows, ch), F32),
        wide=pltpu.VMEM((rows, ch), F32),
        groups=pltpu.VMEM((ch, ch), BF),
        a2=pltpu.VMEM((rows, ch), BF),
        qkv_t=pltpu.VMEM((3 * ch, rows), BF),
        datt_t=pltpu.VMEM((ch, rows), BF),
        dkv=pltpu.VMEM((rows, 2 * ch), F32),
        dqkv=pltpu.VMEM((rows, 3 * ch), BF),
        crossed=pltpu.VMEM((3 * ch, 3 * ch), BF),
    )


MESH = pl.DeviceIdType.MESH
VMEM_LIMIT = 63 * 2**20
FLIPS = ("s", "x", "y", "d", "xs", "ys", "ds")
OTHER = {"x": "y", "y": "x"}
SMALL = ("p", "m", "n", "q")
WEIGHTS = ("w0", "w1", "wqkv", "wproj")


SCHEDULE = {
    "grad_qkv": ((0, 0), (1, 0)),
    ("grad1", 0, 1): ((0, 1), (1, 1)),
    "grad1": ((2, 0), (3, 0), (4, 0), (5, 0)),
    ("back1", 0, 2): ((0, 2), (1, 2)),
    ("back1", 0, 3): ((2, 1), (3, 1)),
    ("dy0", 0, 0): ((0, 3), (1, 3), (0, 4), (5, 1), (4, 1)),
    ("grad0", 0, 1): ((2, 2), (3, 2)),
    ("grad0", 0): ((0, 5), (6, 0), (7, 0), (8, 0), (9, 0)),
    ("grad0", 1, 1): ((4, 2), (5, 2)),
    ("grad0", 1): ((10, 0), (11, 0)),
    ("back0", 0, 0): ((6, 1),),
    ("back0", 0, 1): ((2, 3), (1, 4), (3, 3), (2, 4), (7, 1)),
    ("back0", 0, 2): ((4, 3), (3, 4), (5, 3), (4, 4), (8, 1), (9, 1)),
    ("back0", 0, 3): ((0, 6),),
    ("back0", 1, 0): ((6, 2), (10, 1), (1, 5)),
    "back0": ((7, 2), (11, 1)),
    ("late", 0, 0): ((2, 5), (8, 2)),
    ("late", 0, 2): ((9, 2),),
    ("late", 0, 3): ((3, 5),),
    ("late", 1, 0): ((1, 6), (6, 3), (5, 4)),
    ("grad", 0, 0): ((10, 2),),
    ("grad", 0, 1): ((4, 5),),
    ("grad", 0, 2): ((7, 3), (6, 4)),
    ("grad", 0, 3): ((2, 6),),
    ("grad", 1, 0): ((11, 2),),
}
TAIL = ((3, 6), (5, 5), (11, 4), (9, 3), (8, 4), (8, 3), (7, 4), (1, 7), (0, 7), (6, 5), (10, 3), (4, 6), (9, 4), (11, 5), (11, 3), (10, 4), (2, 7), (5, 6), (8, 5), (6, 6), (11, 6), (7, 5), (3, 7), (9, 5), (8, 6), (4, 7), (10, 5), (7, 6), (5, 7), (9, 6), (6, 7), (11, 7), (10, 6), (8, 7), (7, 7), (9, 7), (10, 7))


class Net:
    def __init__(self, names, send, recv):
        self.at = {name: i for i, name in enumerate(names)}
        self.send, self.recv, self.sent = send, recv, []

    def copy(self, name, src, dst, peer):
        i = self.at[name]
        return pltpu.make_async_remote_copy(
            src_ref=src,
            dst_ref=dst,
            send_sem=self.send.at[i],
            recv_sem=self.recv.at[i],
            device_id=peer,
            device_id_type=MESH,
        )

    def push(self, name, make):
        self.copy(name, *make()).start()
        self.sent.append((name, make))

    def take(self, name, dst, peer):
        self.copy(name, dst, dst, peer).wait_recv()

    def drain(self):
        for name, make in self.sent:
            self.copy(name, *make()).wait_send()
        self.sent = []


def spans(rows, pieces):
    tiles = rows // 16
    cuts = [16 * (tiles * i // pieces) for i in range(pieces)] + [rows]
    return [(a, b - a) for a, b in zip(cuts, cuts[1:])]


def column_spans(ch):
    return [(0, 2 * ch // 3), (2 * ch // 3, ch)]


def reduce_units(block, ch):
    units = [("both", 0, block["wqkv"], 0, 2 * ch, "x"), ("both", 0, block["wqkv"], 2 * ch, 2 * ch, "y")]
    for (first, count), axis in zip(spans(block["w1"], 4), "xyxy"):
        units.append(("w1", first, count, 0, ch, axis))
    for (low, high), pieces in zip(column_spans(ch), (4, 2)):
        for (first, count), axis in zip(spans(block["w0"], pieces), "xyxy"):
            units.append(("w0", first, count, low, high - low, axis))
    return units


OUT_STEPS = ("x0", "x1", "y0", "y1", "s", "d0", "d1", "zx", "zy", "zd", "sx", "sy", "sd", "ox", "oy", "od")


def transfer_names(in_units):
    names = [(-1 - i, t) for i in range(len(WEIGHTS)) for t in OUT_STEPS]
    names += [(i, t) for i in range(len(in_units)) for t in "abc"]
    names += [(i, t) for i in range(len(in_units)) for t in ("z0", "z1", "z2")]
    return names + [("n", 0), ("n", 1)] + [(what, flip) for what in SMALL for flip in FLIPS]


def packed(rows, height):
    count, columns = rows.shape
    pieces = [rows[i : i + 1, j : j + 128] for i in range(count) for j in range(0, columns, 128)]
    return jnp.concatenate(pieces + [jnp.zeros((height - len(pieces), 128), rows.dtype)], axis=0)


def unpacked(values, count, columns):
    per = columns // 128
    return jnp.concatenate(
        [jnp.concatenate([values[i * per + j : i * per + j + 1, :] for j in range(per)], axis=1) for i in range(count)],
        axis=0,
    )


def fused_kernel(sides, block, r):
    segs, _, _ = make_segs(sides)
    ch = r.triple.shape[1] // 3
    wide_rows = 2 * ch
    in_units = reduce_units(block, ch)
    me, z = lax.axis_index("shard"), lax.axis_index("rep")
    core, px, py = me % 2, (me // 2) % 2, me // 4
    outer = (z == 0) | (z == 3)
    inner = jnp.logical_not(outer)

    def index(flip):
        fx = 1 - px if ("x" in flip or "d" in flip) else px
        fy = 1 - py if ("y" in flip or "d" in flip) else py
        fc = 1 - core if "s" in flip else core
        return (fy * 2 + fx) * 2 + fc

    at = {flip: index(flip) for flip in FLIPS + ("",)}
    peer = {flip: (at[flip], z) for flip in FLIPS}
    z_in, z_out, z_cross = (me, jnp.where(z < 2, 1, 2)), (me, jnp.where(z < 2, 0, 3)), (me, 3 - z)
    side = z % 2
    z_peer = (me, z + 1 - 2 * side)
    net = Net(transfer_names(in_units), r.send, r.recv)

    local = []

    def fetch(src, dst):
        copy = pltpu.make_async_copy(src, dst, r.local.at[len(local)])
        copy.start()
        local.append(copy)
        return copy

    got_x = [fetch(src, r.x.at[s.row : s.row + s.pixels, :]) for src, s in zip((r.big_x, r.small_x), segs)]

    barrier = pltpu.get_barrier_semaphore()
    for flip in FLIPS:
        pl.semaphore_signal(barrier, inc=1, device_id=peer[flip], device_id_type=MESH)

    for target in (z_peer, z_cross):
        pl.semaphore_signal(barrier, inc=1, device_id=target, device_id_type=MESH)

    gathered = [getattr(r, name) for name in WEIGHTS]
    own = (r.own_w0, r.own_w1, r.own_wqkv, r.own_wproj)
    mine = {}

    def part(i, flip, first, count):
        third = own[i].shape[0] // 3
        at_third = {-1: side, 0: 2 * side, 1: 1, 2: 2 - 2 * side, 3: 0}[first]
        start = pl.multiple_of((at[flip] * 3 + at_third) * third, 16)
        return gathered[i].at[pl.ds(start, count * third), :]

    def own_part(i, first):
        third = own[i].shape[0] // 3
        return own[i].at[pl.ds(pl.multiple_of((2 * side if first == 0 else 1) * third, 16), third), :]

    def pass_on(i, step, flip, first, count, target):
        place = lambda: part(i, flip, first, count)
        net.push((-1 - i, step), lambda: (place(), place(), target))

    def out_start(i):
        for first in (0, 1):
            for axis in "xy":
                net.push(
                    (-1 - i, axis + str(first)),
                    lambda first=first, axis=axis: (own_part(i, first), part(i, "", first, 1), peer[axis]),
                )
        net.push((-1 - i, "s"), lambda: (own[i], part(i, "", 3, 3), peer["s"]))

    def took(i, step, flip, first, count, source):
        net.take((-1 - i, step), part(i, flip, first, count), source)

    def out_first(i):
        took(i, "x0", "x", 0, 1, peer["x"])
        pass_on(i, "d0", "x", 0, 1, peer["y"])
        pass_on(i, "zx", "x", 0, 1, z_peer)
        took(i, "y0", "y", 0, 1, peer["y"])
        pass_on(i, "zy", "y", 0, 1, z_peer)

    def out_second(i):
        took(i, "y1", "y", 1, 1, peer["y"])
        pass_on(i, "d1", "y", 1, 1, peer["x"])
        pass_on(i, "sy", "y", -1, 2, peer["s"])
        took(i, "x1", "x", 1, 1, peer["x"])
        pass_on(i, "sx", "x", -1, 2, peer["s"])

    def out_third(i):
        took(i, "d0", "d", 0, 1, peer["y"])
        pass_on(i, "zd", "d", 0, 1, z_peer)

    def out_fourth(i):
        took(i, "d1", "d", 1, 1, peer["x"])
        pass_on(i, "sd", "d", -1, 2, peer["s"])
        took(i, "zx", "x", 2, 1, z_peer)
        pass_on(i, "ox", "x", 2, 1, peer["s"])
        took(i, "zy", "y", 2, 1, z_peer)
        pass_on(i, "oy", "y", 2, 1, peer["s"])

    def out_fifth(i):
        took(i, "zd", "d", 2, 1, z_peer)
        pass_on(i, "od", "d", 2, 1, peer["s"])

    def whole_start(i):
        for flip, step in (("x", "x0"), ("y", "y0"), ("d", "d0"), ("s", "s")):
            net.push((-1 - i, step), lambda flip=flip: (own[i], part(i, "", 3, 3), peer[flip]))

    def whole_pass(i, flip):
        took(i, flip + "0", flip, 3, 3, peer[flip])
        pass_on(i, "s" + flip, flip, 3, 3, peer["s"])

    def whole_end(i):
        mine[i].wait()
        for step, flip in (("s", "s"), ("sx", "xs"), ("sy", "ys"), ("sd", "ds")):
            took(i, step, flip, 3, 3, peer["s"])

    def out_end(i):
        mine[i].wait()
        took(i, "s", "s", 3, 3, peer["s"])
        for flip in "xyd":
            took(i, "s" + flip, flip + "s", -1, 2, peer["s"])
            took(i, "o" + flip, flip + "s", 2, 1, peer["s"])

    grads = dict(w0=r.grad_w0, w1=r.grad_w1, both=r.grad_both)
    results = dict(w0=r.out_w0, w1=r.out_w1, both=r.out_both)
    done = []

    def unit_ref(i):
        name, first, count, low, width, _ = in_units[i]
        return grads[name], (slice(first, first + count), slice(low, low + width))

    def in_core(i):
        ref, span = unit_ref(i)
        net.push((i, "a"), lambda i=i, ref=ref, span=span: (ref.at[(1 - core, slice(None), slice(None)) + span], r.ra[i], peer["s"]))

    def away(i):
        axis = in_units[i][5]
        return (slice(None), 1 - px) if axis == "x" else (1 - py, slice(None))

    def near(i):
        axis = in_units[i][5]
        return (slice(None), px) if axis == "x" else (py, slice(None))

    def cross(i):
        return (1 - py, px) if in_units[i][5] == "x" else (py, 1 - px)

    def add_to(ref, where, value):
        ref[where] = ref[where] + value

    def in_first(i):
        ref, span = unit_ref(i)
        axis = in_units[i][5]
        net.take((i, "a"), r.ra[i], peer["s"])
        add_to(ref, (core, slice(None), slice(None)) + span, r.ra[i][...])
        net.push((i, "b"), lambda i=i, ref=ref, span=span, axis=axis: (ref.at[(core,) + away(i) + span], r.rb[i], peer[axis]))

    def in_second(i):
        ref, span = unit_ref(i)
        axis = in_units[i][5]
        net.take((i, "b"), r.rb[i], peer[axis])
        add_to(ref, (core,) + near(i) + span, r.rb[i][...])
        net.push((i, "c"), lambda i=i, ref=ref, span=span, axis=axis: (ref.at[(core,) + cross(i) + span], r.rc[i], peer[OTHER[axis]]))

    z_units = [(r.grad_both, r.out_both, (slice(None), slice(None)))]
    z_units += [unit_ref(i)[:1] + (results[in_units[i][0]],) + unit_ref(i)[1:] for i in range(2, len(in_units))]

    def z_out_of(i):
        if i >= len(z_units):
            return r.own_rows, r.rzr
        ref, _, span = z_units[i]
        return ref.at[(core, py, px) + span], r.rz[i]

    def in_third(i):
        ref, span = unit_ref(i)
        net.take((i, "c"), r.rc[i], peer[OTHER[in_units[i][5]]])
        add_to(ref, (core, py, px) + span, r.rc[i][...])

    def z_first(i):
        if i == len(z_units):
            exchanged("q", r.rows_in)
            r.own_rows[...] = jnp.sum(r.rows_in[...], axis=0)
        src, slots = z_out_of(i)

        @pl.when(outer)
        def _():
            net.copy((i, "z0"), src, slots.at[0], z_in).start()

    def z_second(i):
        src, slots = z_out_of(i)

        @pl.when(inner)
        def _():
            net.take((i, "z0"), slots.at[0], z_out)
            src[...] = src[...] + slots[0]
            net.copy((i, "z1"), src, slots.at[1], z_cross).start()

    def z_third(i):
        src, slots = z_out_of(i)

        @pl.when(inner)
        def _():
            net.take((i, "z1"), slots.at[1], z_cross)
            slots[0] = src[...] + slots[1]
            net.copy((i, "z2"), slots.at[0], slots.at[0], z_out).start()

    def z_end(i):
        src, slots = z_out_of(i)

        @pl.when(outer)
        def _():
            net.take((i, "z2"), slots.at[0], z_in)

        if i >= len(z_units):
            target = r.out_rows
        else:
            target = z_units[i][1].at[z_units[i][2]]
        done.append(fetch(slots.at[0], target))

    def z_drain(chosen):
        for i in chosen:
            src, slots = z_out_of(i)

            @pl.when(outer)
            def _():
                net.copy((i, "z0"), src, slots.at[0], z_in).wait_send()

            @pl.when(inner)
            def _():
                net.copy((i, "z1"), src, slots.at[1], z_cross).wait_send()
                net.copy((i, "z2"), slots.at[0], slots.at[0], z_out).wait_send()

    STEPS = (in_core, in_first, in_second, in_third, z_first, z_second, z_third, z_end)

    def run(chosen):
        for i, step in chosen:
            STEPS[step](i)

    def keep(ref, rows_per):
        def store(row, col, value):
            height, width = value.shape
            start = row
            while start < row + height:
                owner = start // rows_per
                stop = min(row + height, (owner + 1) * rows_per)
                ref[owner % 2, owner // 4, (owner // 2) % 2, start - owner * rows_per : stop - owner * rows_per, col : col + width] = value[
                    start - row : stop - row, :
                ].astype(BF)
                start = stop

        return store

    r.grad = r.a2
    r.columns = column_spans(ch)
    r.live = lambda i: r.loads[0, i] > 0
    r.grad0, r.grad1 = keep(r.grad_w0, block["w0"]), keep(r.grad_w1, block["w1"])
    keep_both = keep(r.grad_both, block["wqkv"])
    r.grad_qkv = lambda value: keep_both(0, 0, value)
    r.grad_proj = lambda value: keep_both(0, 3 * ch, value)

    def exchange(what, src, slots):
        each = len(src.shape) == len(slots.shape)
        for flip in FLIPS:
            net.push(
                (what, flip),
                lambda flip=flip: (src.at[at[flip]] if each else src, slots.at[me], peer[flip]),
            )

    def exchanged(what, slots):
        for flip in FLIPS:
            net.take((what, flip), slots.at[at[flip]], peer[flip])

    def hook(name):
        if name == "shifts":
            copied_message.wait()
            exchanged("p", r.messages)
            own_width = 128
            per = ch // 8
            lane = lax.broadcasted_iota(jnp.int32, (8 * own_width, ch), 1)
            sub = lax.broadcasted_iota(jnp.int32, (8 * own_width, ch), 0)
            place = jnp.where(sub % own_width < per, (sub // own_width) * per + sub % own_width, -1)
            spread = jnp.where(lane == place, 1.0, 0.0).astype(BF)
            side_by_side = jnp.concatenate([r.messages[o, 0:16, :] for o in range(8)], axis=1)
            r.params[...] = mm(side_by_side, spread)
            everyone = r.messages[:, 16:32, :].astype(F32).reshape(16, 8, 128)
            chosen = lax.broadcasted_iota(jnp.int32, (16, 8, 128), 1) == me
            r.embeds[...] = jnp.sum(jnp.where(chosen, everyone, 0.0), axis=1).astype(BF)
            copied_affine.wait()
            partial = mm(r.embeds[...], r.waff[...])
            for o in range(8):
                r.mod_out[o] = packed(partial[2 * o : 2 * o + 2, :], 16)
            exchange("m", r.mod_out, r.mod_in)
            r.mod_in[pl.ds(me, 1)] = r.mod_out[pl.ds(me, 1)]
        if name == "w0":
            out_first(0)
            out_second(0)
            out_start(1)
            out_third(0)
            out_fourth(0)
            out_fifth(0)
            out_first(1)
            out_end(0)
        if name == "affine":
            exchanged("m", r.mod_in)
            r.mod[...] = unpacked(jnp.sum(r.mod_in[...], axis=0), 2, wide_rows)
        if name == "w1":
            out_fifth(1)
            out_end(1)
        if name == "wqkv":
            net.drain()
            whole_end(2)
            whole_end(3)
            for copy in got_g:
                copy.wait()
            for seg in segs:
                rows = slice(seg.row, seg.row + seg.pixels)
                r.g[rows, :] = jnp.where(r.live(seg.index), r.g[rows, :], 0).astype(BF)
        if name == ("grad0", 0):
            exchanged("n", r.planes.at[z, 0:8])
            net.push(("n", 0), lambda: (r.planes.at[z], r.planes.at[z], z_peer))
        if name == ("grad0", 1):
            pair = z - side
            net.take(("n", 0), r.planes.at[z + 1 - 2 * side], z_peer)
            net.push(("n", 1), lambda: (r.planes.at[pl.ds(pair, 2)], r.planes.at[pl.ds(pair, 2)], z_cross))
        if name == "back0":
            net.take(("n", 1), r.planes.at[pl.ds(2 - (z - side), 2)], z_cross)
            values = r.planes[...].astype(F32)
            terms = [unpacked(values[p, o], 2, wide_rows) for p in range(4) for o in range(8)]
            embeds = [values[p, 8] for p in range(4)]
            grad = mm(jnp.concatenate(embeds, axis=0).astype(BF), jnp.concatenate(terms, axis=0).astype(BF), 0, 0)
            r.own_affine[...] = grad[0 : block["waff"], :]
            done.append(fetch(r.own_affine, r.out_affine))
        if name == "rows":
            per = ch // 8
            lane = lax.broadcasted_iota(jnp.int32, (ch, 8 * 128), 1)
            sub = lax.broadcasted_iota(jnp.int32, (ch, 8 * 128), 0)
            spread = jnp.where((sub // per == lane // 128) & (sub % per == lane % 128), 1.0, 0.0).astype(BF)
            cut = mm(jnp.concatenate(three_parts(r.rows[...]), axis=0).astype(BF), spread)
            cut = cut[0:16] + cut[16:32] + cut[32:48]
            for o in range(8):
                r.rows_out[o] = cut[:, 128 * o : 128 * (o + 1)]
            exchange("q", r.rows_out, r.rows_in)
            r.rows_in[pl.ds(me, 1)] = r.rows_out[pl.ds(me, 1)]
        if name == "late":
            for seg, out in zip(segs, (r.big_out, r.small_out)):
                done.append(fetch(r.out.at[seg.row : seg.row + seg.pixels, :], out))
        run(SCHEDULE.get(name, ()))

    def ticks(name):
        if name == "conv0":
            return {
                (0, 1): lambda: out_second(1),
                (0, 2): lambda: (whole_start(2), whole_start(3)),
                (1, 0): lambda: out_third(1),
            }
        if name == "a1":
            return {(0, 3): lambda: out_fourth(1)}
        if name == "conv1":
            return {
                (0, 1): lambda: [whole_pass(i, flip) for i in (2, 3) for flip in "xy"],
                (0, 3): lambda: [whole_pass(i, "d") for i in (2, 3)],
            }
        at_rows = type(name) is str
        due = {
            (key[1:] if at_rows else key[2]): chosen
            for key, chosen in SCHEDULE.items()
            if type(key) is tuple and len(key) == 3 and (key[0] == name if at_rows else key[:2] == name)
        }
        return {where: lambda chosen=chosen: run(chosen) for where, chosen in due.items()}

    def grad_affine(rows):
        r.dmod[...] = packed(jnp.concatenate(rows, axis=0), 16).astype(BF)
        exchange("n", r.dmod, r.planes.at[z, 0:8])
        r.planes[z, me] = r.dmod[...]
        r.planes[z, 8] = r.embeds[...]

    r.grad_affine = grad_affine
    pl.semaphore_wait(barrier, len(FLIPS) + 2)
    exchange("p", r.message, r.messages)
    out_start(0)
    r.waff[...] = jnp.zeros_like(r.waff)
    copied_affine = fetch(r.own_waff, r.waff.at[0 : block["waff"], :])
    copied_message = fetch(r.message, r.messages.at[me])
    got_g = [fetch(src, r.g.at[s.row : s.row + s.pixels, :]) for src, s in zip((r.big_g, r.small_g), segs)]
    for i in range(len(WEIGHTS)):
        mine[i] = fetch(own[i], part(i, "", 3, 3))
    for copy in got_x:
        copy.wait()
    block_body(sides, r, hook, ticks)

    for seg, out in zip(segs, (r.big_grad, r.small_grad)):
        done.append(fetch(r.grad.at[seg.row : seg.row + seg.pixels, :], out))
    run(TAIL[:-8])
    net.drain()
    z_drain(range(5))
    run(TAIL[-8:])
    z_drain(range(5, len(z_units) + 1))
    for copy in done:
        copy.wait()


def embed_rows(class_table, sigma_table, labels, sigmas):
    summed = class_table[labels].astype(F32) + sigma_table[sigmas].astype(F32)
    return jax.nn.silu(summed).astype(BF)


def named(names, refs):
    return dict(zip(names, refs))


def fused_call(sides, ch, arrays):
    block = dict(
        w0=arrays["own_w0"].shape[0],
        w1=arrays["own_w1"].shape[0],
        waff=arrays["own_waff"].shape[0],
        wqkv=arrays["own_wqkv"].shape[0],
        wproj=arrays["own_wproj"].shape[0],
    )
    segs, rows, _ = make_segs(sides)
    in_units = reduce_units(block, ch)
    width = dict(w0=ch, w1=ch, wqkv=3 * ch, wproj=ch)
    buffer = lambda *shape: pltpu.VMEM(shape, BF)
    wide_buffer = lambda *shape: pltpu.VMEM(shape, F32)
    whole = {name: buffer(8 * block[name], width[name]) for name in WEIGHTS}
    copies = len(transfer_names(in_units))
    scratch = dict(
        block_scratch(sides, ch),
        **whole,
        grad_w0=buffer(2, 2, 2, block["w0"], ch),
        grad_w1=buffer(2, 2, 2, block["w1"], ch),
        grad_both=buffer(2, 2, 2, block["wqkv"], 4 * ch),
        x=buffer(rows, ch),
        g=buffer(rows, ch),
        out=buffer(rows, ch),
        params=wide_buffer(16, ch),
        messages=buffer(8, 32, 128),
        embeds=buffer(16, 128),
        waff=buffer(128, 2 * ch),
        mod_out=wide_buffer(8, 16, 128),
        mod_in=wide_buffer(8, 16, 128),
        mod=wide_buffer(2, 2 * ch),
        dmod=buffer(16, 128),
        planes=buffer(4, 9, 16, 128),
        own_affine=wide_buffer(block["waff"], 2 * ch),
        rows=wide_buffer(16, ch),
        rows_out=wide_buffer(8, 16, 128),
        rows_in=wide_buffer(8, 16, 128),
        own_rows=wide_buffer(16, 128),
        rzr=wide_buffer(2, 16, 128),
        send=pltpu.SemaphoreType.DMA((copies,)),
        recv=pltpu.SemaphoreType.DMA((copies,)),
        local=pltpu.SemaphoreType.DMA((48,)),
    )
    slots = [
        [buffer(2, 2, n, w) for _, _, n, _, w, _ in in_units],
        [buffer(2, n, w) for _, _, n, _, w, _ in in_units],
        [buffer(n, w) for _, _, n, _, w, _ in in_units],
        [buffer(2, block["wqkv"], 4 * ch)] + [buffer(2, n, w) for _, _, n, _, w, _ in in_units[2:]],
    ]
    big, small = segs[0].pixels, segs[1].pixels
    outs = dict(
        big_out=((big, ch), BF),
        small_out=((small, ch), BF),
        big_grad=((big, ch), BF),
        small_grad=((small, ch), BF),
        out_rows=((16, 128), F32),
        out_affine=((block["waff"], 2 * ch), F32),
        out_w0=((block["w0"], ch), BF),
        out_w1=((block["w1"], ch), BF),
        out_both=((block["wqkv"], 4 * ch), BF),
    )
    names = list(arrays) + list(outs) + list(scratch)

    def kernel(*refs):
        r = types.SimpleNamespace(**dict(zip(names, refs)))
        rest = list(refs[len(names) :])
        n = len(in_units)
        r.ra, r.rb, r.rc, r.rz = rest[:n], rest[n : 2 * n], rest[2 * n : 3 * n], rest[3 * n :]
        fused_kernel(sides, block, r)

    results = pl.pallas_call(
        kernel,
        out_shape=[jax.ShapeDtypeStruct(*shape) for shape in outs.values()],
        in_specs=[pl.BlockSpec(memory_space=pltpu.SMEM)] + [pl.BlockSpec(memory_space=pl.ANY)] * (len(arrays) - 1),
        out_specs=[pl.BlockSpec(memory_space=pl.ANY)] * len(outs),
        scratch_shapes=list(scratch.values()) + sum(slots, []),
        compiler_params=pltpu.CompilerParams(
            collective_id=0, has_side_effects=True, vmem_limit_bytes=VMEM_LIMIT
        ),
    )(*arrays.values())
    return results


def finish_call(results, per):
    images, both = results[:4], results[8]
    ch = both.shape[1] // 4
    outs = [jax.ShapeDtypeStruct(image.shape, image.dtype) for image in images]
    shapes = [(3, per), (10, per)] + [weight.shape for weight in results[5:8]]
    shapes += [(both.shape[0], 3 * ch), (both.shape[0], ch)]
    outs += [jax.ShapeDtypeStruct(shape, F32) for shape in shapes]
    total_in, total_out = len(results), len(outs)

    def kernel(*refs):
        sources, targets = refs[:total_in], refs[total_in : total_in + total_out]
        rest = refs[total_in + total_out :]
        held, made, sems = rest[:total_in], rest[total_in:-1], rest[-1]
        inward = [pltpu.make_async_copy(s, h, sems.at[i]) for i, (s, h) in enumerate(zip(sources, held))]
        for copy in inward:
            copy.start()
        outward = []

        def send(source, target):
            copy = pltpu.make_async_copy(source, target, sems.at[total_in + len(outward)])
            copy.start()
            outward.append(copy)

        for i in (8, 5, 6, 7):
            inward[i].wait()
            if i == 5:
                send(held[i], targets[i + 1])
            elif i < 8:
                made[i - 3][...] = held[i][...].astype(F32)
                send(made[i - 3], targets[i + 1])
            else:
                made[5][...] = held[i][:, 0 : 3 * ch].astype(F32)
                made[6][...] = held[i][:, 3 * ch :].astype(F32)
                send(made[5], targets[9])
                send(made[6], targets[10])
        for i in range(4):
            inward[i].wait()
            send(held[i], targets[i])
        inward[4].wait()
        made[0][...] = held[4][0:3, 0:per]
        made[1][...] = held[4][3:13, 0:per]
        send(made[0], targets[4])
        send(made[1], targets[5])
        for copy in outward:
            copy.wait()

    any_spec = pl.BlockSpec(memory_space=pl.ANY)
    return pl.pallas_call(
        kernel,
        out_shape=outs,
        in_specs=[any_spec] * total_in,
        out_specs=[any_spec] * total_out,
        scratch_shapes=[pltpu.VMEM(array.shape, array.dtype) for array in results]
        + [pltpu.VMEM(out.shape, out.dtype) for out in outs[4:]]
        + [pltpu.SemaphoreType.DMA((total_in + total_out,))],
        compiler_params=pltpu.CompilerParams(vmem_limit_bytes=VMEM_LIMIT),
    )(*results)


def plain_call(sides, ch, arrays):
    _, rows, _ = make_segs(sides)
    scratch = dict(
        block_scratch(sides, ch), mod=pltpu.VMEM((16, 2 * ch), F32), masked=pltpu.VMEM((rows, ch), BF)
    )
    outs = dict(
        out=((rows, ch), BF),
        grad=((rows, ch), BF),
        terms0=((9 * ch, ch), BF),
        terms1=((9 * ch, ch), BF),
        affine=((2 * ch, 2 * ch), BF),
        terms_qkv=((ch, 3 * ch), BF),
        terms_proj=((ch, ch), BF),
        rows=((16, ch), F32),
    )
    names = list(arrays) + list(outs) + list(scratch)

    def kernel(*refs):
        r = types.SimpleNamespace(**dict(zip(names, refs)))
        segs, _, _ = make_segs(sides)
        given = r.g
        r.live = lambda i: r.loads[0, i] > 0
        r.g = r.masked
        r.columns = [(0, ch)]
        for seg in segs:
            span = slice(seg.row, seg.row + seg.pixels)
            r.masked[span, :] = jnp.where(r.live(seg.index), given[span, :], 0).astype(BF)

        def hook(name):
            if name == "affine":
                r.mod[...] = mm(r.emb[...], r.waff[...])

        def keep(ref):
            def store(row, col, value):
                ref[row : row + value.shape[0], col : col + value.shape[1]] = value.astype(BF)

            return store

        def grad_affine(terms):
            zeros = jnp.zeros((14, 2 * ch), F32)
            r.affine[...] = mm(r.emb[...], jnp.concatenate(terms + [zeros], axis=0).astype(BF), 0, 0).astype(BF)

        r.grad0, r.grad1 = keep(r.terms0), keep(r.terms1)
        r.grad_qkv = lambda value: keep(r.terms_qkv)(0, 0, value)
        r.grad_proj = lambda value: keep(r.terms_proj)(0, 0, value)
        r.grad_affine = grad_affine
        block_body(sides, r, hook)

    return pl.pallas_call(
        kernel,
        out_shape=[jax.ShapeDtypeStruct(*shape) for shape in outs.values()],
        in_specs=[pl.BlockSpec(memory_space=pltpu.SMEM)]
        + [pl.BlockSpec(memory_space=pltpu.VMEM)] * (len(arrays) - 1),
        out_specs=[pl.BlockSpec(memory_space=pltpu.VMEM)] * len(outs),
        scratch_shapes=list(scratch.values()),
        compiler_params=pltpu.CompilerParams(vmem_limit_bytes=VMEM_LIMIT),
    )(*arrays.values())


def on_device(
    fused,
    big_images,
    small_images,
    big_labels,
    small_labels,
    big_sigmas,
    small_sigmas,
    loads,
    class_table,
    sigma_table,
    norm_gains,
    biases,
    w_conv0,
    w_conv1,
    w_affine,
    w_qkv,
    w_proj,
    big_cotangent,
    small_cotangent,
):
    sides = (big_images.shape[1], small_images.shape[1])
    ch = big_images.shape[-1]
    flat = lambda array: array.reshape(-1, ch)
    big_embed = embed_rows(class_table, sigma_table, big_labels, big_sigmas)
    small_embed = embed_rows(class_table, sigma_table, small_labels, small_sigmas)
    emb = jnp.concatenate([big_embed, small_embed], axis=0)
    own_rows = jnp.concatenate([norm_gains, biases], axis=0)
    shapes = [big_images.shape, small_images.shape] * 2
    if fused:
        per = own_rows.shape[1]
        slices = emb.reshape(16, -1)
        message = jnp.concatenate(
            [
                jnp.pad(own_rows, ((0, 3), (0, 128 - per))),
                jnp.pad(slices, ((0, 0), (0, 128 - slices.shape[1]))),
            ],
            axis=0,
        )
        made = fused_call(
            sides,
            ch,
            dict(
                loads=loads,
                big_x=flat(big_images),
                small_x=flat(small_images),
                big_g=flat(big_cotangent),
                small_g=flat(small_cotangent),
                message=message,
                own_w0=w_conv0,
                own_w1=w_conv1,
                own_waff=w_affine,
                own_wqkv=w_qkv,
                own_wproj=w_proj,
            ),
        )
        made = finish_call(made, per)
        images, gains, shifts = made[:4], made[4], made[5]
        affine, first, second, qkv, proj = made[6:]
        weights = [first, second, affine, qkv, proj]
    else:
        gather = lambda array, axis=0: lax.all_gather(array, "shard", axis=axis, tiled=True)
        out, grad, terms0, terms1, affine, terms_qkv, terms_proj, rows = plain_call(
            sides,
            ch,
            dict(
                loads=loads,
                x=jnp.concatenate([flat(big_images), flat(small_images)], axis=0),
                g=jnp.concatenate([flat(big_cotangent), flat(small_cotangent)], axis=0),
                emb=jnp.pad(emb, ((0, 14), (0, 0))),
                params=jnp.pad(gather(own_rows, 1).astype(F32), ((0, 3), (0, 0))),
                w0=gather(w_conv0),
                w1=gather(w_conv1),
                waff=gather(w_affine),
                wqkv=gather(w_qkv),
                wproj=gather(w_proj),
            ),
        )

        def owned(terms, axis=0):
            mine = lax.psum_scatter(terms, "shard", scatter_dimension=axis, tiled=True)
            return lax.psum(mine, "rep").astype(F32)

        big = sides[0] * sides[0]
        images = [out[:big], out[big:], grad[:big], grad[big:]]
        sums = owned(rows, 1)
        gains, shifts = sums[:3], sums[3:13]
        weights = [owned(terms) for terms in (terms0, terms1, affine, terms_qkv, terms_proj)]
    return tuple(image.reshape(shape) for image, shape in zip(images, shapes)) + (gains, shifts, *weights)


def solution(mesh):
    fused = mesh.shape["shard"] == 8 and mesh.shape["rep"] == 4
    split = P(("shard", "rep"))
    image = P(("shard", "rep"), None, None, None)
    rows, columns = P("shard", None), P(None, "shard")
    return jax.shard_map(
        lambda *arrays: on_device(fused, *arrays),
        mesh=mesh,
        in_specs=(image, image, split, split, split, split, P(("shard", "rep"), None), P(), P(), columns, columns)
        + (rows,) * 5
        + (image, image),
        out_specs=(image,) * 4 + (columns,) * 2 + (rows,) * 5,
        check_vma=False,
    )
```

```python
import math
import types

import jax
import jax.numpy as jnp
from jax import lax
from jax.experimental import pallas as pl
from jax.experimental.pallas import tpu as pltpu
from jax.sharding import PartitionSpec as P

HEADS = 6
GROUPS = 32
EPSILON = 1e-05
BF = jnp.bfloat16
F32 = jnp.float32
BLK = 256


def mm(left, right, lc=1, rc=0):
    return lax.dot_general(left, right, (((lc,), (rc,)), ((), ())), preferred_element_type=F32)


def fold(values):
    rows, cols = values.shape
    return jnp.sum(values.reshape(rows // 8, 8, cols), axis=0)


def total(folded):
    return jnp.sum(folded, axis=0, keepdims=True)


def sigmoid(z):
    return 0.5 * jnp.tanh(0.5 * z) + 0.5


class Seg:
    def __init__(self, index, row, pad, side):
        self.index, self.row, self.pad, self.side = index, row, pad, side
        self.pixels = side * side


def make_segs(sides):
    segs, row, pad = [], 0, 0
    for index, side in enumerate(sides):
        segs.append(Seg(index, row, pad + side, side))
        row += side * side
        pad += side * side + 2 * side
    return segs, row, pad


def each_block(seg, body, carry, ticks=None):
    count = seg.pixels // BLK
    due = {n: act for (image, n), act in (ticks or {}).items() if image == seg.index}
    if count == 1:
        for act in due.values():
            act()
        return body(0, carry)

    def step(i, c):
        for n, act in due.items():

            @pl.when(i == n)
            def _(act=act):
                act()

        return body(pl.multiple_of(i * BLK, BLK), c)

    return lax.fori_loop(0, count, step, carry)


def rows_at(start, size=BLK):
    return pl.ds(pl.multiple_of(start, 16) if not isinstance(start, int) else start, size)


def three_parts(value):
    high = value.astype(BF).astype(F32)
    mid = (value - high).astype(BF).astype(F32)
    return [high, mid, (value - high - mid).astype(BF).astype(F32)]


def group_mean(rows, group_ref):
    count, channels = len(rows), rows[0].shape[1]
    parts = []
    for row in rows:
        parts += three_parts(row)
    padded = -(-3 * count // 16) * 16
    parts.append(jnp.zeros((padded - 3 * count, channels), F32))
    stacked = jnp.concatenate(parts, axis=0).astype(BF)
    sums = mm(stacked, group_ref[...]) * (GROUPS / channels)
    return [total(sums[3 * i : 3 * i + 3]) for i in range(count)]


def shift_pair(values, side):
    rows = values.shape[0]
    place = lax.broadcasted_iota(jnp.int32, (rows, 1), 0) % side
    before = jnp.where(place == 0, 0.0, pltpu.roll(values, 1, 0))
    after = jnp.where(place == side - 1, 0.0, pltpu.roll(values, rows - 1, 0))
    return before, after


class Moments:
    @staticmethod
    def start(channels):
        return (jnp.zeros((1, channels), F32), jnp.zeros((8, channels), F32), jnp.zeros((8, channels), F32))

    @staticmethod
    def add(carry, values, first):
        about, once, twice = carry
        about = jnp.where(first, values[0:1], about)
        off = values - about
        return (about, once + fold(off), twice + fold(off * off))


def norm_stats(segs, sums, group_ref):
    means, variances = [], []
    for seg, (about, once, twice) in zip(segs, sums):
        off = total(once) * (1.0 / seg.pixels)
        means.append(about + off)
        variances.append(jnp.maximum(total(twice) * (1.0 / seg.pixels) - off * off, 0.0))
    centres = group_mean(means, group_ref)
    spreads = group_mean(
        [v + (m - c) * (m - c) for v, m, c in zip(variances, means, centres)], group_ref
    )
    return [(c, lax.rsqrt(s + EPSILON)) for c, s in zip(centres, spreads)]


def norm_back_terms(segs, sums, stats, scales, group_ref):
    rows = []
    for seg, (s0, s1), scale in zip(segs, sums, scales):
        rows += [scale * s0 * (1.0 / seg.pixels), scale * s1 * (1.0 / seg.pixels)]
    means = group_mean(rows, group_ref)
    result = []
    for i, ((centre, inverse), scale) in enumerate(zip(stats, scales)):
        result.append((inverse * scale, inverse * means[2 * i], inverse * inverse * means[2 * i + 1]))
    return result


def store_triple(ref, seg, start, values, backward):
    channels = values.shape[1]
    before, after = shift_pair(values, seg.side)
    low, high = (after, before) if backward else (before, after)
    at = rows_at(seg.pad + start)
    ref[at, 0:channels] = low.astype(BF)
    ref[at, channels : 2 * channels] = values.astype(BF)
    ref[at, 2 * channels : 3 * channels] = high.astype(BF)


def zero_pads(ref, segs):
    columns = ref.shape[1]
    for seg in segs:
        ref[seg.pad - seg.side : seg.pad, :] = jnp.zeros((seg.side, columns), ref.dtype)
        ref[seg.pad + seg.pixels : seg.pad + seg.pixels + seg.side, :] = jnp.zeros((seg.side, columns), ref.dtype)


def conv_block(triple, weight, seg, start):
    width = triple.shape[1]
    out = None
    for a in range(3):
        term = mm(triple[rows_at(seg.pad + start + (a - 1) * seg.side), :], weight[a * width : (a + 1) * width, :])
        out = term if out is None else out + term
    return out


def conv_back_block(triple, crossed, seg, start):
    width = triple.shape[1]
    third = width // 3
    out = None
    for a in range(3):
        term = mm(
            triple[rows_at(seg.pad + start - (a - 1) * seg.side), :], crossed[a * third : (a + 1) * third, :], 1, 1
        )
        out = term if out is None else out + term
    return out


def cross_weight(source, target):
    channels = source.shape[1]

    def step(a, carry):
        for b in range(3):
            target[pl.ds(pl.multiple_of(a * channels, channels), channels), b * channels : (b + 1) * channels] = source[
                pl.ds(pl.multiple_of((3 * a + b) * channels, channels), channels), :
            ]
        return carry

    lax.fori_loop(0, 3, step, 0)


def conv_weight_grad(kept, triple, segs, store, columns, ticks):
    channels = kept.shape[1]
    first_col, last_col = columns
    width = last_col - first_col
    for a in range(3):
        ticks.get(a, lambda: None)()
        out = None
        for seg in segs:
            first = seg.pad + (a - 1) * seg.side
            span = slice(seg.pad, seg.pad + seg.pixels)
            if width == channels:
                right = triple[span, :]
            else:
                right = jnp.concatenate(
                    [triple[span, b * channels + first_col : b * channels + last_col] for b in range(3)], axis=1
                )
            term = mm(kept[first : first + seg.pixels, :], right, 0, 0)
            out = term if out is None else out + term
        for b in range(3):
            store((3 * a + b) * channels, first_col, out[:, b * width : (b + 1) * width])


class HeadPart:
    def __init__(self, refs, span, chunk, pair_row, half, at):
        self.qkv_t, self.datt_t, self.keyvalue, self.dkv = refs
        self.first, self.pixels, self.chunk = span.start, span.stop - span.start, chunk
        self.channels = self.datt_t.shape[0]
        self.head = self.channels // HEADS
        self.pair, self.half, self.at = pair_row, half, at
        self.row = pair_row + half * self.head
        self.scores, self.probs, self.d_scores = {}, {}, {}
        self.peak, self.sums, self.out, self.dq = None, 0.0, 0.0, 0.0

    def keys(self, n):
        return slice(self.first + n * self.chunk, self.first + (n + 1) * self.chunk)

    def last(self, n):
        return n == self.pixels // self.chunk - 1

    def score(self, n):
        width = 2 * self.head
        rows = pl.ds(self.pair, width)
        if n == 0:
            place = lax.broadcasted_iota(jnp.int32, (width, 1), 0)
            mine = (place < self.head) if self.half == 0 else (place >= self.head)
            self.q = jnp.where(mine, self.qkv_t[rows, self.at], 0).astype(BF)
            self.d_att = jnp.where(mine, self.datt_t[rows, self.at], 0).astype(F32)
        self.scores[n] = mm(self.keyvalue[self.keys(n), pl.ds(self.channels + self.pair, width)], self.q)
        peak = jnp.max(self.scores[n], axis=0, keepdims=True)
        self.peak = peak if self.peak is None else jnp.maximum(self.peak, peak)

    def attend(self, n):
        probs = jnp.exp(self.scores.pop(n) - self.peak)
        self.sums = self.sums + jnp.sum(probs, axis=0, keepdims=True)
        self.probs[n] = probs.astype(BF)
        values_t = self.qkv_t[pl.ds(2 * self.channels + self.row, self.head), self.keys(n)]
        self.out = self.out + mm(values_t, self.probs[n])
        if self.last(n):
            inverse = 1.0 / self.sums
            out = self.out * inverse
            self.d_att = (self.d_att * inverse).astype(BF)
            mine = self.d_att[self.half * self.head : (self.half + 1) * self.head].astype(F32)
            self.dots = jnp.sum(mine * out, axis=0, keepdims=True)
            self.qkv_t[pl.ds(self.row, self.head), self.at] = out.astype(BF)

    def back(self, n):
        width = 2 * self.head
        lanes = pl.ds(self.channels + self.pair, width)
        d_probs = mm(self.keyvalue[self.keys(n), pl.ds(2 * self.channels + self.pair, width)], self.d_att)
        self.d_scores[n] = (self.probs[n].astype(F32) * (d_probs - self.dots)).astype(BF)
        self.dkv[self.keys(n), lanes] += mm(self.probs.pop(n), self.d_att, 1, 1)

    def last_products(self, n):
        d_scores = self.d_scores.pop(n)
        self.dkv[self.keys(n), pl.ds(self.pair, 2 * self.head)] += mm(d_scores, self.q, 1, 1)
        keys_t = self.qkv_t[pl.ds(self.channels + self.row, self.head), self.keys(n)]
        self.dq = self.dq + mm(keys_t, d_scores)
        if self.last(n):
            self.datt_t[pl.ds(self.row, self.head), self.at] = (self.dq * (1.0 / math.sqrt(self.head))).astype(BF)


def attention(segs, keyvalue, qkv_t, datt_t, dkv):
    pair = 2 * datt_t.shape[0] // HEADS
    dkv[...] = jnp.zeros(dkv.shape, F32)

    parts = []
    for row in range(0, datt_t.shape[0], pair):
        for seg in segs:
            span = slice(seg.row, seg.row + seg.pixels)
            block, chunk = min(512, seg.pixels), min(256, seg.pixels)
            for first in range(span.start, span.stop, block):
                for half in range(2):
                    at = slice(first, first + block)
                    parts.append(HeadPart((qkv_t, datt_t, keyvalue, dkv), span, chunk, row, half, at))

    def step(k, what, n):
        if 0 <= k < len(parts) and n < parts[k].pixels // parts[k].chunk:
            getattr(parts[k], what)(n)

    chunks = max(part.pixels // part.chunk for part in parts)
    for k in range(-1, len(parts) + 2):
        for n in range(chunks):
            step(k - 2, "last_products", n)
            step(k - 1, "back", n)
            step(k, "attend", n)
            step(k + 1, "score", n)


def block_body(sides, r, hook=lambda name: None, ticks=lambda name: {}):
    segs, rows_all, pad_all = make_segs(sides)
    ch = r.x.shape[1]
    x, g, out, grad = r.x, r.g, r.out, r.grad
    triple, kept0, kept1 = r.triple, r.kept0, r.kept1
    y0, res, wide = r.y0, r.res, r.wide
    gain = lambda i: r.params[i : i + 1, :]
    shift_row = lambda i: r.params[3 + i : 4 + i, :]
    groups = r.groups
    for ref in (triple, kept0, kept1):
        zero_pads(ref, segs)
    lane = lax.broadcasted_iota(jnp.int32, (ch, ch), 1)
    sub = lax.broadcasted_iota(jnp.int32, (ch, ch), 0)
    width = ch // GROUPS
    diff = sub // width - lane // width
    groups[...] = jnp.where(diff == 0, 1.0, 0.0).astype(BF)

    sums = []
    for seg in segs:
        def go(start, carry, seg=seg):
            return Moments.add(carry, x[rows_at(seg.row + start), :].astype(F32), start == 0)
        sums.append(each_block(seg, go, Moments.start(ch)))
    hook("shifts")
    stats0 = norm_stats(segs, sums, groups)
    for seg, (centre, inverse) in zip(segs, stats0):
        scale, shift = inverse * gain(0), shift_row(0)
        def go(start, carry, seg=seg, centre=centre, scale=scale, shift=shift):
            z = (x[rows_at(seg.row + start), :].astype(F32) - centre) * scale + shift
            a0 = z * sigmoid(z)
            store_triple(triple, seg, start, a0, False)
            kept0[rows_at(seg.pad + start), :] = a0.astype(BF)
            return carry
        each_block(seg, go, 0)

    hook("w0")
    sums = []
    for seg in segs:
        def go(start, carry, seg=seg):
            value = conv_block(triple, r.w0, seg, start) + shift_row(1)
            y0[rows_at(seg.row + start), :] = value
            return Moments.add(carry, value, start == 0)
        sums.append(each_block(seg, go, Moments.start(ch), ticks("conv0")))
    hook("conv0")
    stats1 = norm_stats(segs, sums, groups)
    hook("affine")
    mod = r.mod
    scales1, consts1 = [], []
    for seg, (centre, inverse) in zip(segs, stats1):
        stretch = mod[seg.index : seg.index + 1, :ch] + shift_row(2) + 1.0
        offset = mod[seg.index : seg.index + 1, ch:] + shift_row(3)
        scales1.append(gain(1) * stretch)
        shift = shift_row(4) * stretch + offset
        consts1.append((stretch, centre, inverse, inverse * scales1[-1], shift))
        _, _, _, scale, _ = consts1[-1]
        def go(start, carry, seg=seg, centre=centre, scale=scale, shift=shift):
            z = (y0[rows_at(seg.row + start), :] - centre) * scale + shift
            a1 = z * sigmoid(z)
            store_triple(triple, seg, start, a1, False)
            kept1[rows_at(seg.pad + start), :] = a1.astype(BF)
            return carry
        each_block(seg, go, 0, ticks("a1"))

    hook("w1")
    sums = []
    for seg in segs:
        def go(start, carry, seg=seg):
            at = rows_at(seg.row + start)
            value = conv_block(triple, r.w1, seg, start) + shift_row(5) + x[at, :].astype(F32)
            res[at, :] = value
            return Moments.add(carry, value, start == 0)
        sums.append(each_block(seg, go, Moments.start(ch), ticks("conv1")))
    stats2 = norm_stats(segs, sums, groups)

    hook("wqkv")
    hook("wproj")
    a2, kv, qkv_t, datt_t = r.a2, r.dqkv, r.qkv_t, r.datt_t
    w_qkv, w_proj = r.wqkv, r.wproj
    for seg, (centre, inverse) in zip(segs, stats2):
        scale, shift = inverse * gain(2), shift_row(6)
        def go(start, carry, seg=seg, centre=centre, scale=scale, shift=shift):
            at = rows_at(seg.row + start)
            normed = ((res[at, :] - centre) * scale + shift).astype(BF)
            a2[at, :] = normed
            lanes = pl.ds(pl.multiple_of(seg.row + start, BLK) if not isinstance(start, int) else seg.row + start, BLK)
            for part in range(3):
                value = mm(normed, w_qkv[:, part * ch : (part + 1) * ch])
                if part != 1:
                    value = value + shift_row(7 if part == 0 else 8)
                low = value.astype(BF)
                if part:
                    kv[at, part * ch : (part + 1) * ch] = low
                else:
                    low = low * (1.0 / math.sqrt(ch // HEADS))
                qkv_t[part * ch : (part + 1) * ch, lanes] = low.T
            datt_t[:, lanes] = mm(w_proj[...], g[at, :], 1, 1).astype(BF)
            return carry
        each_block(seg, go, 0)

    dkv = r.dkv
    attention(segs, kv, qkv_t, datt_t, dkv)

    hook("att")
    dqkv = r.dqkv
    r.grad_proj(mm(qkv_t[0:ch, :], g[...]))
    hook("grad_proj")
    zero = jnp.zeros((8, ch), F32)
    sums2 = []
    q_sum, v_sum, g_sum = zero, zero, zero
    for seg, (centre, inverse) in zip(segs, stats2):
        def go(start, carry, seg=seg, centre=centre, inverse=inverse):
            s0, s1, q_sum, v_sum, g_sum = carry
            at = rows_at(seg.row + start)
            lanes = pl.ds(pl.multiple_of(seg.row + start, BLK) if not isinstance(start, int) else seg.row + start, BLK)
            g_sum = g_sum + fold(g[at, :].astype(F32))
            dq = datt_t[:, lanes].T
            dqkv[at, 0:ch] = dq
            dqkv[at, ch : 3 * ch] = dkv[at, :].astype(BF)
            q_sum = q_sum + fold(dq.astype(F32))
            v_sum = v_sum + fold(dkv[at, ch : 2 * ch])
            da2 = mm(dqkv[at, :], w_qkv[...], 1, 1)
            wide[at, :] = da2
            normal = (res[at, :] - centre) * inverse
            return (s0 + fold(da2), s1 + fold(da2 * normal), q_sum, v_sum, g_sum)
        s0, s1, q_sum, v_sum, g_sum = each_block(seg, go, (zero, zero, q_sum, v_sum, g_sum), ticks("out"))
        sums2.append((total(s0), total(s1)))
    r.grad_qkv(mm(a2[...], dqkv[...], 0, 0))
    hook("grad_qkv")
    terms2 = norm_back_terms(segs, sums2, stats2, [gain(2)] * len(segs), groups)
    y1_sum = zero
    for seg, (centre, inverse), (factor, const, slope) in zip(segs, stats2, terms2):
        def go(start, carry, seg=seg, centre=centre, factor=factor, const=const, slope=slope):
            at = rows_at(seg.row + start)
            d_res = g[at, :].astype(F32) + wide[at, :] * factor - const - (res[at, :] - centre) * slope
            dkv[at, 0:ch] = d_res
            store_triple(triple, seg, start, d_res, True)
            return carry + fold(d_res)
        y1_sum = each_block(seg, go, y1_sum, ticks("dr"))
    gain2 = sums2[0][1] + sums2[1][1]
    shift6 = sums2[0][0] + sums2[1][0]

    hook("dr")

    conv_weight_grad(kept1, triple, segs, r.grad1, (0, ch), ticks(("grad1", 0)))
    hook("grad1")
    cross_weight(r.w1, r.crossed)
    sums1 = []
    for seg, (stretch, centre, inverse, scale, shift) in zip(segs, consts1):
        def go(start, carry, seg=seg, centre=centre, inverse=inverse, scale=scale, shift=shift):
            s0, s1 = carry
            at = rows_at(seg.row + start)
            da1 = conv_back_block(triple, r.crossed, seg, start)
            off = y0[at, :] - centre
            z = off * scale + shift
            sig = sigmoid(z)
            dz = da1 * (sig * (1.0 + z * (1.0 - sig)))
            wide[at, :] = dz
            return (s0 + fold(dz), s1 + fold(dz * (off * inverse)))
        s0, s1 = each_block(seg, go, (zero, zero), ticks("back1"))
        sums1.append((total(s0), total(s1)))
    hook("back1")
    stats = [(centre, inverse) for _, centre, inverse, _, _ in consts1]
    terms1 = norm_back_terms(segs, sums1, stats, scales1, groups)
    y0_sum = zero
    for seg, (centre, inverse), (factor, const, slope) in zip(segs, stats, terms1):
        def go(start, carry, seg=seg, centre=centre, factor=factor, const=const, slope=slope):
            at = rows_at(seg.row + start)
            dy0 = wide[at, :] * factor - const - (y0[at, :] - centre) * slope
            store_triple(triple, seg, start, dy0, True)
            return carry + fold(dy0)
        y0_sum = each_block(seg, go, y0_sum, ticks("dy0"))
    dmod, gain1, shift4 = [], 0.0, 0.0
    for (s0, s1), (stretch, *_) in zip(sums1, consts1):
        dmod.append(jnp.concatenate([gain(1) * s1 + shift_row(4) * s0, s0], axis=1))
        gain1 = gain1 + stretch * s1
        shift4 = shift4 + stretch * s0
    dmod = [d.astype(BF).astype(F32) for d in dmod]
    dmod_sum = dmod[0] + dmod[1]
    r.grad_affine(dmod)

    hook("dy0")

    for n, columns in enumerate(r.columns):
        conv_weight_grad(kept0, triple, segs, r.grad0, columns, ticks(("grad0", n)))
        hook(("grad0", n))
    cross_weight(r.w0, r.crossed)
    sums0 = []
    for seg, (centre, inverse) in zip(segs, stats0):
        scale, shift = inverse * gain(0), shift_row(0)
        def go(start, carry, seg=seg, centre=centre, inverse=inverse, scale=scale, shift=shift):
            s0, s1 = carry
            at = rows_at(seg.row + start)
            da0 = conv_back_block(triple, r.crossed, seg, start)
            off = x[at, :].astype(F32) - centre
            z = off * scale + shift
            sig = sigmoid(z)
            dz = da0 * (sig * (1.0 + z * (1.0 - sig)))
            wide[at, :] = dz
            return (s0 + fold(dz), s1 + fold(dz * (off * inverse)))
        s0, s1 = each_block(seg, go, (zero, zero), ticks("back0"))
        sums0.append((total(s0), total(s1)))
    hook("back0")
    terms0 = norm_back_terms(segs, sums0, stats0, [gain(0)] * len(segs), groups)
    r.rows[...] = jnp.concatenate(
        [
            sums0[0][1] + sums0[1][1],
            gain1,
            gain2,
            sums0[0][0] + sums0[1][0],
            total(y0_sum),
            dmod_sum[:, :ch],
            dmod_sum[:, ch:],
            shift4,
            total(y1_sum),
            shift6,
            total(q_sum),
            total(v_sum),
            total(g_sum),
            jnp.zeros((3, ch), F32),
        ],
        axis=0,
    )
    hook("rows")
    for seg in segs:
        live = r.live(seg.index)
        def go(start, carry, seg=seg, live=live):
            at = rows_at(seg.row + start)
            lanes = pl.ds(pl.multiple_of(seg.row + start, BLK) if not isinstance(start, int) else seg.row + start, BLK)
            made = mm(qkv_t[0:ch, lanes], w_proj[...], 0, 0) + shift_row(9) + res[at, :]
            out[at, :] = jnp.where(live, made, 0.0).astype(BF)
            return carry
        each_block(seg, go, 0, ticks("late"))
    hook("late")
    for seg, (centre, inverse), (factor, const, slope) in zip(segs, stats0, terms0):
        def go(start, carry, seg=seg, centre=centre, factor=factor, const=const, slope=slope):
            at = rows_at(seg.row + start)
            off = x[at, :].astype(F32) - centre
            grad[at, :] = (dkv[at, 0:ch] + wide[at, :] * factor - const - off * slope).astype(BF)
            return carry
        each_block(seg, go, 0, ticks("grad"))


def block_scratch(sides, ch):
    _, rows, pads = make_segs(sides)
    return dict(
        triple=pltpu.VMEM((pads, 3 * ch), BF),
        kept0=pltpu.VMEM((pads, ch), BF),
        kept1=pltpu.VMEM((pads, ch), BF),
        y0=pltpu.VMEM((rows, ch), F32),
        res=pltpu.VMEM((rows, ch), F32),
        wide=pltpu.VMEM((rows, ch), F32),
        groups=pltpu.VMEM((ch, ch), BF),
        a2=pltpu.VMEM((rows, ch), BF),
        qkv_t=pltpu.VMEM((3 * ch, rows), BF),
        datt_t=pltpu.VMEM((ch, rows), BF),
        dkv=pltpu.VMEM((rows, 2 * ch), F32),
        dqkv=pltpu.VMEM((rows, 3 * ch), BF),
        crossed=pltpu.VMEM((3 * ch, 3 * ch), BF),
    )


MESH = pl.DeviceIdType.MESH
VMEM_LIMIT = 63 * 2**20
FLIPS = ("s", "x", "y", "d", "xs", "ys", "ds")
OTHER = {"x": "y", "y": "x"}
SMALL = ("p", "m", "n", "q")
WEIGHTS = ("w0", "w1", "wqkv", "wproj")


SCHEDULE = {
    "grad_qkv": ((0, 0), (1, 0)),
    ("grad1", 0, 1): ((0, 1), (1, 1)),
    "grad1": ((2, 0), (3, 0), (4, 0), (5, 0)),
    ("back1", 0, 2): ((0, 2), (1, 2)),
    ("back1", 0, 3): ((2, 1), (3, 1)),
    ("dy0", 0, 0): ((0, 3), (1, 3), (0, 4), (5, 1), (4, 1)),
    ("grad0", 0, 1): ((2, 2), (3, 2)),
    ("grad0", 0): ((0, 5), (6, 0), (7, 0), (8, 0), (9, 0)),
    ("grad0", 1, 1): ((4, 2), (5, 2)),
    ("grad0", 1): ((10, 0), (11, 0)),
    ("back0", 0, 0): ((6, 1),),
    ("back0", 0, 1): ((2, 3), (1, 4), (3, 3), (2, 4), (7, 1)),
    ("back0", 0, 2): ((4, 3), (3, 4), (5, 3), (4, 4), (8, 1), (9, 1)),
    ("back0", 0, 3): ((0, 6),),
    ("back0", 1, 0): ((6, 2), (10, 1), (1, 5)),
    "back0": ((7, 2), (11, 1)),
    ("late", 0, 0): ((2, 5), (8, 2)),
    ("late", 0, 2): ((9, 2),),
    ("late", 0, 3): ((3, 5),),
    ("late", 1, 0): ((1, 6), (6, 3), (5, 4)),
    ("grad", 0, 0): ((10, 2),),
    ("grad", 0, 1): ((4, 5),),
    ("grad", 0, 2): ((7, 3), (6, 4)),
    ("grad", 0, 3): ((2, 6),),
    ("grad", 1, 0): ((11, 2),),
}
TAIL = ((3, 6), (5, 5), (11, 4), (9, 3), (8, 4), (8, 3), (7, 4), (1, 7), (0, 7), (6, 5), (10, 3), (4, 6), (9, 4), (11, 5), (11, 3), (10, 4), (2, 7), (5, 6), (8, 5), (6, 6), (11, 6), (7, 5), (3, 7), (9, 5), (8, 6), (4, 7), (10, 5), (7, 6), (5, 7), (9, 6), (6, 7), (11, 7), (10, 6), (8, 7), (7, 7), (9, 7), (10, 7))


class Net:
    def __init__(self, names, send, recv):
        self.at = {name: i for i, name in enumerate(names)}
        self.send, self.recv, self.sent = send, recv, []

    def copy(self, name, src, dst, peer):
        i = self.at[name]
        return pltpu.make_async_remote_copy(
            src_ref=src,
            dst_ref=dst,
            send_sem=self.send.at[i],
            recv_sem=self.recv.at[i],
            device_id=peer,
            device_id_type=MESH,
        )

    def push(self, name, make):
        self.copy(name, *make()).start()
        self.sent.append((name, make))

    def take(self, name, dst, peer):
        self.copy(name, dst, dst, peer).wait_recv()

    def drain(self):
        for name, make in self.sent:
            self.copy(name, *make()).wait_send()
        self.sent = []


def spans(rows, pieces):
    tiles = rows // 16
    cuts = [16 * (tiles * i // pieces) for i in range(pieces)] + [rows]
    return [(a, b - a) for a, b in zip(cuts, cuts[1:])]


def column_spans(ch):
    return [(0, 2 * ch // 3), (2 * ch // 3, ch)]


def reduce_units(block, ch):
    units = [("both", 0, block["wqkv"], 0, 2 * ch, "x"), ("both", 0, block["wqkv"], 2 * ch, 2 * ch, "y")]
    for (first, count), axis in zip(spans(block["w1"], 4), "xyxy"):
        units.append(("w1", first, count, 0, ch, axis))
    for (low, high), pieces in zip(column_spans(ch), (4, 2)):
        for (first, count), axis in zip(spans(block["w0"], pieces), "xyxy"):
            units.append(("w0", first, count, low, high - low, axis))
    return units


OUT_STEPS = ("x0", "x1", "y0", "y1", "s", "d0", "d1", "zx", "zy", "zd", "sx", "sy", "sd", "ox", "oy", "od")


def transfer_names(in_units):
    names = [(-1 - i, t) for i in range(len(WEIGHTS)) for t in OUT_STEPS]
    names += [(i, t) for i in range(len(in_units)) for t in "abc"]
    names += [(i, t) for i in range(len(in_units)) for t in ("z0", "z1", "z2")]
    return names + [("n", 0), ("n", 1)] + [(what, flip) for what in SMALL for flip in FLIPS]


def packed(rows, height):
    count, columns = rows.shape
    pieces = [rows[i : i + 1, j : j + 128] for i in range(count) for j in range(0, columns, 128)]
    return jnp.concatenate(pieces + [jnp.zeros((height - len(pieces), 128), rows.dtype)], axis=0)


def unpacked(values, count, columns):
    per = columns // 128
    return jnp.concatenate(
        [jnp.concatenate([values[i * per + j : i * per + j + 1, :] for j in range(per)], axis=1) for i in range(count)],
        axis=0,
    )


def fused_kernel(sides, block, r):
    segs, _, _ = make_segs(sides)
    ch = r.triple.shape[1] // 3
    wide_rows = 2 * ch
    in_units = reduce_units(block, ch)
    me, z = lax.axis_index("shard"), lax.axis_index("rep")
    core, px, py = me % 2, (me // 2) % 2, me // 4
    outer = (z == 0) | (z == 3)
    inner = jnp.logical_not(outer)

    def index(flip):
        fx = 1 - px if ("x" in flip or "d" in flip) else px
        fy = 1 - py if ("y" in flip or "d" in flip) else py
        fc = 1 - core if "s" in flip else core
        return (fy * 2 + fx) * 2 + fc

    at = {flip: index(flip) for flip in FLIPS + ("",)}
    peer = {flip: (at[flip], z) for flip in FLIPS}
    z_in, z_out, z_cross = (me, jnp.where(z < 2, 1, 2)), (me, jnp.where(z < 2, 0, 3)), (me, 3 - z)
    side = z % 2
    z_peer = (me, z + 1 - 2 * side)
    net = Net(transfer_names(in_units), r.send, r.recv)

    local = []

    def fetch(src, dst):
        copy = pltpu.make_async_copy(src, dst, r.local.at[len(local)])
        copy.start()
        local.append(copy)
        return copy

    got_x = [fetch(src, r.x.at[s.row : s.row + s.pixels, :]) for src, s in zip((r.big_x, r.small_x), segs)]

    barrier = pltpu.get_barrier_semaphore()
    for flip in FLIPS:
        pl.semaphore_signal(barrier, inc=1, device_id=peer[flip], device_id_type=MESH)

    for target in (z_peer, z_cross):
        pl.semaphore_signal(barrier, inc=1, device_id=target, device_id_type=MESH)

    gathered = [getattr(r, name) for name in WEIGHTS]
    own = (r.own_w0, r.own_w1, r.own_wqkv, r.own_wproj)
    mine = {}

    def part(i, flip, first, count):
        third = own[i].shape[0] // 3
        at_third = {-1: side, 0: 2 * side, 1: 1, 2: 2 - 2 * side, 3: 0}[first]
        start = pl.multiple_of((at[flip] * 3 + at_third) * third, 16)
        return gathered[i].at[pl.ds(start, count * third), :]

    def own_part(i, first):
        third = own[i].shape[0] // 3
        return own[i].at[pl.ds(pl.multiple_of((2 * side if first == 0 else 1) * third, 16), third), :]

    def pass_on(i, step, flip, first, count, target):
        place = lambda: part(i, flip, first, count)
        net.push((-1 - i, step), lambda: (place(), place(), target))

    def out_start(i):
        for first in (0, 1):
            for axis in "xy":
                net.push(
                    (-1 - i, axis + str(first)),
                    lambda first=first, axis=axis: (own_part(i, first), part(i, "", first, 1), peer[axis]),
                )
        net.push((-1 - i, "s"), lambda: (own[i], part(i, "", 3, 3), peer["s"]))

    def took(i, step, flip, first, count, source):
        net.take((-1 - i, step), part(i, flip, first, count), source)

    def out_first(i):
        took(i, "x0", "x", 0, 1, peer["x"])
        pass_on(i, "d0", "x", 0, 1, peer["y"])
        pass_on(i, "zx", "x", 0, 1, z_peer)
        took(i, "y0", "y", 0, 1, peer["y"])
        pass_on(i, "zy", "y", 0, 1, z_peer)

    def out_second(i):
        took(i, "y1", "y", 1, 1, peer["y"])
        pass_on(i, "d1", "y", 1, 1, peer["x"])
        pass_on(i, "sy", "y", -1, 2, peer["s"])
        took(i, "x1", "x", 1, 1, peer["x"])
        pass_on(i, "sx", "x", -1, 2, peer["s"])

    def out_third(i):
        took(i, "d0", "d", 0, 1, peer["y"])
        pass_on(i, "zd", "d", 0, 1, z_peer)

    def out_fourth(i):
        took(i, "d1", "d", 1, 1, peer["x"])
        pass_on(i, "sd", "d", -1, 2, peer["s"])
        took(i, "zx", "x", 2, 1, z_peer)
        pass_on(i, "ox", "x", 2, 1, peer["s"])
        took(i, "zy", "y", 2, 1, z_peer)
        pass_on(i, "oy", "y", 2, 1, peer["s"])

    def out_fifth(i):
        took(i, "zd", "d", 2, 1, z_peer)
        pass_on(i, "od", "d", 2, 1, peer["s"])

    def whole_start(i):
        for flip, step in (("x", "x0"), ("y", "y0"), ("d", "d0"), ("s", "s")):
            net.push((-1 - i, step), lambda flip=flip: (own[i], part(i, "", 3, 3), peer[flip]))

    def whole_pass(i, flip):
        took(i, flip + "0", flip, 3, 3, peer[flip])
        pass_on(i, "s" + flip, flip, 3, 3, peer["s"])

    def whole_end(i):
        mine[i].wait()
        for step, flip in (("s", "s"), ("sx", "xs"), ("sy", "ys"), ("sd", "ds")):
            took(i, step, flip, 3, 3, peer["s"])

    def out_end(i):
        mine[i].wait()
        took(i, "s", "s", 3, 3, peer["s"])
        for flip in "xyd":
            took(i, "s" + flip, flip + "s", -1, 2, peer["s"])
            took(i, "o" + flip, flip + "s", 2, 1, peer["s"])

    grads = dict(w0=r.grad_w0, w1=r.grad_w1, both=r.grad_both)
    results = dict(w0=r.out_w0, w1=r.out_w1, both=r.out_both)
    done = []

    def unit_ref(i):
        name, first, count, low, width, _ = in_units[i]
        return grads[name], (slice(first, first + count), slice(low, low + width))

    def in_core(i):
        ref, span = unit_ref(i)
        net.push((i, "a"), lambda i=i, ref=ref, span=span: (ref.at[(1 - core, slice(None), slice(None)) + span], r.ra[i], peer["s"]))

    def away(i):
        axis = in_units[i][5]
        return (slice(None), 1 - px) if axis == "x" else (1 - py, slice(None))

    def near(i):
        axis = in_units[i][5]
        return (slice(None), px) if axis == "x" else (py, slice(None))

    def cross(i):
        return (1 - py, px) if in_units[i][5] == "x" else (py, 1 - px)

    def add_to(ref, where, value):
        ref[where] = ref[where] + value

    def in_first(i):
        ref, span = unit_ref(i)
        axis = in_units[i][5]
        net.take((i, "a"), r.ra[i], peer["s"])
        add_to(ref, (core, slice(None), slice(None)) + span, r.ra[i][...])
        net.push((i, "b"), lambda i=i, ref=ref, span=span, axis=axis: (ref.at[(core,) + away(i) + span], r.rb[i], peer[axis]))

    def in_second(i):
        ref, span = unit_ref(i)
        axis = in_units[i][5]
        net.take((i, "b"), r.rb[i], peer[axis])
        add_to(ref, (core,) + near(i) + span, r.rb[i][...])
        net.push((i, "c"), lambda i=i, ref=ref, span=span, axis=axis: (ref.at[(core,) + cross(i) + span], r.rc[i], peer[OTHER[axis]]))

    z_units = [(r.grad_both, r.out_both, (slice(None), slice(None)))]
    z_units += [unit_ref(i)[:1] + (results[in_units[i][0]],) + unit_ref(i)[1:] for i in range(2, len(in_units))]

    def z_out_of(i):
        if i >= len(z_units):
            return r.own_rows, r.rzr
        ref, _, span = z_units[i]
        return ref.at[(core, py, px) + span], r.rz[i]

    def in_third(i):
        ref, span = unit_ref(i)
        net.take((i, "c"), r.rc[i], peer[OTHER[in_units[i][5]]])
        add_to(ref, (core, py, px) + span, r.rc[i][...])

    def z_first(i):
        if i == len(z_units):
            exchanged("q", r.rows_in)
            r.own_rows[...] = jnp.sum(r.rows_in[...], axis=0)
        src, slots = z_out_of(i)

        @pl.when(outer)
        def _():
            net.copy((i, "z0"), src, slots.at[0], z_in).start()

    def z_second(i):
        src, slots = z_out_of(i)

        @pl.when(inner)
        def _():
            net.take((i, "z0"), slots.at[0], z_out)
            src[...] = src[...] + slots[0]
            net.copy((i, "z1"), src, slots.at[1], z_cross).start()

    def z_third(i):
        src, slots = z_out_of(i)

        @pl.when(inner)
        def _():
            net.take((i, "z1"), slots.at[1], z_cross)
            slots[0] = src[...] + slots[1]
            net.copy((i, "z2"), slots.at[0], slots.at[0], z_out).start()

    def z_end(i):
        src, slots = z_out_of(i)

        @pl.when(outer)
        def _():
            net.take((i, "z2"), slots.at[0], z_in)

        if i >= len(z_units):
            target = r.out_rows
        else:
            target = z_units[i][1].at[z_units[i][2]]
        done.append(fetch(slots.at[0], target))

    def z_drain(chosen):
        for i in chosen:
            src, slots = z_out_of(i)

            @pl.when(outer)
            def _():
                net.copy((i, "z0"), src, slots.at[0], z_in).wait_send()

            @pl.when(inner)
            def _():
                net.copy((i, "z1"), src, slots.at[1], z_cross).wait_send()
                net.copy((i, "z2"), slots.at[0], slots.at[0], z_out).wait_send()

    STEPS = (in_core, in_first, in_second, in_third, z_first, z_second, z_third, z_end)

    def run(chosen):
        for i, step in chosen:
            STEPS[step](i)

    def keep(ref, rows_per):
        def store(row, col, value):
            height, width = value.shape
            start = row
            while start < row + height:
                owner = start // rows_per
                stop = min(row + height, (owner + 1) * rows_per)
                ref[owner % 2, owner // 4, (owner // 2) % 2, start - owner * rows_per : stop - owner * rows_per, col : col + width] = value[
                    start - row : stop - row, :
                ].astype(BF)
                start = stop

        return store

    r.grad = r.a2
    r.columns = column_spans(ch)
    r.live = lambda i: r.loads[0, i] > 0
    r.grad0, r.grad1 = keep(r.grad_w0, block["w0"]), keep(r.grad_w1, block["w1"])
    keep_both = keep(r.grad_both, block["wqkv"])
    r.grad_qkv = lambda value: keep_both(0, 0, value)
    r.grad_proj = lambda value: keep_both(0, 3 * ch, value)

    def exchange(what, src, slots):
        each = len(src.shape) == len(slots.shape)
        for flip in FLIPS:
            net.push(
                (what, flip),
                lambda flip=flip: (src.at[at[flip]] if each else src, slots.at[me], peer[flip]),
            )

    def exchanged(what, slots):
        for flip in FLIPS:
            net.take((what, flip), slots.at[at[flip]], peer[flip])

    def hook(name):
        if name == "shifts":
            copied_message.wait()
            exchanged("p", r.messages)
            own_width = 128
            per = ch // 8
            lane = lax.broadcasted_iota(jnp.int32, (8 * own_width, ch), 1)
            sub = lax.broadcasted_iota(jnp.int32, (8 * own_width, ch), 0)
            place = jnp.where(sub % own_width < per, (sub // own_width) * per + sub % own_width, -1)
            spread = jnp.where(lane == place, 1.0, 0.0).astype(BF)
            side_by_side = jnp.concatenate([r.messages[o, 0:16, :] for o in range(8)], axis=1)
            r.params[...] = mm(side_by_side, spread)
            everyone = r.messages[:, 16:32, :].astype(F32).reshape(16, 8, 128)
            chosen = lax.broadcasted_iota(jnp.int32, (16, 8, 128), 1) == me
            r.embeds[...] = jnp.sum(jnp.where(chosen, everyone, 0.0), axis=1).astype(BF)
            copied_affine.wait()
            partial = mm(r.embeds[...], r.waff[...])
            for o in range(8):
                r.mod_out[o] = packed(partial[2 * o : 2 * o + 2, :], 16)
            exchange("m", r.mod_out, r.mod_in)
            r.mod_in[pl.ds(me, 1)] = r.mod_out[pl.ds(me, 1)]
        if name == "w0":
            out_first(0)
            out_second(0)
            out_start(1)
            out_third(0)
            out_fourth(0)
            out_fifth(0)
            out_first(1)
            out_end(0)
        if name == "affine":
            exchanged("m", r.mod_in)
            r.mod[...] = unpacked(jnp.sum(r.mod_in[...], axis=0), 2, wide_rows)
        if name == "w1":
            out_fifth(1)
            out_end(1)
        if name == "wqkv":
            net.drain()
            whole_end(2)
            whole_end(3)
            for copy in got_g:
                copy.wait()
            for seg in segs:
                rows = slice(seg.row, seg.row + seg.pixels)
                r.g[rows, :] = jnp.where(r.live(seg.index), r.g[rows, :], 0).astype(BF)
        if name == ("grad0", 0):
            exchanged("n", r.planes.at[z, 0:8])
            net.push(("n", 0), lambda: (r.planes.at[z], r.planes.at[z], z_peer))
        if name == ("grad0", 1):
            pair = z - side
            net.take(("n", 0), r.planes.at[z + 1 - 2 * side], z_peer)
            net.push(("n", 1), lambda: (r.planes.at[pl.ds(pair, 2)], r.planes.at[pl.ds(pair, 2)], z_cross))
        if name == "back0":
            net.take(("n", 1), r.planes.at[pl.ds(2 - (z - side), 2)], z_cross)
            values = r.planes[...].astype(F32)
            terms = [unpacked(values[p, o], 2, wide_rows) for p in range(4) for o in range(8)]
            embeds = [values[p, 8] for p in range(4)]
            grad = mm(jnp.concatenate(embeds, axis=0).astype(BF), jnp.concatenate(terms, axis=0).astype(BF), 0, 0)
            r.own_affine[...] = grad[0 : block["waff"], :]
            done.append(fetch(r.own_affine, r.out_affine))
        if name == "rows":
            per = ch // 8
            lane = lax.broadcasted_iota(jnp.int32, (ch, 8 * 128), 1)
            sub = lax.broadcasted_iota(jnp.int32, (ch, 8 * 128), 0)
            spread = jnp.where((sub // per == lane // 128) & (sub % per == lane % 128), 1.0, 0.0).astype(BF)
            cut = mm(jnp.concatenate(three_parts(r.rows[...]), axis=0).astype(BF), spread)
            cut = cut[0:16] + cut[16:32] + cut[32:48]
            for o in range(8):
                r.rows_out[o] = cut[:, 128 * o : 128 * (o + 1)]
            exchange("q", r.rows_out, r.rows_in)
            r.rows_in[pl.ds(me, 1)] = r.rows_out[pl.ds(me, 1)]
        if name == "late":
            for seg, out in zip(segs, (r.big_out, r.small_out)):
                done.append(fetch(r.out.at[seg.row : seg.row + seg.pixels, :], out))
        run(SCHEDULE.get(name, ()))

    def ticks(name):
        if name == "conv0":
            return {
                (0, 1): lambda: out_second(1),
                (0, 2): lambda: (whole_start(2), whole_start(3)),
                (1, 0): lambda: out_third(1),
            }
        if name == "a1":
            return {(0, 3): lambda: out_fourth(1)}
        if name == "conv1":
            return {
                (0, 1): lambda: [whole_pass(i, flip) for i in (2, 3) for flip in "xy"],
                (0, 3): lambda: [whole_pass(i, "d") for i in (2, 3)],
            }
        at_rows = type(name) is str
        due = {
            (key[1:] if at_rows else key[2]): chosen
            for key, chosen in SCHEDULE.items()
            if type(key) is tuple and len(key) == 3 and (key[0] == name if at_rows else key[:2] == name)
        }
        return {where: lambda chosen=chosen: run(chosen) for where, chosen in due.items()}

    def grad_affine(rows):
        r.dmod[...] = packed(jnp.concatenate(rows, axis=0), 16).astype(BF)
        exchange("n", r.dmod, r.planes.at[z, 0:8])
        r.planes[z, me] = r.dmod[...]
        r.planes[z, 8] = r.embeds[...]

    r.grad_affine = grad_affine
    pl.semaphore_wait(barrier, len(FLIPS) + 2)
    exchange("p", r.message, r.messages)
    out_start(0)
    r.waff[...] = jnp.zeros_like(r.waff)
    copied_affine = fetch(r.own_waff, r.waff.at[0 : block["waff"], :])
    copied_message = fetch(r.message, r.messages.at[me])
    got_g = [fetch(src, r.g.at[s.row : s.row + s.pixels, :]) for src, s in zip((r.big_g, r.small_g), segs)]
    for i in range(len(WEIGHTS)):
        mine[i] = fetch(own[i], part(i, "", 3, 3))
    for copy in got_x:
        copy.wait()
    block_body(sides, r, hook, ticks)

    for seg, out in zip(segs, (r.big_grad, r.small_grad)):
        done.append(fetch(r.grad.at[seg.row : seg.row + seg.pixels, :], out))
    run(TAIL[:-8])
    net.drain()
    z_drain(range(5))
    run(TAIL[-8:])
    z_drain(range(5, len(z_units) + 1))
    for copy in done:
        copy.wait()


def embed_rows(class_table, sigma_table, labels, sigmas):
    summed = class_table[labels].astype(F32) + sigma_table[sigmas].astype(F32)
    return jax.nn.silu(summed).astype(BF)


def named(names, refs):
    return dict(zip(names, refs))


def fused_call(sides, ch, arrays):
    block = dict(
        w0=arrays["own_w0"].shape[0],
        w1=arrays["own_w1"].shape[0],
        waff=arrays["own_waff"].shape[0],
        wqkv=arrays["own_wqkv"].shape[0],
        wproj=arrays["own_wproj"].shape[0],
    )
    segs, rows, _ = make_segs(sides)
    in_units = reduce_units(block, ch)
    width = dict(w0=ch, w1=ch, wqkv=3 * ch, wproj=ch)
    buffer = lambda *shape: pltpu.VMEM(shape, BF)
    wide_buffer = lambda *shape: pltpu.VMEM(shape, F32)
    whole = {name: buffer(8 * block[name], width[name]) for name in WEIGHTS}
    copies = len(transfer_names(in_units))
    scratch = dict(
        block_scratch(sides, ch),
        **whole,
        grad_w0=buffer(2, 2, 2, block["w0"], ch),
        grad_w1=buffer(2, 2, 2, block["w1"], ch),
        grad_both=buffer(2, 2, 2, block["wqkv"], 4 * ch),
        x=buffer(rows, ch),
        g=buffer(rows, ch),
        out=buffer(rows, ch),
        params=wide_buffer(16, ch),
        messages=buffer(8, 32, 128),
        embeds=buffer(16, 128),
        waff=buffer(128, 2 * ch),
        mod_out=wide_buffer(8, 16, 128),
        mod_in=wide_buffer(8, 16, 128),
        mod=wide_buffer(2, 2 * ch),
        dmod=buffer(16, 128),
        planes=buffer(4, 9, 16, 128),
        own_affine=wide_buffer(block["waff"], 2 * ch),
        rows=wide_buffer(16, ch),
        rows_out=wide_buffer(8, 16, 128),
        rows_in=wide_buffer(8, 16, 128),
        own_rows=wide_buffer(16, 128),
        rzr=wide_buffer(2, 16, 128),
        send=pltpu.SemaphoreType.DMA((copies,)),
        recv=pltpu.SemaphoreType.DMA((copies,)),
        local=pltpu.SemaphoreType.DMA((48,)),
    )
    slots = [
        [buffer(2, 2, n, w) for _, _, n, _, w, _ in in_units],
        [buffer(2, n, w) for _, _, n, _, w, _ in in_units],
        [buffer(n, w) for _, _, n, _, w, _ in in_units],
        [buffer(2, block["wqkv"], 4 * ch)] + [buffer(2, n, w) for _, _, n, _, w, _ in in_units[2:]],
    ]
    big, small = segs[0].pixels, segs[1].pixels
    outs = dict(
        big_out=((big, ch), BF),
        small_out=((small, ch), BF),
        big_grad=((big, ch), BF),
        small_grad=((small, ch), BF),
        out_rows=((16, 128), F32),
        out_affine=((block["waff"], 2 * ch), F32),
        out_w0=((block["w0"], ch), BF),
        out_w1=((block["w1"], ch), BF),
        out_both=((block["wqkv"], 4 * ch), BF),
    )
    names = list(arrays) + list(outs) + list(scratch)

    def kernel(*refs):
        r = types.SimpleNamespace(**dict(zip(names, refs)))
        rest = list(refs[len(names) :])
        n = len(in_units)
        r.ra, r.rb, r.rc, r.rz = rest[:n], rest[n : 2 * n], rest[2 * n : 3 * n], rest[3 * n :]
        fused_kernel(sides, block, r)

    results = pl.pallas_call(
        kernel,
        out_shape=[jax.ShapeDtypeStruct(*shape) for shape in outs.values()],
        in_specs=[pl.BlockSpec(memory_space=pltpu.SMEM)] + [pl.BlockSpec(memory_space=pl.ANY)] * (len(arrays) - 1),
        out_specs=[pl.BlockSpec(memory_space=pl.ANY)] * len(outs),
        scratch_shapes=list(scratch.values()) + sum(slots, []),
        compiler_params=pltpu.CompilerParams(
            collective_id=0, has_side_effects=True, vmem_limit_bytes=VMEM_LIMIT
        ),
    )(*arrays.values())
    return results


def finish_call(results, per):
    images, both = results[:4], results[8]
    ch = both.shape[1] // 4
    outs = [jax.ShapeDtypeStruct(image.shape, image.dtype) for image in images]
    shapes = [(3, per), (10, per)] + [weight.shape for weight in results[5:8]]
    shapes += [(both.shape[0], 3 * ch), (both.shape[0], ch)]
    outs += [jax.ShapeDtypeStruct(shape, F32) for shape in shapes]
    total_in, total_out = len(results), len(outs)

    def kernel(*refs):
        sources, targets = refs[:total_in], refs[total_in : total_in + total_out]
        rest = refs[total_in + total_out :]
        held, made, sems = rest[:total_in], rest[total_in:-1], rest[-1]
        inward = [pltpu.make_async_copy(s, h, sems.at[i]) for i, (s, h) in enumerate(zip(sources, held))]
        for copy in inward:
            copy.start()
        outward = []

        def send(source, target):
            copy = pltpu.make_async_copy(source, target, sems.at[total_in + len(outward)])
            copy.start()
            outward.append(copy)

        for i in (8, 5, 6, 7):
            inward[i].wait()
            if i == 5:
                send(held[i], targets[i + 1])
            elif i < 8:
                made[i - 3][...] = held[i][...].astype(F32)
                send(made[i - 3], targets[i + 1])
            else:
                made[5][...] = held[i][:, 0 : 3 * ch].astype(F32)
                made[6][...] = held[i][:, 3 * ch :].astype(F32)
                send(made[5], targets[9])
                send(made[6], targets[10])
        for i in range(4):
            inward[i].wait()
            send(held[i], targets[i])
        inward[4].wait()
        made[0][...] = held[4][0:3, 0:per]
        made[1][...] = held[4][3:13, 0:per]
        send(made[0], targets[4])
        send(made[1], targets[5])
        for copy in outward:
            copy.wait()

    any_spec = pl.BlockSpec(memory_space=pl.ANY)
    return pl.pallas_call(
        kernel,
        out_shape=outs,
        in_specs=[any_spec] * total_in,
        out_specs=[any_spec] * total_out,
        scratch_shapes=[pltpu.VMEM(array.shape, array.dtype) for array in results]
        + [pltpu.VMEM(out.shape, out.dtype) for out in outs[4:]]
        + [pltpu.SemaphoreType.DMA((total_in + total_out,))],
        compiler_params=pltpu.CompilerParams(vmem_limit_bytes=VMEM_LIMIT),
    )(*results)


def plain_call(sides, ch, arrays):
    _, rows, _ = make_segs(sides)
    scratch = dict(
        block_scratch(sides, ch), mod=pltpu.VMEM((16, 2 * ch), F32), masked=pltpu.VMEM((rows, ch), BF)
    )
    outs = dict(
        out=((rows, ch), BF),
        grad=((rows, ch), BF),
        terms0=((9 * ch, ch), BF),
        terms1=((9 * ch, ch), BF),
        affine=((2 * ch, 2 * ch), BF),
        terms_qkv=((ch, 3 * ch), BF),
        terms_proj=((ch, ch), BF),
        rows=((16, ch), F32),
    )
    names = list(arrays) + list(outs) + list(scratch)

    def kernel(*refs):
        r = types.SimpleNamespace(**dict(zip(names, refs)))
        segs, _, _ = make_segs(sides)
        given = r.g
        r.live = lambda i: r.loads[0, i] > 0
        r.g = r.masked
        r.columns = [(0, ch)]
        for seg in segs:
            span = slice(seg.row, seg.row + seg.pixels)
            r.masked[span, :] = jnp.where(r.live(seg.index), given[span, :], 0).astype(BF)

        def hook(name):
            if name == "affine":
                r.mod[...] = mm(r.emb[...], r.waff[...])

        def keep(ref):
            def store(row, col, value):
                ref[row : row + value.shape[0], col : col + value.shape[1]] = value.astype(BF)

            return store

        def grad_affine(terms):
            zeros = jnp.zeros((14, 2 * ch), F32)
            r.affine[...] = mm(r.emb[...], jnp.concatenate(terms + [zeros], axis=0).astype(BF), 0, 0).astype(BF)

        r.grad0, r.grad1 = keep(r.terms0), keep(r.terms1)
        r.grad_qkv = lambda value: keep(r.terms_qkv)(0, 0, value)
        r.grad_proj = lambda value: keep(r.terms_proj)(0, 0, value)
        r.grad_affine = grad_affine
        block_body(sides, r, hook)

    return pl.pallas_call(
        kernel,
        out_shape=[jax.ShapeDtypeStruct(*shape) for shape in outs.values()],
        in_specs=[pl.BlockSpec(memory_space=pltpu.SMEM)]
        + [pl.BlockSpec(memory_space=pltpu.VMEM)] * (len(arrays) - 1),
        out_specs=[pl.BlockSpec(memory_space=pltpu.VMEM)] * len(outs),
        scratch_shapes=list(scratch.values()),
        compiler_params=pltpu.CompilerParams(vmem_limit_bytes=VMEM_LIMIT),
    )(*arrays.values())


def on_device(
    fused,
    big_images,
    small_images,
    big_labels,
    small_labels,
    big_sigmas,
    small_sigmas,
    loads,
    class_table,
    sigma_table,
    norm_gains,
    biases,
    w_conv0,
    w_conv1,
    w_affine,
    w_qkv,
    w_proj,
    big_cotangent,
    small_cotangent,
):
    sides = (big_images.shape[1], small_images.shape[1])
    ch = big_images.shape[-1]
    flat = lambda array: array.reshape(-1, ch)
    big_embed = embed_rows(class_table, sigma_table, big_labels, big_sigmas)
    small_embed = embed_rows(class_table, sigma_table, small_labels, small_sigmas)
    emb = jnp.concatenate([big_embed, small_embed], axis=0)
    own_rows = jnp.concatenate([norm_gains, biases], axis=0)
    shapes = [big_images.shape, small_images.shape] * 2
    if fused:
        per = own_rows.shape[1]
        slices = emb.reshape(16, -1)
        message = jnp.concatenate(
            [
                jnp.pad(own_rows, ((0, 3), (0, 128 - per))),
                jnp.pad(slices, ((0, 0), (0, 128 - slices.shape[1]))),
            ],
            axis=0,
        )
        made = fused_call(
            sides,
            ch,
            dict(
                loads=loads,
                big_x=flat(big_images),
                small_x=flat(small_images),
                big_g=flat(big_cotangent),
                small_g=flat(small_cotangent),
                message=message,
                own_w0=w_conv0,
                own_w1=w_conv1,
                own_waff=w_affine,
                own_wqkv=w_qkv,
                own_wproj=w_proj,
            ),
        )
        made = finish_call(made, per)
        images, gains, shifts = made[:4], made[4], made[5]
        affine, first, second, qkv, proj = made[6:]
        weights = [first, second, affine, qkv, proj]
    else:
        gather = lambda array, axis=0: lax.all_gather(array, "shard", axis=axis, tiled=True)
        out, grad, terms0, terms1, affine, terms_qkv, terms_proj, rows = plain_call(
            sides,
            ch,
            dict(
                loads=loads,
                x=jnp.concatenate([flat(big_images), flat(small_images)], axis=0),
                g=jnp.concatenate([flat(big_cotangent), flat(small_cotangent)], axis=0),
                emb=jnp.pad(emb, ((0, 14), (0, 0))),
                params=jnp.pad(gather(own_rows, 1).astype(F32), ((0, 3), (0, 0))),
                w0=gather(w_conv0),
                w1=gather(w_conv1),
                waff=gather(w_affine),
                wqkv=gather(w_qkv),
                wproj=gather(w_proj),
            ),
        )

        def owned(terms, axis=0):
            mine = lax.psum_scatter(terms, "shard", scatter_dimension=axis, tiled=True)
            return lax.psum(mine, "rep").astype(F32)

        big = sides[0] * sides[0]
        images = [out[:big], out[big:], grad[:big], grad[big:]]
        sums = owned(rows, 1)
        gains, shifts = sums[:3], sums[3:13]
        weights = [owned(terms) for terms in (terms0, terms1, affine, terms_qkv, terms_proj)]
    return tuple(image.reshape(shape) for image, shape in zip(images, shapes)) + (gains, shifts, *weights)


def solution(mesh):
    fused = mesh.shape["shard"] == 8 and mesh.shape["rep"] == 4
    split = P(("shard", "rep"))
    image = P(("shard", "rep"), None, None, None)
    rows, columns = P("shard", None), P(None, "shard")
    return jax.shard_map(
        lambda *arrays: on_device(fused, *arrays),
        mesh=mesh,
        in_specs=(image, image, split, split, split, split, P(("shard", "rep"), None), P(), P(), columns, columns)
        + (rows,) * 5
        + (image, image),
        out_specs=(image,) * 4 + (columns,) * 2 + (rows,) * 5,
        check_vma=False,
    )
```
